32 devices in a mesh: layer: 4 (over y, core), latent: 8 (over z, x).
Axes of the slice: x: 2, y: 2, z: 4, core: 2. Of those that a mesh axis runs over, the one named last changes fastest.
Arguments:
- resid: bfloat16 [2, 128, 3584], P(None, 'latent'), may hold values from -6 to 6
- target: bfloat16 [3, 128, 3584], P(None, 'latent'), may hold values from -6 to 6
- enc_weight: bfloat16 [4, 3584, 1024], P('layer', None, 'latent'), may hold values from -0.09375 to 0.09375
- enc_bias: float32 [4, 1024], P('layer', 'latent'), may hold values from -3 to 3
- dec_weight: bfloat16 [4, 2, 2, 1024, 1792], P('layer', None, None, 'latent'), may hold values from -0.125 to 0.125
- blocks: int32 [2, 1, 12], replicated, may hold values from 0 to 15, all different within a row
Outputs:
- errors: bfloat16 [4, 128, 1792], P('layer', 'latent')
- enc_grad: bfloat16 [4, 3584, 1024], P('layer', None, 'latent')
- bias_grad: float32 [4, 1024], P('layer', 'latent')
The draws below stay inside these ranges and needn't reach their ends.
Inputs may be any that keep to these rules, and one draw needn't show every extreme that they name: Each row names 12 different blocks; every block is named in some row.
All inputs are finite; a program needn't handle non-finite values.
Results may differ from the reference program's by a relative error of at most 0.007.
Values may be sent and summed in bfloat16 or wider, within the bound.
No kernel may reach another device: no remote copies, remote signals or barrier semaphores. Data moves between devices by JAX's collectives and lax.ppermute only.
A program may use at most 64 MiB of HBM per device.

```python
import jax
import jax.numpy as jnp
from jax import lax

D = 3584
DH = 1792
BLOCK = 128
LATENTS = 2048
HALF = 1024
BLOCKS = 16
ACTIVE = 12
LAYERS = 2
TOKENS = 128
TILE = 128


def levels(own_key, extent, pieces, low, high):
    factor_of = 1.0
    for position, shards_of in pieces:
        heights = jax.random.uniform(jax.random.fold_in(jax.random.fold_in(own_key, 6), position), (shards_of,), jnp.float32, low / len(pieces), high / len(pieces))
        factor_of = factor_of * jnp.repeat(jnp.exp(heights), extent[position] // shards_of).reshape((-1,) + (1,) * (len(extent) - 1 - position))
    return factor_of


def picks_of(rng, rows, number_of, top, lift):
    ranking = jax.random.permutation(jax.random.fold_in(rng, 1), number_of)
    favour = ranking
    for power in range(3):
        favour = favour * favour // number_of
    favour = favour * lift // number_of
    tickets = jax.random.randint(jax.random.fold_in(rng, 2), (rows, number_of), 0, 4096) + favour
    sure = jax.random.permutation(jax.random.fold_in(rng, 3), rows)[jnp.arange(number_of) % rows]
    tickets = jnp.where(jnp.arange(rows)[:, None] == sure[None, :], 1 << 14, tickets)
    merit = tickets * number_of + jnp.arange(number_of)
    return lax.top_k(merit.astype(jnp.int32), top)[1].astype(jnp.int32)


def gaussian(stream_key, dims, deviation, limit, pieces=(), kind=jnp.bfloat16):
    array = deviation * jax.random.normal(stream_key, dims, jnp.float32)
    if pieces:
        array = array * levels(stream_key, dims, pieces, -0.22, 0.18)
    return jnp.clip(array, -limit, limit).astype(kind)


def setup_inputs(seed: int = 0) -> dict:
    seeds = jax.random.split(jax.random.key(seed), 7)
    resid = gaussian(seeds[0], (LAYERS, TOKENS, D), 1.0, 6.0, ((1, 8),))
    target = gaussian(seeds[1], (LAYERS + 1, TOKENS, D), 1.0, 6.0, ((1, 8),))
    enc_weight = gaussian(seeds[2], (2 * LAYERS, D, HALF), D ** -0.5, 0.09375, ((0, 4), (2, 8)))
    enc_bias = gaussian(seeds[3], (2 * LAYERS, HALF), 0.5, 3.0, ((0, 4), (1, 8)), jnp.float32)
    dec_weight = gaussian(seeds[4], (2 * LAYERS, 2, 2, HALF, DH), LATENTS ** -0.5, 0.125, ((0, 4), (3, 8)))
    blocks = picks_of(seeds[5], LAYERS * (TOKENS // TILE), BLOCKS, ACTIVE, 12000).reshape((LAYERS, TOKENS // TILE, ACTIVE))
    return {"resid": resid, "target": target, "enc_weight": enc_weight, "enc_bias": enc_bias, "dec_weight": dec_weight, "blocks": blocks}


def decoder_of(dec_weight, layer_pos, target_pos):
    left_cols = dec_weight[2 * layer_pos, target_pos].reshape(LATENTS, DH)
    right_cols = dec_weight[2 * layer_pos + 1, target_pos].reshape(LATENTS, DH)
    return jnp.concatenate([left_cols, right_cols], axis=1)


def reference(resid, target, enc_weight, enc_bias, dec_weight, blocks):
    block_ids = jnp.arange(LATENTS, dtype=jnp.int32) // BLOCK
    activations = []
    gate_masks = []
    for index in range(LAYERS):
        encoder = jnp.concatenate([enc_weight[2 * index], enc_weight[2 * index + 1]], axis=1)
        bias_row = jnp.concatenate([enc_bias[2 * index], enc_bias[2 * index + 1]])
        preact = jnp.dot(resid[index], encoder, preferred_element_type=jnp.float32) + bias_row
        listed = jnp.any(blocks[index][:, :, None] == block_ids[None, None, :], axis=1)
        gate_mask = jnp.repeat(listed.astype(jnp.float32), TILE, axis=0)
        activations.append((preact * gate_mask).astype(jnp.bfloat16))
        gate_masks.append(gate_mask)
    recon = [jnp.zeros((TOKENS, D), jnp.float32) for index in range(LAYERS + 1)]
    for index in range(LAYERS):
        for step in range(2):
            recon[index + step] = recon[index + step] + jnp.dot(activations[index], decoder_of(dec_weight, index, step), preferred_element_type=jnp.float32)
    error_list = [(recon[index] - target[index].astype(jnp.float32)).astype(jnp.bfloat16) for index in range(LAYERS + 1)]
    error_rows = []
    grad_rows = []
    bias_rows = []
    for index in range(LAYERS):
        grad_act = jnp.dot(error_list[index], decoder_of(dec_weight, index, 0).T, preferred_element_type=jnp.float32)
        grad_act = grad_act + jnp.dot(error_list[index + 1], decoder_of(dec_weight, index, 1).T, preferred_element_type=jnp.float32)
        grad_pre = grad_act * gate_masks[index]
        bias_full = jnp.sum(grad_pre, axis=0)
        grad_full = jnp.dot(resid[index].T, grad_pre.astype(jnp.bfloat16), preferred_element_type=jnp.float32).astype(jnp.bfloat16)
        for which_half in range(2):
            error_rows.append(error_list[index][:, which_half * DH:(which_half + 1) * DH])
            grad_rows.append(grad_full[:, which_half * HALF:(which_half + 1) * HALF])
            bias_rows.append(bias_full[which_half * HALF:(which_half + 1) * HALF])
    return jnp.stack(error_rows), jnp.stack(grad_rows), jnp.stack(bias_rows)
```

```python
import jax
import jax.numpy as jnp
from jax import lax
from jax.sharding import PartitionSpec as P

BLOCK = 128


def halves_swapped(block):
    count = lax.axis_size("layer")
    return lax.ppermute(block, "layer", [(i, i ^ 1) for i in range(count)])


def shifted(block, distance):
    count = lax.axis_size("layer")
    route = [(i, i + distance) for i in range(count) if 0 <= i + distance < count]
    return lax.ppermute(block, "layer", route)


def neighbours_sums(own_sum, ahead_part):
    count = lax.axis_size("layer")
    if count == 4:
        first = lax.axis_index("layer") < 2
        sent = jnp.where(first, ahead_part, own_sum)
        got = lax.ppermute(sent, "layer", [(i, i ^ 2) for i in range(count)])
        nothing = jnp.zeros_like(got)
        return jnp.where(first, nothing, got), jnp.where(first, got, nothing)
    return shifted(ahead_part, 2), shifted(own_sum, -2)


def to_all(block):
    count = lax.axis_size("latent")
    copies = jnp.broadcast_to(block[None], (count,) + block.shape)
    return lax.all_to_all(copies, "latent", 0, 0).reshape((count * block.shape[0],) + block.shape[1:])


def on_device(resid, target, enc_weight, enc_bias, dec_weight, blocks):
    f32, bf16 = jnp.float32, jnp.bfloat16
    slots = lax.axis_size("latent")
    layer_slot = lax.axis_index("layer")
    layer, half = layer_slot // 2, layer_slot % 2
    slot = lax.axis_index("latent")
    _, rows, width = resid.shape
    tokens = rows * slots
    cols = width // 2
    weight = enc_weight[0]
    latents = weight.shape[1]
    decoder = dec_weight[0]
    dec_own = decoder[0].reshape(2 * latents, cols)
    dec_next = decoder[1].reshape(2 * latents, cols)

    mine = lax.dynamic_slice(resid, (layer, 0, half * cols), (1, rows, cols))[0]
    resid_half = to_all(mine)
    weight_mine = lax.dynamic_slice_in_dim(weight, half * cols, cols, 0)
    weight_other = halves_swapped(lax.dynamic_slice_in_dim(weight, (1 - half) * cols, cols, 0))
    bias_other = halves_swapped(enc_bias[0])
    weight_pair = jnp.concatenate(
        [
            jnp.where(half == 0, weight_mine, weight_other),
            jnp.where(half == 0, weight_other, weight_mine),
        ],
        axis=1,
    )
    bias_pair = jnp.concatenate(
        [jnp.where(half == 0, enc_bias[0], bias_other), jnp.where(half == 0, bias_other, enc_bias[0])]
    )
    listed = lax.dynamic_index_in_dim(blocks, layer, 0, keepdims=False)
    tile = tokens // listed.shape[0]
    per_device = latents // BLOCK
    firing = []
    for side in range(2):
        first = (side * slots + slot) * per_device
        names = first + jnp.arange(per_device)
        flags = jnp.any(listed[:, :, None] == names, axis=1).astype(f32)
        firing.append(jnp.repeat(jnp.repeat(flags, tile, axis=0), BLOCK, axis=1))
    gate_pair = jnp.concatenate(firing, axis=1)
    gate = jnp.where(half == 0, firing[0], firing[1])

    part = jnp.dot(resid_half, weight_pair, preferred_element_type=f32)
    preact = part + halves_swapped(part) + bias_pair
    acts = (preact * gate_pair).astype(bf16)
    resid_other = halves_swapped(resid_half)

    sums = jnp.concatenate(
        [
            jnp.dot(acts, dec_own, preferred_element_type=f32).astype(bf16),
            jnp.dot(acts, dec_next, preferred_element_type=f32).astype(bf16),
        ],
        axis=1,
    )
    pieces = lax.all_to_all(sums.reshape(slots, rows, width), "latent", 0, 0)
    totals = jnp.sum(pieces.astype(f32), axis=0)
    own_sum, ahead_part = totals[:, :cols], totals[:, cols:]
    behind, next_own = neighbours_sums(own_sum, ahead_part)
    wanted = lax.dynamic_slice(target, (layer, 0, half * cols), (2, rows, cols)).astype(f32)
    err_own = (own_sum + behind - wanted[0]).astype(bf16)
    err_next = (ahead_part + next_own - wanted[1]).astype(bf16)

    errs = to_all(jnp.concatenate([err_own, err_next], axis=1))
    across = (((1,), (1,)), ((), ()))
    grad_pair = lax.dot_general(errs[:, :cols], dec_own, across, preferred_element_type=f32)
    grad_pair = grad_pair + lax.dot_general(errs[:, cols:], dec_next, across, preferred_element_type=f32)
    lower, upper = grad_pair[:, :latents], grad_pair[:, latents:]
    kept = jnp.where(half == 0, lower, upper)
    sent = jnp.where(half == 0, upper, lower)
    grad_pre = (kept + halves_swapped(sent)) * gate
    bias_grad = jnp.sum(grad_pre, axis=0)[None, :]
    grad_low = grad_pre.astype(bf16)
    whole = jnp.concatenate(
        [jnp.where(half == 0, resid_half, resid_other), jnp.where(half == 0, resid_other, resid_half)], axis=1
    )
    enc_grad = lax.dot_general(whole, grad_low, (((0,), (0,)), ((), ())), preferred_element_type=f32)
    return err_own[None], enc_grad.astype(bf16)[None], bias_grad


def solution(mesh):
    return jax.shard_map(
        on_device,
        mesh=mesh,
        in_specs=(
            P(None, "latent", None),
            P(None, "latent", None),
            P("layer", None, "latent"),
            P("layer", "latent"),
            P("layer", None, None, "latent", None),
            P(),
        ),
        out_specs=(P("layer", "latent", None), P("layer", None, "latent"), P("layer", "latent")),
        check_vma=False,
    )
```

```python
import jax
import jax.numpy as jnp
from jax import lax
from jax.sharding import PartitionSpec as P

BLOCK = 128
F32, BF16 = jnp.float32, jnp.bfloat16


def crossed(block, axis, mask):
    return lax.ppermute(block, axis, [(i, i ^ mask) for i in range(lax.axis_size(axis))])


def times(left, right):
    return jnp.dot(left, right, preferred_element_type=F32)


def times_transposed(left, right):
    return lax.dot_general(left, right, (((1,), (1,)), ((), ())), preferred_element_type=F32)


def both_halves(half, mine, other, axis):
    return jnp.concatenate([jnp.where(half == 0, mine, other), jnp.where(half == 0, other, mine)], axis=axis)


def gates(blocks, layer, slot, slots, latents, tokens):
    listed = lax.dynamic_index_in_dim(blocks, layer, 0, keepdims=False)
    tile = tokens // listed.shape[0]
    here = latents // BLOCK
    out = []
    for side in range(2):
        names = (side * slots + slot) * here + jnp.arange(here)
        flags = jnp.any(listed[:, :, None] == names, axis=1).astype(F32)
        out.append(jnp.repeat(jnp.repeat(flags, tile, axis=0), BLOCK, axis=1))
    return out


def paired_encoder(weight, bias, half, cols):
    other = crossed(lax.dynamic_slice_in_dim(weight, (1 - half) * cols, cols, 0), "layer", 1)
    mine = lax.dynamic_slice_in_dim(weight, half * cols, cols, 0)
    return both_halves(half, mine, other, 1), both_halves(half, bias, crossed(bias, "layer", 1), 0)


def encoder_gradient(resid_half, resid_other, grad_low, half):
    whole = both_halves(half, resid_half, resid_other, 1)
    grad = lax.dot_general(whole, grad_low, (((0,), (0,)), ((), ())), preferred_element_type=F32)
    return grad.astype(BF16)


def two_layers(resid, target, enc_weight, enc_bias, dec_weight, blocks):
    slots = lax.axis_size("latent")
    far = slots // 2
    layer, half = lax.axis_index("layer") // 2, lax.axis_index("layer") % 2
    slot = lax.axis_index("latent")
    _, rows, width = resid.shape
    tokens, cols, part = rows * slots, width // 2, width // 4
    latents = enc_weight.shape[2]
    near_rows = tokens // 2
    decoder = dec_weight[0].reshape(2, 2 * latents, cols)

    mine = lax.dynamic_slice(resid, (layer, 0, half * cols), (1, rows, cols))[0]
    along = [mine] + [crossed(mine, "latent", 2 * k) for k in range(1, far)]
    beside = [crossed(block, "latent", 1) for block in along]
    resid_half = jnp.concatenate(along + beside, axis=0)

    shared = lax.dynamic_index_in_dim(decoder, 1 - layer, 0, keepdims=False)
    dec_given = crossed(lax.dynamic_slice_in_dim(shared, (1 - layer) * part, part, 1), "layer", 2)
    dec_kept = lax.dynamic_slice_in_dim(shared, layer * part, part, 1)
    dec_own = lax.dynamic_index_in_dim(decoder, layer, 0, keepdims=False)
    weight_pair, bias_pair = paired_encoder(enc_weight[0], enc_bias[0], half, cols)
    firing = gates(blocks, layer, slot, slots, latents, tokens)
    gate = jnp.where(half == 0, firing[0], firing[1])

    partial = times(resid_half, weight_pair)
    preact = partial + crossed(partial, "layer", 1) + bias_pair
    acts = (preact * jnp.concatenate(firing, axis=1)).astype(BF16)
    acts_other = crossed(acts, "layer", 2)
    resid_other = crossed(resid_half, "layer", 1)

    def scattered(product):
        leaving = product(slice(near_rows, tokens)).astype(BF16)
        near = product(slice(0, near_rows)) + crossed(leaving, "latent", 1).astype(F32)
        total = near[:rows]
        for k in range(1, far):
            total = total + crossed(near[k * rows:(k + 1) * rows].astype(BF16), "latent", 2 * k).astype(F32)
        return total

    def gathered(block):
        along = [block] + [crossed(block, "latent", 2 * k) for k in range(1, far)]
        near = jnp.concatenate(along, axis=0)
        return jnp.concatenate([near, crossed(near, "latent", 1)], axis=0)

    sum_own = scattered(lambda at: times(acts[at], dec_own))
    sum_shared = scattered(lambda at: times(acts[at], dec_kept) + times(acts_other[at], dec_given))
    wanted_own = lax.dynamic_slice(target, (2 * layer, 0, half * cols), (1, rows, cols))[0]
    wanted_shared = lax.dynamic_slice(target, (1, 0, half * cols + layer * part), (1, rows, part))[0]
    err_own = (sum_own - wanted_own.astype(F32)).astype(BF16)
    err_shared = (sum_shared - wanted_shared.astype(F32)).astype(BF16)
    err_across = crossed(err_shared, "layer", 2)
    errors = jnp.where(layer == 0, err_own, jnp.concatenate([err_across, err_shared], axis=1))

    errs_own, errs_shared = gathered(err_own), gathered(err_shared)
    back = times_transposed(errs_shared, dec_given).astype(BF16)
    here = times_transposed(errs_own, dec_own) + times_transposed(errs_shared, dec_kept)

    def of_half(pair, which):
        return jnp.where(which == 0, pair[:, :latents], pair[:, latents:])

    grad = of_half(here, half) + crossed(of_half(here, 1 - half), "layer", 1)
    grad = grad + crossed(of_half(back, half), "layer", 2).astype(F32)
    grad = grad + crossed(of_half(back, 1 - half), "layer", 3).astype(F32)
    grad_pre = grad * gate
    bias_grad = jnp.sum(grad_pre, axis=0)[None, :]
    enc_grad = encoder_gradient(resid_half, resid_other, grad_pre.astype(BF16), half)
    return errors[None], enc_grad[None], bias_grad


def any_layers(resid, target, enc_weight, enc_bias, dec_weight, blocks):
    slots = lax.axis_size("latent")
    count = lax.axis_size("layer")
    layer, half = lax.axis_index("layer") // 2, lax.axis_index("layer") % 2
    slot = lax.axis_index("latent")
    _, rows, width = resid.shape
    tokens, cols = rows * slots, width // 2
    latents = enc_weight.shape[2]
    decoder = dec_weight[0].reshape(2, 2 * latents, cols)

    def to_all(block):
        copies = jnp.broadcast_to(block[None], (slots,) + block.shape)
        return lax.all_to_all(copies, "latent", 0, 0).reshape(tokens, block.shape[1])

    def shifted(block, distance):
        route = [(i, i + distance) for i in range(count) if 0 <= i + distance < count]
        return lax.ppermute(block, "layer", route)

    resid_half = to_all(lax.dynamic_slice(resid, (layer, 0, half * cols), (1, rows, cols))[0])
    weight_pair, bias_pair = paired_encoder(enc_weight[0], enc_bias[0], half, cols)
    firing = gates(blocks, layer, slot, slots, latents, tokens)
    gate = jnp.where(half == 0, firing[0], firing[1])
    partial = times(resid_half, weight_pair)
    preact = partial + crossed(partial, "layer", 1) + bias_pair
    acts = (preact * jnp.concatenate(firing, axis=1)).astype(BF16)
    resid_other = crossed(resid_half, "layer", 1)

    sums = jnp.concatenate([times(acts, decoder[t]).astype(BF16) for t in range(2)], axis=1)
    pieces = lax.all_to_all(sums.reshape(slots, rows, width), "latent", 0, 0)
    totals = jnp.sum(pieces.astype(F32), axis=0)
    own_sum, ahead_part = totals[:, :cols], totals[:, cols:]
    wanted = lax.dynamic_slice(target, (layer, 0, half * cols), (2, rows, cols)).astype(F32)
    err_own = (own_sum + shifted(ahead_part, 2) - wanted[0]).astype(BF16)
    err_next = (ahead_part + shifted(own_sum, -2) - wanted[1]).astype(BF16)
    errs = to_all(jnp.concatenate([err_own, err_next], axis=1))
    here = times_transposed(errs[:, :cols], decoder[0]) + times_transposed(errs[:, cols:], decoder[1])
    lower, upper = here[:, :latents], here[:, latents:]
    grad = jnp.where(half == 0, lower, upper) + crossed(jnp.where(half == 0, upper, lower), "layer", 1)
    grad_pre = grad * gate
    bias_grad = jnp.sum(grad_pre, axis=0)[None, :]
    enc_grad = encoder_gradient(resid_half, resid_other, grad_pre.astype(BF16), half)
    return err_own[None], enc_grad[None], bias_grad


def solution(mesh):
    small = mesh.shape["layer"] == 4 and mesh.shape["latent"] == 8
    return jax.shard_map(
        two_layers if small else any_layers,
        mesh=mesh,
        in_specs=(
            P(None, "latent", None),
            P(None, "latent", None),
            P("layer", None, "latent"),
            P("layer", "latent"),
            P("layer", None, None, "latent", None),
            P(),
        ),
        out_specs=(P("layer", "latent", None), P("layer", None, "latent"), P("layer", "latent")),
        check_vma=False,
    )
```

```python
import jax
import jax.numpy as jnp
from jax import lax
from jax.sharding import PartitionSpec as P

BLOCK = 128
F32, BF16 = jnp.float32, jnp.bfloat16


def crossed(block, axis, mask):
    return lax.ppermute(block, axis, [(i, i ^ mask) for i in range(lax.axis_size(axis))])


def times(left, right):
    return jnp.dot(left, right, preferred_element_type=F32)


def times_transposed(left, right):
    return lax.dot_general(left, right, (((1,), (1,)), ((), ())), preferred_element_type=F32)


def both_halves(half, mine, other, axis):
    return jnp.concatenate([jnp.where(half == 0, mine, other), jnp.where(half == 0, other, mine)], axis=axis)


def gates(blocks, layer, slot, slots, latents, tokens):
    listed = lax.dynamic_index_in_dim(blocks, layer, 0, keepdims=False)
    tile = tokens // listed.shape[0]
    here = latents // BLOCK
    out = []
    for side in range(2):
        names = (side * slots + slot) * here + jnp.arange(here)
        flags = jnp.any(listed[:, :, None] == names, axis=1).astype(F32)
        out.append(jnp.repeat(jnp.repeat(flags, tile, axis=0), BLOCK, axis=1))
    return out


def half_preacts(resid_half, weight, weight_other, bias, half):
    cols = resid_half.shape[1]
    mine = lax.dynamic_slice_in_dim(weight, half * cols, cols, 0)
    other = lax.dynamic_slice_in_dim(weight_other, half * cols, cols, 0)
    nothing = jnp.zeros_like(bias)
    return times(resid_half, both_halves(half, mine, other, 1)) + both_halves(half, bias, nothing, 0)


def encoder_gradient(resid_half, resid_other, grad_low, half):
    whole = both_halves(half, resid_half, resid_other, 1)
    grad = lax.dot_general(whole, grad_low, (((0,), (0,)), ((), ())), preferred_element_type=F32)
    return grad.astype(BF16)


def two_layers(resid, target, enc_weight, enc_bias, dec_weight, blocks):
    slots = lax.axis_size("latent")
    far = slots // 2
    layer, half = lax.axis_index("layer") // 2, lax.axis_index("layer") % 2
    slot = lax.axis_index("latent")
    _, rows, width = resid.shape
    tokens, cols, part = rows * slots, width // 2, width // 4
    latents = enc_weight.shape[2]
    near_rows = tokens // 2
    decoder = dec_weight[0].reshape(2, 2 * latents, cols)

    weight = enc_weight[0]
    mine = lax.dynamic_slice(resid, (layer, 0, half * cols), (1, rows, cols))[0]
    along = [mine] + [None] * (far - 1)
    for k in range(far - 1, 0, -1):
        along[k] = crossed(mine, "latent", 2 * k)
    beside = [crossed(mine, "latent", 1)]

    shared = lax.dynamic_index_in_dim(decoder, 1 - layer, 0, keepdims=False)
    given = lax.dynamic_slice_in_dim(shared, (1 - layer) * part, part, 1)
    dec_given = crossed(given, "layer", 2)
    wanted = [
        lax.dynamic_slice(target, (2 * layer, 0, half * cols + i * part), (1, rows, part))[0] for i in range(2)
    ]
    wanted.append(lax.dynamic_slice(target, (1, 0, half * cols + layer * part), (1, rows, part))[0])
    decoder, blocks, weight, *along = lax.optimization_barrier((decoder, blocks, weight, *along))
    weight_other = crossed(weight, "layer", 1)
    beside += [crossed(block, "latent", 1) for block in along[1:]]
    shared = lax.dynamic_index_in_dim(decoder, 1 - layer, 0, keepdims=False)
    dec_kept = lax.dynamic_slice_in_dim(shared, layer * part, part, 1)
    dec_own = lax.dynamic_index_in_dim(decoder, layer, 0, keepdims=False)
    firing = gates(blocks, layer, slot, slots, latents, tokens)
    gate = jnp.where(half == 0, firing[0], firing[1])
    resid_half = jnp.concatenate(along + beside, axis=0)
    resid_half, dec_given, *wanted = lax.optimization_barrier((resid_half, dec_given, *wanted))

    partial = half_preacts(resid_half, weight, weight_other, enc_bias[0], half)
    acts = ((partial + crossed(partial, "layer", 1)) * jnp.concatenate(firing, axis=1)).astype(BF16)
    acts_other = crossed(acts, "layer", 2)
    resid_other = crossed(resid_half, "layer", 1)

    near, away = slice(0, near_rows), slice(near_rows, tokens)
    parts = [slice(0, part), slice(part, cols)]
    products = {at: [times(acts[at], dec_own[:, p]) for p in parts] for at in (near, away)}
    crossing = [crossed(product.astype(BF16), "latent", 1) for product in products[away]]
    for at in (away, near):
        products[at].append(times(acts[at], dec_kept) + times(acts_other[at], dec_given))
    crossing.append(crossed(products[away][2].astype(BF16), "latent", 1))
    sums = []
    for product, came in zip(products[near], crossing):
        total = product + came.astype(F32)
        pieces = [total[:rows]]
        for k in range(far - 1, 0, -1):
            pieces.append(crossed(total[k * rows:(k + 1) * rows].astype(BF16), "latent", 2 * k).astype(F32))
        sums.append(sum(pieces))
    errs = [(total - aim.astype(F32)).astype(BF16) for total, aim in zip(sums, wanted)]
    everywhere = []
    for err in errs:
        along = [err] + [None] * (far - 1)
        for k in range(far - 1, 0, -1):
            along[k] = crossed(err, "latent", 2 * k)
        block = jnp.concatenate(along, axis=0)
        everywhere.append(jnp.concatenate([block, crossed(block, "latent", 1)], axis=0))
    err_across = crossed(errs[2], "layer", 2)
    errors = jnp.concatenate(
        [jnp.where(layer == 0, errs[0], err_across), jnp.where(layer == 0, errs[1], errs[2])], axis=1
    )

    back = times_transposed(everywhere[2], dec_given).astype(BF16)
    here = times_transposed(everywhere[0], dec_own[:, parts[0]])
    here = here + times_transposed(everywhere[1], dec_own[:, parts[1]])
    here = here + times_transposed(everywhere[2], dec_kept)

    def of_half(pair, which):
        return jnp.where(which == 0, pair[:, :latents], pair[:, latents:])

    grad = of_half(here, half) + crossed(of_half(here, 1 - half), "layer", 1)
    grad = grad + crossed(of_half(back, half), "layer", 2).astype(F32)
    grad = grad + crossed(of_half(back, 1 - half), "layer", 3).astype(F32)
    grad_pre = grad * gate
    bias_grad = jnp.sum(grad_pre, axis=0)[None, :]
    enc_grad = encoder_gradient(resid_half, resid_other, grad_pre.astype(BF16), half)
    return errors[None], enc_grad[None], bias_grad


def any_layers(resid, target, enc_weight, enc_bias, dec_weight, blocks):
    slots = lax.axis_size("latent")
    count = lax.axis_size("layer")
    layer, half = lax.axis_index("layer") // 2, lax.axis_index("layer") % 2
    slot = lax.axis_index("latent")
    _, rows, width = resid.shape
    tokens, cols = rows * slots, width // 2
    latents = enc_weight.shape[2]
    decoder = dec_weight[0].reshape(2, 2 * latents, cols)

    def to_all(block):
        copies = jnp.broadcast_to(block[None], (slots,) + block.shape)
        return lax.all_to_all(copies, "latent", 0, 0).reshape(tokens, block.shape[1])

    def shifted(block, distance):
        route = [(i, i + distance) for i in range(count) if 0 <= i + distance < count]
        return lax.ppermute(block, "layer", route)

    resid_half = to_all(lax.dynamic_slice(resid, (layer, 0, half * cols), (1, rows, cols))[0])
    firing = gates(blocks, layer, slot, slots, latents, tokens)
    gate = jnp.where(half == 0, firing[0], firing[1])
    weight_other = crossed(enc_weight[0], "layer", 1)
    partial = half_preacts(resid_half, enc_weight[0], weight_other, enc_bias[0], half)
    preact = partial + crossed(partial, "layer", 1)
    acts = (preact * jnp.concatenate(firing, axis=1)).astype(BF16)
    resid_other = crossed(resid_half, "layer", 1)

    sums = jnp.concatenate([times(acts, decoder[t]).astype(BF16) for t in range(2)], axis=1)
    pieces = lax.all_to_all(sums.reshape(slots, rows, width), "latent", 0, 0)
    totals = jnp.sum(pieces.astype(F32), axis=0)
    own_sum, ahead_part = totals[:, :cols], totals[:, cols:]
    wanted = lax.dynamic_slice(target, (layer, 0, half * cols), (2, rows, cols)).astype(F32)
    err_own = (own_sum + shifted(ahead_part, 2) - wanted[0]).astype(BF16)
    err_next = (ahead_part + shifted(own_sum, -2) - wanted[1]).astype(BF16)
    errs = to_all(jnp.concatenate([err_own, err_next], axis=1))
    here = times_transposed(errs[:, :cols], decoder[0]) + times_transposed(errs[:, cols:], decoder[1])
    lower, upper = here[:, :latents], here[:, latents:]
    grad = jnp.where(half == 0, lower, upper) + crossed(jnp.where(half == 0, upper, lower), "layer", 1)
    grad_pre = grad * gate
    bias_grad = jnp.sum(grad_pre, axis=0)[None, :]
    enc_grad = encoder_gradient(resid_half, resid_other, grad_pre.astype(BF16), half)
    return err_own[None], enc_grad[None], bias_grad


def solution(mesh):
    small = mesh.shape["layer"] == 4 and mesh.shape["latent"] == 8
    return jax.shard_map(
        two_layers if small else any_layers,
        mesh=mesh,
        in_specs=(
            P(None, "latent", None),
            P(None, "latent", None),
            P("layer", None, "latent"),
            P("layer", "latent"),
            P("layer", None, None, "latent", None),
            P(),
        ),
        out_specs=(P("layer", "latent", None), P("layer", None, "latent"), P("layer", "latent")),
        check_vma=False,
    )
```

```python
import jax
import jax.numpy as jnp
from jax import lax
from jax.sharding import PartitionSpec as P

BLOCK = 128
F32, BF16 = jnp.float32, jnp.bfloat16


def crossed(block, axis, mask):
    return lax.ppermute(block, axis, [(i, i ^ mask) for i in range(lax.axis_size(axis))])


def times(left, right):
    return jnp.dot(left, right, preferred_element_type=F32)


def times_transposed(left, right):
    return lax.dot_general(left, right, (((1,), (1,)), ((), ())), preferred_element_type=F32)


def both_halves(half, mine, other, axis):
    return jnp.concatenate([jnp.where(half == 0, mine, other), jnp.where(half == 0, other, mine)], axis=axis)


def gates(blocks, layer, slot, slots, latents, tokens):
    listed = lax.dynamic_index_in_dim(blocks, layer, 0, keepdims=False)
    tile = tokens // listed.shape[0]
    here = latents // BLOCK
    out = []
    for side in range(2):
        names = (side * slots + slot) * here + jnp.arange(here)
        flags = jnp.any(listed[:, :, None] == names, axis=1).astype(F32)
        out.append(jnp.repeat(jnp.repeat(flags, tile, axis=0), BLOCK, axis=1))
    return out


def half_preacts(resid_half, weight, weight_other, bias, half):
    cols = resid_half.shape[1]
    mine = lax.dynamic_slice_in_dim(weight, half * cols, cols, 0)
    other = lax.dynamic_slice_in_dim(weight_other, half * cols, cols, 0)
    nothing = jnp.zeros_like(bias)
    return times(resid_half, both_halves(half, mine, other, 1)) + both_halves(half, bias, nothing, 0)


def encoder_gradient(resid_half, resid_other, grad_low, half):
    whole = both_halves(half, resid_half, resid_other, 1)
    grad = lax.dot_general(whole, grad_low, (((0,), (0,)), ((), ())), preferred_element_type=F32)
    return grad.astype(BF16)


def two_layers(resid, target, enc_weight, enc_bias, dec_weight, blocks):
    slots = lax.axis_size("latent")
    far = slots // 2
    layer, half = lax.axis_index("layer") // 2, lax.axis_index("layer") % 2
    slot = lax.axis_index("latent")
    side = slot % 2
    _, rows, width = resid.shape
    tokens, cols, part = rows * slots, width // 2, width // 4
    latents = enc_weight.shape[2]
    decoder = dec_weight[0].reshape(2, 2 * latents, cols)

    def over_x(block):
        return crossed(block, "latent", 1)

    def along_z(block):
        out = [block] + [None] * (far - 1)
        for k in range(far - 1, 0, -1):
            out[k] = crossed(block, "latent", 2 * k)
        return out

    def decoder_part(decoder, which, where):
        return lax.dynamic_slice(decoder, (which, 0, where * part), (1, 2 * latents, part))[0]

    def turned(array):
        return array.reshape(far, 2, rows, array.shape[1])[:, ::-1].reshape(array.shape)

    weight_other = crossed(enc_weight[0], "layer", 1)
    mine = lax.dynamic_slice(resid, (layer, 0, half * cols), (1, rows, cols))[0]
    pair = jnp.concatenate([mine, over_x(mine)], axis=0)
    pair, weight_other, later = lax.optimization_barrier((pair, weight_other, decoder))
    column = along_z(pair)

    shared_other = over_x(decoder_part(decoder, 1 - layer, 1 - side))
    own_other = over_x(decoder_part(later, layer, 1 - side))
    decoder, target, blocks, *column = lax.optimization_barrier((decoder, target, blocks, *column))
    shared_mine, own_mine = decoder_part(decoder, 1 - layer, side), decoder_part(decoder, layer, side)
    resid_half = jnp.concatenate(column, axis=0)
    firing = gates(blocks, layer, slot, slots, latents, tokens)
    gate = jnp.where(half == 0, firing[0], firing[1])

    def aims_for(where):
        start = half * cols + where * part
        own = lax.dynamic_slice(target, (2 * layer, 0, start), (1, rows, part))
        return jnp.concatenate([own, lax.dynamic_slice(target, (1, 0, start), (1, rows, part))], axis=0)

    aims, aims_other = aims_for(side), over_x(aims_for(1 - side))
    aim_own = jnp.concatenate([aims[0], aims_other[0]], axis=0).astype(F32)
    aim_shared = jnp.where(layer == 0, aims[1], aims_other[1]).astype(F32)

    partial = half_preacts(resid_half, enc_weight[0], weight_other, enc_bias[0], half)
    acts = ((partial + crossed(partial, "layer", 1)) * jnp.concatenate(firing, axis=1)).astype(BF16)
    acts_other = turned(over_x(acts))
    resid_other = crossed(resid_half, "layer", 1)

    def rows_of(array, which):
        split = array.reshape(far, 2, rows, array.shape[1])
        return jnp.where(which == 0, split[:, 0], split[:, 1]).reshape(tokens // 2, array.shape[1])

    def kept(array):
        return rows_of(array, layer)

    def left(array):
        return rows_of(array, 1 - layer)

    leaving = times(left(acts), shared_mine) + times(left(acts_other), shared_other)
    staying = times(kept(acts), shared_mine) + times(kept(acts_other), shared_other)
    staying = staying + crossed(leaving.astype(BF16), "layer", 2).astype(F32)
    sum_shared = staying[:rows]
    for k in range(far - 1, 0, -1):
        piece = staying[k * rows:(k + 1) * rows].astype(BF16)
        sum_shared = sum_shared + crossed(piece, "latent", 2 * k).astype(F32)
    err_shared = (sum_shared - aim_shared).astype(BF16)

    acts, acts_other, staying = lax.optimization_barrier((acts, acts_other, staying))
    product = times(acts, own_mine) + times(acts_other, own_other)
    sum_own = product[:2 * rows]
    for k in range(far - 1, 0, -1):
        piece = product[2 * k * rows:2 * (k + 1) * rows].astype(BF16)
        sum_own = sum_own + crossed(piece, "latent", 2 * k).astype(F32)
    err_own = (sum_own - aim_own).astype(BF16)

    shared_near = jnp.concatenate(along_z(err_shared), axis=0)
    shared_far = crossed(shared_near, "layer", 2)
    halves = [block.reshape(far, 1, rows, part) for block in (shared_near, shared_far)]
    errs_shared = jnp.where(
        layer == 0, jnp.concatenate(halves, axis=1), jnp.concatenate(halves[::-1], axis=1)
    ).reshape(tokens, part)
    errs_own = jnp.concatenate(along_z(err_own), axis=0)

    here = jnp.where(layer == 0, err_own[:rows], shared_far[:rows])
    there = over_x(jnp.where(layer == 0, err_own[rows:], err_shared))
    errors = jnp.concatenate([jnp.where(side == 0, here, there), jnp.where(side == 0, there, here)], axis=1)

    to_mine = times_transposed(errs_shared, shared_mine) + times_transposed(errs_own, own_mine)
    to_other = times_transposed(errs_shared, shared_other) + times_transposed(errs_own, own_other)
    to_other = turned(to_other.astype(BF16))

    def of_half(pair, which):
        return jnp.where(which == 0, pair[:, :latents], pair[:, latents:])

    diagonal = of_half(to_other, 1 - half)
    count = lax.axis_size("layer")
    route = [(i * slots + j, (i ^ 1) * slots + (j ^ 1)) for i in range(count) for j in range(slots)]
    grad = of_half(to_mine, half) + crossed(of_half(to_mine, 1 - half), "layer", 1)
    grad = grad + over_x(of_half(to_other, half)).astype(F32)
    grad = grad + lax.ppermute(diagonal, ("layer", "latent"), route).astype(F32)
    grad_pre = grad * gate
    bias_grad = jnp.sum(grad_pre, axis=0)[None, :]
    enc_grad = encoder_gradient(resid_half, resid_other, grad_pre.astype(BF16), half)
    return errors[None], enc_grad[None], bias_grad


def any_layers(resid, target, enc_weight, enc_bias, dec_weight, blocks):
    slots = lax.axis_size("latent")
    count = lax.axis_size("layer")
    layer, half = lax.axis_index("layer") // 2, lax.axis_index("layer") % 2
    slot = lax.axis_index("latent")
    _, rows, width = resid.shape
    tokens, cols = rows * slots, width // 2
    latents = enc_weight.shape[2]
    decoder = dec_weight[0].reshape(2, 2 * latents, cols)

    def to_all(block):
        copies = jnp.broadcast_to(block[None], (slots,) + block.shape)
        return lax.all_to_all(copies, "latent", 0, 0).reshape(tokens, block.shape[1])

    def shifted(block, distance):
        route = [(i, i + distance) for i in range(count) if 0 <= i + distance < count]
        return lax.ppermute(block, "layer", route)

    resid_half = to_all(lax.dynamic_slice(resid, (layer, 0, half * cols), (1, rows, cols))[0])
    firing = gates(blocks, layer, slot, slots, latents, tokens)
    gate = jnp.where(half == 0, firing[0], firing[1])
    weight_other = crossed(enc_weight[0], "layer", 1)
    partial = half_preacts(resid_half, enc_weight[0], weight_other, enc_bias[0], half)
    preact = partial + crossed(partial, "layer", 1)
    acts = (preact * jnp.concatenate(firing, axis=1)).astype(BF16)
    resid_other = crossed(resid_half, "layer", 1)

    sums = jnp.concatenate([times(acts, decoder[t]).astype(BF16) for t in range(2)], axis=1)
    pieces = lax.all_to_all(sums.reshape(slots, rows, width), "latent", 0, 0)
    totals = jnp.sum(pieces.astype(F32), axis=0)
    own_sum, ahead_part = totals[:, :cols], totals[:, cols:]
    wanted = lax.dynamic_slice(target, (layer, 0, half * cols), (2, rows, cols)).astype(F32)
    err_own = (own_sum + shifted(ahead_part, 2) - wanted[0]).astype(BF16)
    err_next = (ahead_part + shifted(own_sum, -2) - wanted[1]).astype(BF16)
    errs = to_all(jnp.concatenate([err_own, err_next], axis=1))
    here = times_transposed(errs[:, :cols], decoder[0]) + times_transposed(errs[:, cols:], decoder[1])
    lower, upper = here[:, :latents], here[:, latents:]
    grad = jnp.where(half == 0, lower, upper) + crossed(jnp.where(half == 0, upper, lower), "layer", 1)
    grad_pre = grad * gate
    bias_grad = jnp.sum(grad_pre, axis=0)[None, :]
    enc_grad = encoder_gradient(resid_half, resid_other, grad_pre.astype(BF16), half)
    return err_own[None], enc_grad[None], bias_grad


def solution(mesh):
    small = mesh.shape["layer"] == 4 and mesh.shape["latent"] == 8
    return jax.shard_map(
        two_layers if small else any_layers,
        mesh=mesh,
        in_specs=(
            P(None, "latent", None),
            P(None, "latent", None),
            P("layer", None, "latent"),
            P("layer", "latent"),
            P("layer", None, None, "latent", None),
            P(),
        ),
        out_specs=(P("layer", "latent", None), P("layer", None, "latent"), P("layer", "latent")),
        check_vma=False,
    )
```

```python
import jax
import jax.numpy as jnp
from jax import lax
from jax.experimental import pallas as pl
from jax.experimental.pallas import tpu as pltpu
from jax.sharding import PartitionSpec as P

BLOCK = 128
F32, BF16 = jnp.float32, jnp.bfloat16


def crossed(block, axis, mask):
    return lax.ppermute(block, axis, [(i, i ^ mask) for i in range(lax.axis_size(axis))])


def times(left, right):
    return jnp.dot(left, right, preferred_element_type=F32)


def times_transposed(left, right):
    return lax.dot_general(left, right, (((1,), (1,)), ((), ())), preferred_element_type=F32)


def both_halves(half, mine, other, axis):
    return jnp.concatenate([jnp.where(half == 0, mine, other), jnp.where(half == 0, other, mine)], axis=axis)


def gates(blocks, layer, slot, slots, latents, tokens):
    listed = lax.dynamic_index_in_dim(blocks, layer, 0, keepdims=False)
    tile = tokens // listed.shape[0]
    here = latents // BLOCK
    out = []
    for side in range(2):
        names = (side * slots + slot) * here + jnp.arange(here)
        flags = jnp.any(listed[:, :, None] == names, axis=1).astype(F32)
        out.append(jnp.repeat(jnp.repeat(flags, tile, axis=0), BLOCK, axis=1))
    return out


def side_by_side(half_ref, mine_ref, other_ref, out_ref, sems):
    rows, latents = out_ref.shape[0], mine_ref.shape[1]
    half = half_ref[0]
    here = pl.ds(pl.multiple_of(half * rows, rows), rows)
    copies = []
    for i, (ref, place) in enumerate(((mine_ref, half), (other_ref, 1 - half))):
        columns = pl.ds(pl.multiple_of(place * latents, latents), latents)
        copies.append(pltpu.make_async_copy(ref.at[here], out_ref.at[:, columns], sems.at[i]))
        copies[-1].start()
    for copy in copies:
        copy.wait()


def paired_weights(weight, weight_other, half, cols):
    latents = weight.shape[1]
    return pl.pallas_call(
        side_by_side,
        out_shape=jax.ShapeDtypeStruct((cols, 2 * latents), weight.dtype),
        in_specs=[
            pl.BlockSpec(memory_space=pltpu.SMEM),
            pl.BlockSpec(memory_space=pl.ANY),
            pl.BlockSpec(memory_space=pl.ANY),
        ],
        out_specs=pl.BlockSpec(memory_space=pltpu.VMEM),
        scratch_shapes=[pltpu.SemaphoreType.DMA((2,))],
        cost_estimate=pl.CostEstimate(flops=2 * 10**10, bytes_accessed=4 * cols * latents * 2, transcendentals=0),
        name="paired_weights",
    )(half.reshape(1), weight, weight_other)


def half_preacts(resid_half, weight, weight_other, bias, half):
    cols = resid_half.shape[1]
    mine = lax.dynamic_slice_in_dim(weight, half * cols, cols, 0)
    other = lax.dynamic_slice_in_dim(weight_other, half * cols, cols, 0)
    nothing = jnp.zeros_like(bias)
    return times(resid_half, both_halves(half, mine, other, 1)) + both_halves(half, bias, nothing, 0)


def encoder_gradient(resid_half, resid_other, grad_low, half):
    whole = both_halves(half, resid_half, resid_other, 1)
    grad = lax.dot_general(whole, grad_low, (((0,), (0,)), ((), ())), preferred_element_type=F32)
    return grad.astype(BF16)


def two_layers(resid, target, enc_weight, enc_bias, dec_weight, blocks):
    hold = lax.optimization_barrier
    slots = lax.axis_size("latent")
    far = slots // 2
    layer, half = lax.axis_index("layer") // 2, lax.axis_index("layer") % 2
    slot = lax.axis_index("latent")
    side = slot % 2
    _, rows, width = resid.shape
    tokens, cols, part = rows * slots, width // 2, width // 4
    latents = enc_weight.shape[2]
    decoder = dec_weight[0].reshape(2, 2 * latents, cols)

    def over_x(block):
        return crossed(block, "latent", 1)

    def along_z(block):
        out = [block] + [None] * (far - 1)
        for k in range(far - 1, 0, -1):
            out[k] = crossed(block, "latent", 2 * k)
        return out

    def sent_along_z(total):
        count = total.shape[0] // far
        pieces = [total[k * count:(k + 1) * count].astype(BF16) for k in range(1, far)]
        return [crossed(pieces[k - 1], "latent", 2 * k) for k in range(1, far)] + [total[:count]]

    def added(terms):
        return sum(term.astype(F32) for term in terms[::-1])

    def decoder_part(decoder, which, where):
        return lax.dynamic_slice(decoder, (which, 0, where * part), (1, 2 * latents, part))[0]

    def ordered(which, lower, upper, axis=0):
        return jnp.concatenate([jnp.where(which == 0, lower, upper), jnp.where(which == 0, upper, lower)], axis=axis)

    def rows_at(array, which):
        split = array.reshape(-1, 2, rows, array.shape[1])
        return jnp.where(which == 0, split[:, 0], split[:, 1]).reshape(-1, array.shape[1])

    weight_other = crossed(enc_weight[0], "layer", 1)
    mine = lax.dynamic_slice(resid, (layer, 0, half * cols), (1, rows, cols))[0]
    pair, weight_other, later, target, blocks = hold(
        (ordered(side, mine, over_x(mine)), weight_other, decoder, target, blocks)
    )
    weight_pair = paired_weights(enc_weight[0], weight_other, half, cols)
    column = along_z(pair)

    shared_other = over_x(decoder_part(decoder, 1 - layer, 1 - side))
    own_other = over_x(decoder_part(later, layer, 1 - side))

    def aims_for(where):
        start = half * cols + where * part
        own = lax.dynamic_slice(target, (2 * layer, 0, start), (1, rows, part))
        return jnp.concatenate([own, lax.dynamic_slice(target, (1, 0, start), (1, rows, part))], axis=0)

    aims, aims_other = aims_for(side), over_x(aims_for(1 - side))
    decoder, aims_other, shared_other, *column = hold((decoder, aims_other, shared_other, *column))
    shared_mine, own_mine = decoder_part(decoder, 1 - layer, side), decoder_part(decoder, layer, side)
    resid_half = jnp.concatenate(column, axis=0)
    firing = gates(blocks, layer, slot, slots, latents, tokens)
    gate = jnp.where(half == 0, firing[0], firing[1])

    bias_pair = ordered(half, enc_bias[0], jnp.zeros_like(enc_bias[0]))
    partial = times(resid_half, weight_pair) + bias_pair
    acts = ((partial + crossed(partial, "layer", 1)) * jnp.concatenate(firing, axis=1)).astype(BF16)
    acts_other = over_x(acts)
    resid_swapped, _ = hold((resid_half, acts_other))
    resid_other = crossed(resid_swapped, "layer", 1)
    aim_own = ordered(side, aims[0], aims_other[0]).astype(F32)
    aim_shared = jnp.where(layer == side, aims[1], aims_other[1]).astype(F32)

    leaving = times(rows_at(acts, 1 - layer), shared_mine) + times(rows_at(acts_other, 1 - layer), shared_other)
    staying = times(rows_at(acts, layer), shared_mine) + times(rows_at(acts_other, layer), shared_other)
    arrived = crossed(leaving.astype(BF16), "layer", 2)
    product = times(acts, own_mine) + times(acts_other, own_other)
    arrived, staying = hold((arrived, staying))
    shared_terms = sent_along_z(staying + arrived.astype(F32))
    own_terms = sent_along_z(product)
    err_shared = (added(shared_terms) - aim_shared).astype(BF16)
    err_own = (added(own_terms) - aim_own).astype(BF16)

    shared_near = jnp.concatenate(along_z(err_shared), axis=0)
    shared_far = crossed(shared_near, "layer", 2)
    pairs = [block.reshape(far, 1, rows, part) for block in (shared_near, shared_far)]
    errs_shared = ordered(layer, *pairs, axis=1).reshape(tokens, part)
    errs_own = jnp.concatenate(along_z(err_own), axis=0)

    to_mine = times_transposed(errs_shared, shared_mine) + times_transposed(errs_own, own_mine)
    to_other = times_transposed(errs_shared, shared_other) + times_transposed(errs_own, own_other)

    def of_half(pair, which):
        return jnp.where(which == 0, pair[:, :latents], pair[:, latents:])

    count = lax.axis_size("layer")
    diagonal = [(i * slots + j, (i ^ 1) * slots + (j ^ 1)) for i in range(count) for j in range(slots)]

    here = jnp.where(layer == 0, rows_at(err_own, side), rows_at(errs_shared[:2 * rows], side))
    sent = jnp.where(layer == 0, rows_at(err_own, 1 - side), rows_at(errs_shared[:2 * rows], 1 - side))
    tiles = [sent[:, at:at + latents] for at in range(0, part, latents)]
    from_x = over_x(jnp.concatenate([of_half(to_other, half).astype(BF16)] + tiles, axis=0))
    there = from_x[tokens:].reshape(part // latents, rows, latents)
    there = jnp.concatenate([there[i] for i in range(part // latents)], axis=1)
    errors = ordered(side, here, there, axis=1)
    from_x = from_x[:tokens]
    from_diagonal = lax.ppermute(of_half(to_other, 1 - half).astype(BF16), ("layer", "latent"), diagonal)
    grad = of_half(to_mine, half) + crossed(of_half(to_mine, 1 - half), "layer", 1)
    grad_pre = (grad + from_x.astype(F32) + from_diagonal.astype(F32)) * gate
    bias_grad = jnp.sum(grad_pre, axis=0)[None, :]
    enc_grad = encoder_gradient(resid_half, resid_other, grad_pre.astype(BF16), half)
    return errors[None], enc_grad[None], bias_grad


def any_layers(resid, target, enc_weight, enc_bias, dec_weight, blocks):
    slots = lax.axis_size("latent")
    count = lax.axis_size("layer")
    layer, half = lax.axis_index("layer") // 2, lax.axis_index("layer") % 2
    slot = lax.axis_index("latent")
    _, rows, width = resid.shape
    tokens, cols = rows * slots, width // 2
    latents = enc_weight.shape[2]
    decoder = dec_weight[0].reshape(2, 2 * latents, cols)

    def to_all(block):
        copies = jnp.broadcast_to(block[None], (slots,) + block.shape)
        return lax.all_to_all(copies, "latent", 0, 0).reshape(tokens, block.shape[1])

    def shifted(block, distance):
        route = [(i, i + distance) for i in range(count) if 0 <= i + distance < count]
        return lax.ppermute(block, "layer", route)

    resid_half = to_all(lax.dynamic_slice(resid, (layer, 0, half * cols), (1, rows, cols))[0])
    firing = gates(blocks, layer, slot, slots, latents, tokens)
    gate = jnp.where(half == 0, firing[0], firing[1])
    weight_other = crossed(enc_weight[0], "layer", 1)
    partial = half_preacts(resid_half, enc_weight[0], weight_other, enc_bias[0], half)
    preact = partial + crossed(partial, "layer", 1)
    acts = (preact * jnp.concatenate(firing, axis=1)).astype(BF16)
    resid_other = crossed(resid_half, "layer", 1)

    sums = jnp.concatenate([times(acts, decoder[t]).astype(BF16) for t in range(2)], axis=1)
    pieces = lax.all_to_all(sums.reshape(slots, rows, width), "latent", 0, 0)
    totals = jnp.sum(pieces.astype(F32), axis=0)
    own_sum, ahead_part = totals[:, :cols], totals[:, cols:]
    wanted = lax.dynamic_slice(target, (layer, 0, half * cols), (2, rows, cols)).astype(F32)
    err_own = (own_sum + shifted(ahead_part, 2) - wanted[0]).astype(BF16)
    err_next = (ahead_part + shifted(own_sum, -2) - wanted[1]).astype(BF16)
    errs = to_all(jnp.concatenate([err_own, err_next], axis=1))
    here = times_transposed(errs[:, :cols], decoder[0]) + times_transposed(errs[:, cols:], decoder[1])
    lower, upper = here[:, :latents], here[:, latents:]
    grad = jnp.where(half == 0, lower, upper) + crossed(jnp.where(half == 0, upper, lower), "layer", 1)
    grad_pre = grad * gate
    bias_grad = jnp.sum(grad_pre, axis=0)[None, :]
    enc_grad = encoder_gradient(resid_half, resid_other, grad_pre.astype(BF16), half)
    return err_own[None], enc_grad[None], bias_grad


def solution(mesh):
    small = mesh.shape["layer"] == 4 and mesh.shape["latent"] == 8
    return jax.shard_map(
        two_layers if small else any_layers,
        mesh=mesh,
        in_specs=(
            P(None, "latent", None),
            P(None, "latent", None),
            P("layer", None, "latent"),
            P("layer", "latent"),
            P("layer", None, None, "latent", None),
            P(),
        ),
        out_specs=(P("layer", "latent", None), P("layer", None, "latent"), P("layer", "latent")),
        check_vma=False,
    )
```

```python
import jax
import jax.numpy as jnp
from jax import lax
from jax.experimental import pallas as pl
from jax.experimental.pallas import tpu as pltpu
from jax.sharding import PartitionSpec as P

BLOCK = 128
F32, BF16 = jnp.float32, jnp.bfloat16


def crossed(block, axis, mask):
    return lax.ppermute(block, axis, [(i, i ^ mask) for i in range(lax.axis_size(axis))])


def times(left, right):
    return jnp.dot(left, right, preferred_element_type=F32)


def times_transposed(left, right):
    return lax.dot_general(left, right, (((1,), (1,)), ((), ())), preferred_element_type=F32)


def both_halves(half, mine, other, axis):
    return jnp.concatenate([jnp.where(half == 0, mine, other), jnp.where(half == 0, other, mine)], axis=axis)


def gates(blocks, layer, slot, slots, latents, tokens):
    listed = lax.dynamic_index_in_dim(blocks, layer, 0, keepdims=False)
    tile = tokens // listed.shape[0]
    here = latents // BLOCK
    out = []
    for side in range(2):
        names = (side * slots + slot) * here + jnp.arange(here)
        flags = jnp.any(listed[:, :, None] == names, axis=1).astype(F32)
        out.append(jnp.repeat(jnp.repeat(flags, tile, axis=0), BLOCK, axis=1))
    return out


def side_by_side(half_ref, mine_ref, other_ref, out_ref, sems):
    rows, latents = out_ref.shape[0], mine_ref.shape[1]
    half = half_ref[0]
    here = pl.ds(pl.multiple_of(half * rows, rows), rows)
    copies = []
    for i, (ref, place) in enumerate(((mine_ref, half), (other_ref, 1 - half))):
        columns = pl.ds(pl.multiple_of(place * latents, latents), latents)
        copies.append(pltpu.make_async_copy(ref.at[here], out_ref.at[:, columns], sems.at[i]))
        copies[-1].start()
    for copy in copies:
        copy.wait()


def paired_weights(weight, weight_other, half, cols):
    latents = weight.shape[1]
    return pl.pallas_call(
        side_by_side,
        out_shape=jax.ShapeDtypeStruct((cols, 2 * latents), weight.dtype),
        in_specs=[
            pl.BlockSpec(memory_space=pltpu.SMEM),
            pl.BlockSpec(memory_space=pl.ANY),
            pl.BlockSpec(memory_space=pl.ANY),
        ],
        out_specs=pl.BlockSpec(memory_space=pltpu.VMEM),
        scratch_shapes=[pltpu.SemaphoreType.DMA((2,))],
        cost_estimate=pl.CostEstimate(flops=2 * 10**10, bytes_accessed=4 * cols * latents * 2, transcendentals=0),
        name="paired_weights",
    )(half.reshape(1), weight, weight_other)


def half_preacts(resid_half, weight, weight_other, bias, half):
    cols = resid_half.shape[1]
    mine = lax.dynamic_slice_in_dim(weight, half * cols, cols, 0)
    other = lax.dynamic_slice_in_dim(weight_other, half * cols, cols, 0)
    nothing = jnp.zeros_like(bias)
    return times(resid_half, both_halves(half, mine, other, 1)) + both_halves(half, bias, nothing, 0)


def encoder_gradient(resid_half, resid_other, grad_low, half):
    whole = both_halves(half, resid_half, resid_other, 1)
    grad = lax.dot_general(whole, grad_low, (((0,), (0,)), ((), ())), preferred_element_type=F32)
    return grad.astype(BF16)


def two_layers(resid, target, enc_weight, enc_bias, dec_weight, blocks):
    hold = lax.optimization_barrier
    slots = lax.axis_size("latent")
    far = slots // 2
    layer, half = lax.axis_index("layer") // 2, lax.axis_index("layer") % 2
    slot = lax.axis_index("latent")
    side = slot % 2
    _, rows, width = resid.shape
    tokens, cols, part = rows * slots, width // 2, width // 4
    latents = enc_weight.shape[2]
    decoder = dec_weight[0].reshape(2, 2 * latents, cols)

    def over_x(block):
        return crossed(block, "latent", 1)

    def along_z(block):
        out = [block] + [None] * (far - 1)
        for k in range(far - 1, 0, -1):
            out[k] = crossed(block, "latent", 2 * k)
        return out

    def sent_along_z(total):
        count = total.shape[0] // far
        pieces = [total[k * count:(k + 1) * count].astype(BF16) for k in range(1, far)]
        return [crossed(pieces[k - 1], "latent", 2 * k) for k in range(1, far)] + [total[:count]]

    def added(terms):
        return sum(term.astype(F32) for term in terms[::-1])

    def decoder_part(decoder, which, where):
        return lax.dynamic_slice(decoder, (which, 0, where * part), (1, 2 * latents, part))[0]

    def ordered(which, lower, upper, axis=0):
        return jnp.concatenate([jnp.where(which == 0, lower, upper), jnp.where(which == 0, upper, lower)], axis=axis)

    def rows_at(array, which):
        split = array.reshape(-1, 2, rows, array.shape[1])
        return jnp.where(which == 0, split[:, 0], split[:, 1]).reshape(-1, array.shape[1])

    weight_other = crossed(enc_weight[0], "layer", 1)
    mine = lax.dynamic_slice(resid, (layer, 0, half * cols), (1, rows, cols))[0]
    pair, weight_other, later, bias, blocks = hold(
        (ordered(side, mine, over_x(mine)), weight_other, decoder, enc_bias[0], blocks)
    )
    weight_pair = paired_weights(enc_weight[0], weight_other, half, cols)
    column = along_z(pair)

    shared_other = over_x(decoder_part(decoder, 1 - layer, 1 - side))
    own_other = over_x(decoder_part(later, layer, 1 - side))

    def aims_for(where):
        start = half * cols + where * part
        own = lax.dynamic_slice(target, (2 * layer, 0, start), (1, rows, part))
        return jnp.concatenate([own, lax.dynamic_slice(target, (1, 0, start), (1, rows, part))], axis=0)

    decoder, shared_other, *column = hold((decoder, shared_other, *column))
    shared_mine, own_mine = decoder_part(decoder, 1 - layer, side), decoder_part(decoder, layer, side)
    resid_half = jnp.concatenate(column, axis=0)
    firing = gates(blocks, layer, slot, slots, latents, tokens)
    gate = jnp.where(half == 0, firing[0], firing[1])

    bias_pair = ordered(half, bias, jnp.zeros_like(bias))
    partial = times(resid_half, weight_pair) + bias_pair
    acts = ((partial + crossed(partial, "layer", 1)) * jnp.concatenate(firing, axis=1)).astype(BF16)
    acts_other, own_other = hold((over_x(acts), own_other))
    target, _ = hold((target, acts))
    aims, aims_other = aims_for(side), over_x(aims_for(1 - side))
    resid_swapped, _ = hold((resid_half, acts_other))
    resid_other = crossed(resid_swapped, "layer", 1)
    leaving = times(rows_at(acts, 1 - layer), shared_mine) + times(rows_at(acts_other, 1 - layer), shared_other)
    staying = times(rows_at(acts, layer), shared_mine) + times(rows_at(acts_other, layer), shared_other)
    arrived = crossed(leaving.astype(BF16), "layer", 2)
    product = times(acts, own_mine) + times(acts_other, own_other)
    arrived, staying, aims_other = hold((arrived, staying, aims_other))
    shared_terms = sent_along_z(staying + arrived.astype(F32))
    own_terms = sent_along_z(product)
    aim_own = ordered(side, aims[0], aims_other[0]).astype(F32)
    aim_shared = jnp.where(layer == side, aims[1], aims_other[1]).astype(F32)
    err_shared = (added(shared_terms) - aim_shared).astype(BF16)
    err_own = (added(own_terms) - aim_own).astype(BF16)

    shared_near = jnp.concatenate(along_z(err_shared), axis=0)
    shared_far = crossed(shared_near, "layer", 2)
    resid_turned, shared_far = hold((both_halves(half, resid_half, resid_other, 1).T, shared_far))
    pairs = [block.reshape(far, 1, rows, part) for block in (shared_near, shared_far)]
    errs_shared = ordered(layer, *pairs, axis=1).reshape(tokens, part)
    errs_own = jnp.concatenate(along_z(err_own), axis=0)

    to_mine = times_transposed(errs_shared, shared_mine) + times_transposed(errs_own, own_mine)
    to_other = times_transposed(errs_shared, shared_other) + times_transposed(errs_own, own_other)

    def of_half(pair, which):
        return jnp.where(which == 0, pair[:, :latents], pair[:, latents:])

    count = lax.axis_size("layer")
    diagonal = [(i * slots + j, (i ^ 1) * slots + (j ^ 1)) for i in range(count) for j in range(slots)]

    here = jnp.where(layer == 0, rows_at(err_own, side), rows_at(errs_shared[:2 * rows], side))
    sent = jnp.where(layer == 0, rows_at(err_own, 1 - side), rows_at(errs_shared[:2 * rows], 1 - side))
    tiles = [sent[:, at:at + latents] for at in range(0, part, latents)]
    from_x = over_x(jnp.concatenate([of_half(to_other, half).astype(BF16)] + tiles, axis=0))
    there = from_x[tokens:].reshape(part // latents, rows, latents)
    there = jnp.concatenate([there[i] for i in range(part // latents)], axis=1)
    errors = ordered(side, here, there, axis=1)
    from_x = from_x[:tokens]
    from_diagonal = lax.ppermute(of_half(to_other, 1 - half).astype(BF16), ("layer", "latent"), diagonal)
    grad = of_half(to_mine, half) + crossed(of_half(to_mine, 1 - half), "layer", 1)
    grad_pre = (grad + from_x.astype(F32) + from_diagonal.astype(F32)) * gate
    bias_grad = jnp.sum(grad_pre, axis=0)[None, :]
    enc_grad = times(resid_turned, grad_pre.astype(BF16)).astype(BF16)
    return errors[None], enc_grad[None], bias_grad


def any_layers(resid, target, enc_weight, enc_bias, dec_weight, blocks):
    slots = lax.axis_size("latent")
    count = lax.axis_size("layer")
    layer, half = lax.axis_index("layer") // 2, lax.axis_index("layer") % 2
    slot = lax.axis_index("latent")
    _, rows, width = resid.shape
    tokens, cols = rows * slots, width // 2
    latents = enc_weight.shape[2]
    decoder = dec_weight[0].reshape(2, 2 * latents, cols)

    def to_all(block):
        copies = jnp.broadcast_to(block[None], (slots,) + block.shape)
        return lax.all_to_all(copies, "latent", 0, 0).reshape(tokens, block.shape[1])

    def shifted(block, distance):
        route = [(i, i + distance) for i in range(count) if 0 <= i + distance < count]
        return lax.ppermute(block, "layer", route)

    resid_half = to_all(lax.dynamic_slice(resid, (layer, 0, half * cols), (1, rows, cols))[0])
    firing = gates(blocks, layer, slot, slots, latents, tokens)
    gate = jnp.where(half == 0, firing[0], firing[1])
    weight_other = crossed(enc_weight[0], "layer", 1)
    partial = half_preacts(resid_half, enc_weight[0], weight_other, enc_bias[0], half)
    preact = partial + crossed(partial, "layer", 1)
    acts = (preact * jnp.concatenate(firing, axis=1)).astype(BF16)
    resid_other = crossed(resid_half, "layer", 1)

    sums = jnp.concatenate([times(acts, decoder[t]).astype(BF16) for t in range(2)], axis=1)
    pieces = lax.all_to_all(sums.reshape(slots, rows, width), "latent", 0, 0)
    totals = jnp.sum(pieces.astype(F32), axis=0)
    own_sum, ahead_part = totals[:, :cols], totals[:, cols:]
    wanted = lax.dynamic_slice(target, (layer, 0, half * cols), (2, rows, cols)).astype(F32)
    err_own = (own_sum + shifted(ahead_part, 2) - wanted[0]).astype(BF16)
    err_next = (ahead_part + shifted(own_sum, -2) - wanted[1]).astype(BF16)
    errs = to_all(jnp.concatenate([err_own, err_next], axis=1))
    here = times_transposed(errs[:, :cols], decoder[0]) + times_transposed(errs[:, cols:], decoder[1])
    lower, upper = here[:, :latents], here[:, latents:]
    grad = jnp.where(half == 0, lower, upper) + crossed(jnp.where(half == 0, upper, lower), "layer", 1)
    grad_pre = grad * gate
    bias_grad = jnp.sum(grad_pre, axis=0)[None, :]
    enc_grad = encoder_gradient(resid_half, resid_other, grad_pre.astype(BF16), half)
    return err_own[None], enc_grad[None], bias_grad


def solution(mesh):
    small = mesh.shape["layer"] == 4 and mesh.shape["latent"] == 8
    return jax.shard_map(
        two_layers if small else any_layers,
        mesh=mesh,
        in_specs=(
            P(None, "latent", None),
            P(None, "latent", None),
            P("layer", None, "latent"),
            P("layer", "latent"),
            P("layer", None, None, "latent", None),
            P(),
        ),
        out_specs=(P("layer", "latent", None), P("layer", None, "latent"), P("layer", "latent")),
        check_vma=False,
    )
```

```python
import jax
import jax.numpy as jnp
from jax import lax
from jax.sharding import PartitionSpec as P

BLOCK = 128
F32, BF16 = jnp.float32, jnp.bfloat16


def crossed(block, axis, mask):
    return lax.ppermute(block, axis, [(i, i ^ mask) for i in range(lax.axis_size(axis))])


def times(left, right):
    return jnp.dot(left, right, preferred_element_type=F32)


def times_transposed(left, right):
    return lax.dot_general(left, right, (((1,), (1,)), ((), ())), preferred_element_type=F32)


def both_halves(half, mine, other, axis):
    return jnp.concatenate([jnp.where(half == 0, mine, other), jnp.where(half == 0, other, mine)], axis=axis)


def gates(blocks, layer, slot, slots, latents, tokens):
    listed = lax.dynamic_index_in_dim(blocks, layer, 0, keepdims=False)
    tile = tokens // listed.shape[0]
    here = latents // BLOCK
    out = []
    for side in range(2):
        names = (side * slots + slot) * here + jnp.arange(here)
        flags = jnp.any(listed[:, :, None] == names, axis=1).astype(F32)
        out.append(jnp.repeat(jnp.repeat(flags, tile, axis=0), BLOCK, axis=1))
    return out


def half_preacts(resid_half, weight, weight_other, bias, half):
    cols = resid_half.shape[1]
    mine = lax.dynamic_slice_in_dim(weight, half * cols, cols, 0)
    other = lax.dynamic_slice_in_dim(weight_other, half * cols, cols, 0)
    nothing = jnp.zeros_like(bias)
    return times(resid_half, both_halves(half, mine, other, 1)) + both_halves(half, bias, nothing, 0)


def encoder_gradient(resid_half, resid_other, grad_low, half):
    whole = both_halves(half, resid_half, resid_other, 1)
    grad = lax.dot_general(whole, grad_low, (((0,), (0,)), ((), ())), preferred_element_type=F32)
    return grad.astype(BF16)


def two_layers(resid, target, enc_weight, enc_bias, dec_weight, blocks):
    hold = lax.optimization_barrier
    slots = lax.axis_size("latent")
    far = slots // 2
    layer, half = lax.axis_index("layer") // 2, lax.axis_index("layer") % 2
    slot = lax.axis_index("latent")
    side = slot % 2
    _, rows, width = resid.shape
    tokens, cols, part = rows * slots, width // 2, width // 4
    latents = enc_weight.shape[2]
    decoder = dec_weight[0].reshape(2, 2 * latents, cols)

    def over_x(block):
        return crossed(block, "latent", 1)

    def over_y(block):
        return crossed(block, "layer", 2)

    def over_core(block):
        return crossed(block, "layer", 1)

    def along_z(block):
        out = [block] + [None] * (far - 1)
        for k in range(far - 1, 0, -1):
            out[k] = crossed(block, "latent", 2 * k)
        return out

    def sent_along_z(total):
        count = total.shape[0] // far
        pieces = [total[k * count:(k + 1) * count].astype(BF16) for k in range(1, far)]
        return [crossed(pieces[k - 1], "latent", 2 * k) for k in range(1, far)] + [total[:count]]

    def added(terms):
        return sum(term.astype(F32) for term in terms[::-1])

    def decoder_part(decoder, which, where):
        return lax.dynamic_slice(decoder, (which, 0, where * part), (1, 2 * latents, part))[0]

    def ordered(which, lower, upper, axis=0):
        return jnp.concatenate([jnp.where(which == 0, lower, upper), jnp.where(which == 0, upper, lower)], axis=axis)

    def rows_at(array, which):
        split = array.reshape(-1, 2, rows, array.shape[1])
        return jnp.where(which == 0, split[:, 0], split[:, 1]).reshape(-1, array.shape[1])

    weight_other = over_core(enc_weight[0])
    mine = lax.dynamic_slice(resid, (layer, 0, half * cols), (1, rows, cols))[0]
    pair, weight_other, bias, blocks = hold((ordered(side, mine, over_x(mine)), weight_other, enc_bias[0], blocks))
    column = along_z(pair)

    own_other = over_x(decoder_part(decoder, layer, 1 - side))
    shared_other = over_y(decoder_part(decoder, 1 - layer, 1 - layer))
    decoder, own_other, shared_other, *column = hold((decoder, own_other, shared_other, *column))
    own_mine, shared_mine = decoder_part(decoder, layer, side), decoder_part(decoder, 1 - layer, layer)
    resid_half = jnp.concatenate(column, axis=0)
    firing = gates(blocks, layer, slot, slots, latents, tokens)
    gate = jnp.where(half == 0, firing[0], firing[1])

    partial = half_preacts(resid_half, enc_weight[0], weight_other, bias, half)
    acts = ((partial + over_core(partial)) * jnp.concatenate(firing, axis=1)).astype(BF16)
    acts_y, acts_x = over_y(acts), over_x(acts)
    target, _ = hold((target, acts))
    start = half * cols

    def aim_own(where):
        return lax.dynamic_slice(target, (2 * layer, 0, start + where * part), (1, rows, part))[0]

    aim_other = over_x(aim_own(1 - side))
    aim_shared = lax.dynamic_slice(target, (1, 0, start + layer * part), (1, rows, part))[0]
    resid_swapped, _ = hold((resid_half, acts_x))
    resid_other = over_core(resid_swapped)

    leaving = times(rows_at(acts, 1 - side), shared_mine) + times(rows_at(acts_y, 1 - side), shared_other)
    staying = times(rows_at(acts, side), shared_mine) + times(rows_at(acts_y, side), shared_other)
    arrived = over_x(leaving.astype(BF16))
    product = times(acts, own_mine) + times(acts_x, own_other)
    arrived, staying, aim_other = hold((arrived, staying, aim_other))
    shared_terms = sent_along_z(staying + arrived.astype(F32))
    own_terms = sent_along_z(product)
    err_shared = (added(shared_terms) - aim_shared.astype(F32)).astype(BF16)
    err_own = (added(own_terms) - ordered(side, aim_own(side), aim_other).astype(F32)).astype(BF16)

    shared_near = jnp.concatenate(along_z(err_shared), axis=0)
    pairs = [block.reshape(far, 1, rows, part) for block in (shared_near, over_x(shared_near))]
    errs_shared = ordered(side, *pairs, axis=1).reshape(tokens, part)
    errs_own = jnp.concatenate(along_z(err_own), axis=0)

    grads = jnp.concatenate(
        [
            times_transposed(errs_own, own_mine) + times_transposed(errs_shared, shared_mine),
            times_transposed(errs_own, own_other),
            times_transposed(errs_shared, shared_other),
        ],
        axis=0,
    )
    lower, upper = grads[:, :latents], grads[:, latents:]
    grads = jnp.where(half == 0, lower, upper) + over_core(jnp.where(half == 0, upper, lower))

    def with_errors(grad, block):
        tiles = [block[:, at:at + latents] for at in range(0, part, latents)]
        return jnp.concatenate([grad.astype(BF16)] + tiles, axis=0)

    def without_errors(message):
        tiles = message[tokens:].reshape(part // latents, rows, latents)
        return message[:tokens].astype(F32), jnp.concatenate([tiles[i] for i in range(part // latents)], axis=1)

    from_x, own_there = without_errors(over_x(with_errors(grads[tokens:2 * tokens], rows_at(err_own, 1 - side))))
    from_y, shared_there = without_errors(over_y(with_errors(grads[2 * tokens:], err_shared)))
    errors = jnp.where(
        layer == 0,
        ordered(side, rows_at(err_own, side), own_there, axis=1),
        jnp.concatenate([shared_there, err_shared], axis=1),
    )
    grad_pre = (grads[:tokens] + from_x + from_y) * gate
    bias_grad = jnp.sum(grad_pre, axis=0)[None, :]
    enc_grad = encoder_gradient(resid_half, resid_other, grad_pre.astype(BF16), half)
    return errors[None], enc_grad[None], bias_grad


def any_layers(resid, target, enc_weight, enc_bias, dec_weight, blocks):
    slots = lax.axis_size("latent")
    count = lax.axis_size("layer")
    layer, half = lax.axis_index("layer") // 2, lax.axis_index("layer") % 2
    slot = lax.axis_index("latent")
    _, rows, width = resid.shape
    tokens, cols = rows * slots, width // 2
    latents = enc_weight.shape[2]
    decoder = dec_weight[0].reshape(2, 2 * latents, cols)

    def to_all(block):
        copies = jnp.broadcast_to(block[None], (slots,) + block.shape)
        return lax.all_to_all(copies, "latent", 0, 0).reshape(tokens, block.shape[1])

    def shifted(block, distance):
        route = [(i, i + distance) for i in range(count) if 0 <= i + distance < count]
        return lax.ppermute(block, "layer", route)

    resid_half = to_all(lax.dynamic_slice(resid, (layer, 0, half * cols), (1, rows, cols))[0])
    firing = gates(blocks, layer, slot, slots, latents, tokens)
    gate = jnp.where(half == 0, firing[0], firing[1])
    weight_other = crossed(enc_weight[0], "layer", 1)
    partial = half_preacts(resid_half, enc_weight[0], weight_other, enc_bias[0], half)
    preact = partial + crossed(partial, "layer", 1)
    acts = (preact * jnp.concatenate(firing, axis=1)).astype(BF16)
    resid_other = crossed(resid_half, "layer", 1)

    sums = jnp.concatenate([times(acts, decoder[t]).astype(BF16) for t in range(2)], axis=1)
    pieces = lax.all_to_all(sums.reshape(slots, rows, width), "latent", 0, 0)
    totals = jnp.sum(pieces.astype(F32), axis=0)
    own_sum, ahead_part = totals[:, :cols], totals[:, cols:]
    wanted = lax.dynamic_slice(target, (layer, 0, half * cols), (2, rows, cols)).astype(F32)
    err_own = (own_sum + shifted(ahead_part, 2) - wanted[0]).astype(BF16)
    err_next = (ahead_part + shifted(own_sum, -2) - wanted[1]).astype(BF16)
    errs = to_all(jnp.concatenate([err_own, err_next], axis=1))
    here = times_transposed(errs[:, :cols], decoder[0]) + times_transposed(errs[:, cols:], decoder[1])
    lower, upper = here[:, :latents], here[:, latents:]
    grad = jnp.where(half == 0, lower, upper) + crossed(jnp.where(half == 0, upper, lower), "layer", 1)
    grad_pre = grad * gate
    bias_grad = jnp.sum(grad_pre, axis=0)[None, :]
    enc_grad = encoder_gradient(resid_half, resid_other, grad_pre.astype(BF16), half)
    return err_own[None], enc_grad[None], bias_grad


def solution(mesh):
    small = mesh.shape["layer"] == 4 and mesh.shape["latent"] == 8
    return jax.shard_map(
        two_layers if small else any_layers,
        mesh=mesh,
        in_specs=(
            P(None, "latent", None),
            P(None, "latent", None),
            P("layer", None, "latent"),
            P("layer", "latent"),
            P("layer", None, None, "latent", None),
            P(),
        ),
        out_specs=(P("layer", "latent", None), P("layer", None, "latent"), P("layer", "latent")),
        check_vma=False,
    )
```

```python
import jax
import jax.numpy as jnp
from jax import lax
from jax.sharding import PartitionSpec as P

BLOCK = 128
F32, BF16 = jnp.float32, jnp.bfloat16


def crossed(block, axis, mask):
    return lax.ppermute(block, axis, [(i, i ^ mask) for i in range(lax.axis_size(axis))])


def times(left, right):
    return jnp.dot(left, right, preferred_element_type=F32)


def times_transposed(left, right):
    return lax.dot_general(left, right, (((1,), (1,)), ((), ())), preferred_element_type=F32)


def both_halves(half, mine, other, axis):
    return jnp.concatenate([jnp.where(half == 0, mine, other), jnp.where(half == 0, other, mine)], axis=axis)


def gates(blocks, layer, slot, slots, latents, tokens):
    listed = lax.dynamic_index_in_dim(blocks, layer, 0, keepdims=False)
    tile = tokens // listed.shape[0]
    here = latents // BLOCK
    out = []
    for side in range(2):
        names = (side * slots + slot) * here + jnp.arange(here)
        flags = jnp.any(listed[:, :, None] == names, axis=1).astype(F32)
        out.append(jnp.repeat(jnp.repeat(flags, tile, axis=0), BLOCK, axis=1))
    return out


def half_preacts(resid_half, weight, weight_other, bias, half):
    cols = resid_half.shape[1]
    mine = lax.dynamic_slice_in_dim(weight, half * cols, cols, 0)
    other = lax.dynamic_slice_in_dim(weight_other, half * cols, cols, 0)
    nothing = jnp.zeros_like(bias)
    return times(resid_half, both_halves(half, mine, other, 1)) + both_halves(half, bias, nothing, 0)


def encoder_gradient(resid_half, resid_other, grad_low, half):
    whole = both_halves(half, resid_half, resid_other, 1)
    grad = lax.dot_general(whole, grad_low, (((0,), (0,)), ((), ())), preferred_element_type=F32)
    return grad.astype(BF16)


def two_layers(resid, target, enc_weight, enc_bias, dec_weight, blocks):
    hold = lax.optimization_barrier
    slots = lax.axis_size("latent")
    far = slots // 2
    layer, half = lax.axis_index("layer") // 2, lax.axis_index("layer") % 2
    slot = lax.axis_index("latent")
    side = slot % 2
    _, rows, width = resid.shape
    tokens, cols, part = rows * slots, width // 2, width // 4
    latents = enc_weight.shape[2]
    decoder = dec_weight[0].reshape(2, 2 * latents, cols)

    def over_x(block):
        return crossed(block, "latent", 1)

    def over_y(block):
        return crossed(block, "layer", 2)

    def over_core(block):
        return crossed(block, "layer", 1)

    def along_z(block):
        out = [block] + [None] * (far - 1)
        for k in range(far - 1, 0, -1):
            out[k] = crossed(block, "latent", 2 * k)
        return out

    def sent_along_z(total):
        count = total.shape[0] // far
        pieces = [total[k * count:(k + 1) * count].astype(BF16) for k in range(1, far)]
        return [crossed(pieces[k - 1], "latent", 2 * k) for k in range(1, far)] + [total[:count]]

    def added(terms):
        return sum(term.astype(F32) for term in terms[::-1])

    def decoder_part(decoder, which, where):
        return lax.dynamic_slice(decoder, (which, 0, where * part), (1, 2 * latents, part))[0]

    def ordered(which, lower, upper, axis=0):
        return jnp.concatenate([jnp.where(which == 0, lower, upper), jnp.where(which == 0, upper, lower)], axis=axis)

    def rows_at(array, which):
        return array.reshape(-1, 2, rows, array.shape[1])[:, which].reshape(-1, array.shape[1])

    def paired(first, second):
        blocks = [block.reshape(-1, 1, rows, block.shape[1]) for block in (first, second)]
        return jnp.concatenate(blocks, axis=1).reshape(-1, first.shape[1])

    def turned(array):
        return paired(rows_at(array, 1), rows_at(array, 0))

    weight_other = over_core(enc_weight[0])
    mine = lax.dynamic_slice(resid, (layer, 0, half * cols), (1, rows, cols))[0]
    pair, weight_other, bias, blocks = hold((paired(mine, over_x(mine)), weight_other, enc_bias[0], blocks))
    column = along_z(pair)

    own_other = over_x(decoder_part(decoder, layer, 1 - side))
    shared_other = over_y(decoder_part(decoder, 1 - layer, 1 - layer))
    decoder, own_other, shared_other, *column = hold((decoder, own_other, shared_other, *column))
    own_mine, shared_mine = decoder_part(decoder, layer, side), decoder_part(decoder, 1 - layer, layer)
    resid_half = jnp.concatenate(column, axis=0)
    firing = gates(blocks, layer, slot, slots, latents, tokens)
    gate = jnp.where(half == 0, firing[0], firing[1])

    partial = half_preacts(resid_half, enc_weight[0], weight_other, bias, half)
    acts = ((partial + over_core(partial)) * jnp.concatenate(firing, axis=1)).astype(BF16)
    acts_turned = turned(acts)
    acts_y, acts_x = over_y(acts), over_x(acts_turned)
    target, _ = hold((target, acts_turned))
    start = half * cols

    def aim_own(where):
        return lax.dynamic_slice(target, (2 * layer, 0, start + where * part), (1, rows, part))[0]

    aim_other = over_x(aim_own(1 - side))
    aim_shared = lax.dynamic_slice(target, (1, 0, start + layer * part), (1, rows, part))[0]

    leaving = times(rows_at(acts, 1), shared_mine) + times(rows_at(acts_y, 1), shared_other)
    staying = times(rows_at(acts, 0), shared_mine) + times(rows_at(acts_y, 0), shared_other)
    arrived = over_x(leaving.astype(BF16))
    product = times(acts, own_mine) + times(acts_x, own_other)
    arrived, staying = hold((arrived, staying))
    own_terms = sent_along_z(product)
    shared_terms = sent_along_z(staying + arrived.astype(F32))
    terms = hold((*shared_terms, *own_terms))
    shared_terms, own_terms = terms[:far], terms[far:]
    err_own = (added(own_terms) - paired(aim_own(side), aim_other).astype(F32)).astype(BF16)
    own_column = along_z(err_own)
    err_shared = (added(shared_terms) - aim_shared.astype(F32)).astype(BF16)

    shared_near = jnp.concatenate(along_z(err_shared), axis=0)
    resid_swapped, _ = hold((resid_half, shared_near))
    resid_other = over_core(resid_swapped)
    errs_shared = paired(shared_near, over_x(shared_near))
    errs_own = jnp.concatenate(own_column, axis=0)

    grads = jnp.concatenate(
        [
            times_transposed(errs_own, own_mine) + times_transposed(errs_shared, shared_mine),
            turned(times_transposed(errs_own, own_other)),
            times_transposed(errs_shared, shared_other),
        ],
        axis=0,
    )
    lower, upper = grads[:, :latents], grads[:, latents:]
    grads = jnp.where(half == 0, lower, upper) + over_core(jnp.where(half == 0, upper, lower))

    def with_errors(grad, block):
        tiles = [block[:, at:at + latents] for at in range(0, part, latents)]
        return jnp.concatenate([grad.astype(BF16)] + tiles, axis=0)

    def without_errors(message):
        tiles = message[tokens:].reshape(part // latents, rows, latents)
        return message[:tokens].astype(F32), jnp.concatenate([tiles[i] for i in range(part // latents)], axis=1)

    from_x, own_there = without_errors(over_x(with_errors(grads[tokens:2 * tokens], rows_at(err_own, 1))))
    from_y, shared_there = without_errors(over_y(with_errors(grads[2 * tokens:], err_shared)))
    errors = jnp.where(
        layer == 0,
        ordered(side, rows_at(err_own, 0), own_there, axis=1),
        jnp.concatenate([shared_there, err_shared], axis=1),
    )
    grad_pre = (grads[:tokens] + from_x + from_y) * gate
    bias_grad = jnp.sum(grad_pre, axis=0)[None, :]
    enc_grad = encoder_gradient(resid_half, resid_other, grad_pre.astype(BF16), half)
    return errors[None], enc_grad[None], bias_grad


def any_layers(resid, target, enc_weight, enc_bias, dec_weight, blocks):
    slots = lax.axis_size("latent")
    count = lax.axis_size("layer")
    layer, half = lax.axis_index("layer") // 2, lax.axis_index("layer") % 2
    slot = lax.axis_index("latent")
    _, rows, width = resid.shape
    tokens, cols = rows * slots, width // 2
    latents = enc_weight.shape[2]
    decoder = dec_weight[0].reshape(2, 2 * latents, cols)

    def to_all(block):
        copies = jnp.broadcast_to(block[None], (slots,) + block.shape)
        return lax.all_to_all(copies, "latent", 0, 0).reshape(tokens, block.shape[1])

    def shifted(block, distance):
        route = [(i, i + distance) for i in range(count) if 0 <= i + distance < count]
        return lax.ppermute(block, "layer", route)

    resid_half = to_all(lax.dynamic_slice(resid, (layer, 0, half * cols), (1, rows, cols))[0])
    firing = gates(blocks, layer, slot, slots, latents, tokens)
    gate = jnp.where(half == 0, firing[0], firing[1])
    weight_other = crossed(enc_weight[0], "layer", 1)
    partial = half_preacts(resid_half, enc_weight[0], weight_other, enc_bias[0], half)
    preact = partial + crossed(partial, "layer", 1)
    acts = (preact * jnp.concatenate(firing, axis=1)).astype(BF16)
    resid_other = crossed(resid_half, "layer", 1)

    sums = jnp.concatenate([times(acts, decoder[t]).astype(BF16) for t in range(2)], axis=1)
    pieces = lax.all_to_all(sums.reshape(slots, rows, width), "latent", 0, 0)
    totals = jnp.sum(pieces.astype(F32), axis=0)
    own_sum, ahead_part = totals[:, :cols], totals[:, cols:]
    wanted = lax.dynamic_slice(target, (layer, 0, half * cols), (2, rows, cols)).astype(F32)
    err_own = (own_sum + shifted(ahead_part, 2) - wanted[0]).astype(BF16)
    err_next = (ahead_part + shifted(own_sum, -2) - wanted[1]).astype(BF16)
    errs = to_all(jnp.concatenate([err_own, err_next], axis=1))
    here = times_transposed(errs[:, :cols], decoder[0]) + times_transposed(errs[:, cols:], decoder[1])
    lower, upper = here[:, :latents], here[:, latents:]
    grad = jnp.where(half == 0, lower, upper) + crossed(jnp.where(half == 0, upper, lower), "layer", 1)
    grad_pre = grad * gate
    bias_grad = jnp.sum(grad_pre, axis=0)[None, :]
    enc_grad = encoder_gradient(resid_half, resid_other, grad_pre.astype(BF16), half)
    return err_own[None], enc_grad[None], bias_grad


def solution(mesh):
    small = mesh.shape["layer"] == 4 and mesh.shape["latent"] == 8
    return jax.shard_map(
        two_layers if small else any_layers,
        mesh=mesh,
        in_specs=(
            P(None, "latent", None),
            P(None, "latent", None),
            P("layer", None, "latent"),
            P("layer", "latent"),
            P("layer", None, None, "latent", None),
            P(),
        ),
        out_specs=(P("layer", "latent", None), P("layer", None, "latent"), P("layer", "latent")),
        check_vma=False,
    )
```

```python
import jax
import jax.numpy as jnp
from jax import lax
from jax.experimental import pallas as pl
from jax.experimental.pallas import tpu as pltpu
from jax.sharding import PartitionSpec as P

BLOCK = 128
F32, BF16 = jnp.float32, jnp.bfloat16


def crossed(block, axis, mask):
    return lax.ppermute(block, axis, [(i, i ^ mask) for i in range(lax.axis_size(axis))])


def times(left, right):
    return jnp.dot(left, right, preferred_element_type=F32)


def times_transposed(left, right):
    return lax.dot_general(left, right, (((1,), (1,)), ((), ())), preferred_element_type=F32)


def both_halves(half, mine, other, axis):
    return jnp.concatenate([jnp.where(half == 0, mine, other), jnp.where(half == 0, other, mine)], axis=axis)


def gates(blocks, layer, slot, slots, latents, tokens):
    listed = lax.dynamic_index_in_dim(blocks, layer, 0, keepdims=False)
    tile = tokens // listed.shape[0]
    here = latents // BLOCK
    out = []
    for side in range(2):
        names = (side * slots + slot) * here + jnp.arange(here)
        flags = jnp.any(listed[:, :, None] == names, axis=1).astype(F32)
        out.append(jnp.repeat(jnp.repeat(flags, tile, axis=0), BLOCK, axis=1))
    return out


def half_preacts(resid_half, weight, weight_other, bias, half):
    cols = resid_half.shape[1]
    mine = lax.dynamic_slice_in_dim(weight, half * cols, cols, 0)
    other = lax.dynamic_slice_in_dim(weight_other, half * cols, cols, 0)
    nothing = jnp.zeros_like(bias)
    return times(resid_half, both_halves(half, mine, other, 1)) + both_halves(half, bias, nothing, 0)


def encoder_gradient(resid_half, resid_other, grad_low, half):
    whole = both_halves(half, resid_half, resid_other, 1)
    grad = lax.dot_general(whole, grad_low, (((0,), (0,)), ((), ())), preferred_element_type=F32)
    return grad.astype(BF16)


def copy_parts(place_ref, decoder_ref, target_ref, x_ref, y_ref, sems):
    layer, half, side = place_ref[0], place_ref[1], place_ref[2]
    depth, part = y_ref.shape
    cols = decoder_ref.shape[2]

    def columns(where, start=0):
        return pl.ds(pl.multiple_of(start + where * part, 128), part)

    copies = [
        pltpu.make_async_copy(decoder_ref.at[layer, :, columns(1 - side)], x_ref.at[pl.ds(0, depth)], sems.at[0]),
        pltpu.make_async_copy(decoder_ref.at[1 - layer, :, columns(1 - layer)], y_ref, sems.at[1]),
        pltpu.make_async_copy(
            target_ref.at[2 * layer, :, columns(1 - side, half * cols)],
            x_ref.at[pl.ds(depth, target_ref.shape[1])],
            sems.at[2],
        ),
    ]
    for copy in copies:
        copy.start()
    for copy in copies:
        copy.wait()


def neighbours_parts(decoder, target, layer, half, side, part):
    depth, rows = decoder.shape[1], target.shape[1]
    place = jnp.stack([layer, half, side]).astype(jnp.int32)
    return pl.pallas_call(
        copy_parts,
        out_shape=[
            jax.ShapeDtypeStruct((depth + rows, part), decoder.dtype),
            jax.ShapeDtypeStruct((depth, part), decoder.dtype),
        ],
        in_specs=[
            pl.BlockSpec(memory_space=pltpu.SMEM),
            pl.BlockSpec(memory_space=pl.ANY),
            pl.BlockSpec(memory_space=pl.ANY),
        ],
        out_specs=[pl.BlockSpec(memory_space=pl.ANY)] * 2,
        scratch_shapes=[pltpu.SemaphoreType.DMA((3,))],
        cost_estimate=pl.CostEstimate(flops=0, bytes_accessed=4 * depth * part * 2, transcendentals=0),
        name="neighbours_parts",
    )(place, decoder, target)


def two_layers(resid, target, enc_weight, enc_bias, dec_weight, blocks):
    hold = lax.optimization_barrier
    slots = lax.axis_size("latent")
    far = slots // 2
    layer, half = lax.axis_index("layer") // 2, lax.axis_index("layer") % 2
    slot = lax.axis_index("latent")
    side = slot % 2
    _, rows, width = resid.shape
    tokens, cols, part = rows * slots, width // 2, width // 4
    latents = enc_weight.shape[2]
    decoder = dec_weight[0].reshape(2, 2 * latents, cols)

    def over_x(block):
        return crossed(block, "latent", 1)

    def over_y(block):
        return crossed(block, "layer", 2)

    def over_core(block):
        return crossed(block, "layer", 1)

    def along_z(blocks):
        out = [blocks[0]] + [None] * (far - 1)
        for k in range(far - 1, 0, -1):
            out[k] = crossed(blocks[k], "latent", 2 * k)
        return out

    def pieces_of(total):
        count = total.shape[0] // far
        return [total[:count]] + [total[k * count:(k + 1) * count].astype(BF16) for k in range(1, far)]

    def added(terms):
        return sum(term.astype(F32) for term in terms)

    def decoder_part(decoder, which, where):
        return lax.dynamic_slice(decoder, (which, 0, where * part), (1, 2 * latents, part))[0]

    def ordered(which, lower, upper, axis=0):
        return jnp.concatenate([jnp.where(which == 0, lower, upper), jnp.where(which == 0, upper, lower)], axis=axis)

    def rows_at(array, which):
        return array.reshape(-1, 2, rows, array.shape[1])[:, which].reshape(-1, array.shape[1])

    def paired(first, second):
        blocks = [block.reshape(-1, 1, rows, block.shape[1]) for block in (first, second)]
        return jnp.concatenate(blocks, axis=1).reshape(-1, first.shape[1])

    def turned(array):
        return paired(rows_at(array, 1), rows_at(array, 0))

    weight_other = over_core(enc_weight[0])
    mine = lax.dynamic_slice(resid, (layer, 0, half * cols), (1, rows, cols))[0]
    pair, weight_other, bias, blocks, early = hold(
        (paired(mine, over_x(mine)), weight_other, enc_bias[0], blocks, target)
    )
    column = along_z([pair] * far)

    start = half * cols

    aim_mine = lax.dynamic_slice(early, (2 * layer, 0, start + side * part), (1, rows, part))[0]
    aim_shared = lax.dynamic_slice(early, (1, 0, start + layer * part), (1, rows, part))[0]

    for_x, for_y = neighbours_parts(decoder, target, layer, half, side, part)
    from_side, shared_other = over_x(for_x), over_y(for_y)
    decoder, from_side, shared_other, aim_mine, aim_shared, *column = hold(
        (decoder, from_side, shared_other, aim_mine, aim_shared, *column)
    )
    own_other, aim_other = from_side[:2 * latents], from_side[2 * latents:]
    own_mine, shared_mine = decoder_part(decoder, layer, side), decoder_part(decoder, 1 - layer, layer)
    resid_half = jnp.concatenate(column, axis=0)
    firing = gates(blocks, layer, slot, slots, latents, tokens)
    gate = jnp.where(half == 0, firing[0], firing[1])

    partial = half_preacts(resid_half, enc_weight[0], weight_other, bias, half)
    acts = ((partial + over_core(partial)) * jnp.concatenate(firing, axis=1)).astype(BF16)
    acts_turned = turned(acts)
    acts_y, acts_x = over_y(acts), over_x(acts_turned)

    leaving = times(rows_at(acts, 1), shared_mine) + times(rows_at(acts_y, 1), shared_other)
    staying = times(rows_at(acts, 0), shared_mine) + times(rows_at(acts_y, 0), shared_other)
    arrived = over_x(leaving.astype(BF16))
    product = times(acts, own_mine) + times(acts_x, own_other)
    arrived, staying = hold((arrived, staying))
    shared_terms = along_z(pieces_of(staying + arrived.astype(F32)))
    count = tokens // 2
    arrived = crossed(product[count:].astype(BF16), "latent", 4)
    sum_own = product[:count] + arrived.astype(F32)
    count = tokens // 4
    arrived = crossed(sum_own[count:].astype(BF16), "latent", 2)
    arrived, *shared_terms = hold((arrived, *shared_terms))
    err_shared = (added(shared_terms) - aim_shared.astype(F32)).astype(BF16)
    sum_own = sum_own[:count] + arrived.astype(F32)
    err_own = (sum_own - paired(aim_mine, aim_other).astype(F32)).astype(BF16)

    arrived = crossed(err_own, "latent", 2)
    message = jnp.concatenate(along_z([err_shared] * far) + [rows_at(err_own, 1)], axis=0)
    message, arrived, resid_swapped = hold((message, arrived, resid_half))
    errs_own = jnp.concatenate([err_own, arrived], axis=0)
    errs_own = jnp.concatenate([errs_own, crossed(errs_own, "latent", 4)], axis=0)
    returned = over_x(message)
    resid_other = over_core(resid_swapped)

    own_grads = [times_transposed(errs_own, weights) for weights in (own_mine, own_other)]
    errs_shared = paired(message[:tokens // 2], returned[:tokens // 2])
    shared_grads = [times_transposed(errs_shared, weights) for weights in (shared_mine, shared_other)]
    grads = jnp.concatenate([own_grads[0] + shared_grads[0], turned(own_grads[1]), shared_grads[1]], axis=0)
    lower, upper = grads[:, :latents], grads[:, latents:]
    leaving, late_shared = hold((jnp.where(half == 0, upper, lower), err_shared))
    grads = jnp.where(half == 0, lower, upper) + over_core(leaving)
    shared_there = over_y(late_shared)

    from_x = over_x(grads[tokens:2 * tokens].astype(BF16)).astype(F32)
    from_y = over_y(grads[2 * tokens:].astype(BF16)).astype(F32)
    errors = jnp.where(
        layer == 0,
        ordered(side, rows_at(err_own, 0), returned[tokens // 2:], axis=1),
        jnp.concatenate([shared_there, err_shared], axis=1),
    )
    grad_pre = (grads[:tokens] + from_x + from_y) * gate
    bias_grad = jnp.sum(grad_pre, axis=0)[None, :]
    enc_grad = encoder_gradient(resid_half, resid_other, grad_pre.astype(BF16), half)
    return errors[None], enc_grad[None], bias_grad


def any_layers(resid, target, enc_weight, enc_bias, dec_weight, blocks):
    slots = lax.axis_size("latent")
    count = lax.axis_size("layer")
    layer, half = lax.axis_index("layer") // 2, lax.axis_index("layer") % 2
    slot = lax.axis_index("latent")
    _, rows, width = resid.shape
    tokens, cols = rows * slots, width // 2
    latents = enc_weight.shape[2]
    decoder = dec_weight[0].reshape(2, 2 * latents, cols)

    def to_all(block):
        copies = jnp.broadcast_to(block[None], (slots,) + block.shape)
        return lax.all_to_all(copies, "latent", 0, 0).reshape(tokens, block.shape[1])

    def shifted(block, distance):
        route = [(i, i + distance) for i in range(count) if 0 <= i + distance < count]
        return lax.ppermute(block, "layer", route)

    resid_half = to_all(lax.dynamic_slice(resid, (layer, 0, half * cols), (1, rows, cols))[0])
    firing = gates(blocks, layer, slot, slots, latents, tokens)
    gate = jnp.where(half == 0, firing[0], firing[1])
    weight_other = crossed(enc_weight[0], "layer", 1)
    partial = half_preacts(resid_half, enc_weight[0], weight_other, enc_bias[0], half)
    preact = partial + crossed(partial, "layer", 1)
    acts = (preact * jnp.concatenate(firing, axis=1)).astype(BF16)
    resid_other = crossed(resid_half, "layer", 1)

    sums = jnp.concatenate([times(acts, decoder[t]).astype(BF16) for t in range(2)], axis=1)
    pieces = lax.all_to_all(sums.reshape(slots, rows, width), "latent", 0, 0)
    totals = jnp.sum(pieces.astype(F32), axis=0)
    own_sum, ahead_part = totals[:, :cols], totals[:, cols:]
    wanted = lax.dynamic_slice(target, (layer, 0, half * cols), (2, rows, cols)).astype(F32)
    err_own = (own_sum + shifted(ahead_part, 2) - wanted[0]).astype(BF16)
    err_next = (ahead_part + shifted(own_sum, -2) - wanted[1]).astype(BF16)
    errs = to_all(jnp.concatenate([err_own, err_next], axis=1))
    here = times_transposed(errs[:, :cols], decoder[0]) + times_transposed(errs[:, cols:], decoder[1])
    lower, upper = here[:, :latents], here[:, latents:]
    grad = jnp.where(half == 0, lower, upper) + crossed(jnp.where(half == 0, upper, lower), "layer", 1)
    grad_pre = grad * gate
    bias_grad = jnp.sum(grad_pre, axis=0)[None, :]
    enc_grad = encoder_gradient(resid_half, resid_other, grad_pre.astype(BF16), half)
    return err_own[None], enc_grad[None], bias_grad


def solution(mesh):
    small = mesh.shape["layer"] == 4 and mesh.shape["latent"] == 8
    return jax.shard_map(
        two_layers if small else any_layers,
        mesh=mesh,
        in_specs=(
            P(None, "latent", None),
            P(None, "latent", None),
            P("layer", None, "latent"),
            P("layer", "latent"),
            P("layer", None, None, "latent", None),
            P(),
        ),
        out_specs=(P("layer", "latent", None), P("layer", None, "latent"), P("layer", "latent")),
        check_vma=False,
    )
```

```python
import jax
import jax.numpy as jnp
from jax import lax
from jax.sharding import PartitionSpec as P

BLOCK = 128
F32, BF16 = jnp.float32, jnp.bfloat16


def crossed(block, axis, mask):
    return lax.ppermute(block, axis, [(i, i ^ mask) for i in range(lax.axis_size(axis))])


def times(left, right):
    return jnp.dot(left, right, preferred_element_type=F32)


def times_transposed(left, right):
    return lax.dot_general(left, right, (((1,), (1,)), ((), ())), preferred_element_type=F32)


def both_halves(half, mine, other, axis):
    return jnp.concatenate([jnp.where(half == 0, mine, other), jnp.where(half == 0, other, mine)], axis=axis)


def firing_flags(blocks, layer, slot, slots, latents):
    listed = lax.dynamic_index_in_dim(blocks, layer, 0, keepdims=False)
    here = latents // BLOCK
    names = [(side * slots + slot) * here + jnp.arange(here) for side in range(2)]
    return [jnp.any(listed[:, :, None] == these, axis=1).astype(F32) for these in names]


def gates(flags, tokens):
    return [jnp.repeat(jnp.repeat(each, tokens // each.shape[0], axis=0), BLOCK, axis=1) for each in flags]


def half_preacts(resid_half, weight, weight_other, bias, half):
    cols = resid_half.shape[1]
    mine = lax.dynamic_slice_in_dim(weight, half * cols, cols, 0)
    other = lax.dynamic_slice_in_dim(weight_other, half * cols, cols, 0)
    nothing = jnp.zeros_like(bias)
    return times(resid_half, both_halves(half, mine, other, 1)) + both_halves(half, bias, nothing, 0)


def encoder_gradient(resid_half, resid_other, grad_low, half):
    whole = both_halves(half, resid_half, resid_other, 1)
    grad = lax.dot_general(whole, grad_low, (((0,), (0,)), ((), ())), preferred_element_type=F32)
    return grad.astype(BF16)


def two_layers(resid, target, enc_weight, enc_bias, dec_weight, blocks):
    hold = lax.optimization_barrier
    slots = lax.axis_size("latent")
    far = slots // 2
    layer, half = lax.axis_index("layer") // 2, lax.axis_index("layer") % 2
    slot = lax.axis_index("latent")
    side = slot % 2
    _, rows, width = resid.shape
    tokens, cols, part = rows * slots, width // 2, width // 4
    latents = enc_weight.shape[2]
    decoder = dec_weight[0].reshape(2, 2 * latents, cols)

    def over_x(block):
        return crossed(block, "latent", 1)

    def over_y(block):
        return crossed(block, "layer", 2)

    def over_core(block):
        return crossed(block, "layer", 1)

    def along_z(blocks):
        out = [blocks[0]] + [None] * (far - 1)
        for k in range(far - 1, 0, -1):
            out[k] = crossed(blocks[k], "latent", 2 * k)
        return out

    def pieces_of(total):
        count = total.shape[0] // far
        return [total[:count]] + [total[k * count:(k + 1) * count].astype(BF16) for k in range(1, far)]

    def added(terms):
        return sum(term.astype(F32) for term in terms)

    def decoder_part(decoder, which, where):
        return lax.dynamic_slice(decoder, (which, 0, where * part), (1, 2 * latents, part))[0]

    def ordered(which, lower, upper, axis=0):
        return jnp.concatenate([jnp.where(which == 0, lower, upper), jnp.where(which == 0, upper, lower)], axis=axis)

    def rows_at(array, which):
        return array.reshape(-1, 2, rows, array.shape[1])[:, which].reshape(-1, array.shape[1])

    def paired(first, second):
        blocks = [block.reshape(-1, 1, rows, block.shape[1]) for block in (first, second)]
        return jnp.concatenate(blocks, axis=1).reshape(-1, first.shape[1])

    def turned(array):
        return paired(rows_at(array, 1), rows_at(array, 0))

    weight_other = over_core(enc_weight[0])
    mine = lax.dynamic_slice(resid, (layer, 0, half * cols), (1, rows, cols))[0]
    pair, weight_other, bias, blocks, early = hold(
        (paired(mine, over_x(mine)), weight_other, enc_bias[0], blocks, target)
    )
    column = along_z([pair] * far)

    start = half * cols

    def aim_own(target, where):
        return lax.dynamic_slice(target, (2 * layer, 0, start + where * part), (1, rows, part))[0]

    aim_mine = aim_own(early, side)
    aim_shared = lax.dynamic_slice(early, (1, 0, start + layer * part), (1, rows, part))[0]

    own_other = over_x(decoder_part(decoder, layer, 1 - side))
    shared_other = over_y(decoder_part(decoder, 1 - layer, 1 - layer))
    flags = firing_flags(blocks, layer, slot, slots, latents)
    decoder, own_other, shared_other, aim_mine, aim_shared, flags, *column = hold(
        (decoder, own_other, shared_other, aim_mine, aim_shared, flags, *column[::-1])
    )
    column = column[::-1]
    own_mine, shared_mine = decoder_part(decoder, layer, side), decoder_part(decoder, 1 - layer, layer)
    resid_half = jnp.concatenate(column, axis=0)
    firing = gates(flags, tokens)
    gate = jnp.where(half == 0, firing[0], firing[1])

    partial = half_preacts(resid_half, enc_weight[0], weight_other, bias, half)
    acts = ((partial + over_core(partial)) * jnp.concatenate(firing, axis=1)).astype(BF16)
    acts_turned = turned(acts)
    acts_y, acts_x = over_y(acts), over_x(acts_turned)
    target, _ = hold((target, partial))
    aim_other = over_x(aim_own(target, 1 - side))

    leaving = times(rows_at(acts, 1), shared_mine) + times(rows_at(acts_y, 1), shared_other)
    staying = times(rows_at(acts, 0), shared_mine) + times(rows_at(acts_y, 0), shared_other)
    arrived = over_x(leaving.astype(BF16))
    product = times(acts, own_mine) + times(acts_x, own_other)
    own_pieces = pieces_of(product)
    arrived, staying, own_pieces[1] = hold((arrived, staying, own_pieces[1]))
    own_terms = along_z(own_pieces)
    shared_terms = along_z(pieces_of(staying + arrived.astype(F32)))
    terms = hold((*shared_terms[::-1], *own_terms[::-1]))
    err_shared = (added(terms[far - 1::-1]) - aim_shared.astype(F32)).astype(BF16)
    err_own = (added(terms[:far - 1:-1]) - paired(aim_mine, aim_other).astype(F32)).astype(BF16)

    own_column = along_z([err_own] * far)
    message = jnp.concatenate(along_z([err_shared] * far), axis=0)
    message, resid_swapped = hold((message, resid_half))
    returned = over_x(message)
    resid_other = over_core(resid_swapped)
    errs_own = jnp.concatenate(own_column, axis=0)

    own_grads = [times_transposed(errs_own, weights) for weights in (own_mine, own_other)]
    errs_shared = paired(message, returned)
    shared_grads = [times_transposed(errs_shared, weights) for weights in (shared_mine, shared_other)]
    grads = jnp.concatenate([own_grads[0] + shared_grads[0], turned(own_grads[1]), shared_grads[1]], axis=0)
    lower, upper = grads[:, :latents], grads[:, latents:]
    grads = jnp.where(half == 0, lower, upper) + over_core(jnp.where(half == 0, upper, lower))


    def with_errors(grad, block):
        tiles = [block[:, at:at + latents] for at in range(0, part, latents)]
        return jnp.concatenate([grad.astype(BF16)] + tiles, axis=0)

    def without_errors(message):
        tiles = message[tokens:].reshape(part // latents, rows, latents)
        return message[:tokens].astype(F32), jnp.concatenate([tiles[i] for i in range(part // latents)], axis=1)

    from_x, own_there = without_errors(over_x(with_errors(grads[tokens:2 * tokens], rows_at(err_own, 1))))
    from_y, shared_there = without_errors(over_y(with_errors(grads[2 * tokens:], err_shared)))
    errors = jnp.where(
        layer == 0,
        ordered(side, rows_at(err_own, 0), own_there, axis=1),
        jnp.concatenate([shared_there, err_shared], axis=1),
    )
    grad_pre = (grads[:tokens] + from_x + from_y) * gate
    bias_grad = jnp.sum(grad_pre, axis=0)[None, :]
    enc_grad = encoder_gradient(resid_half, resid_other, grad_pre.astype(BF16), half)
    return errors[None], enc_grad[None], bias_grad


def any_layers(resid, target, enc_weight, enc_bias, dec_weight, blocks):
    slots = lax.axis_size("latent")
    count = lax.axis_size("layer")
    layer, half = lax.axis_index("layer") // 2, lax.axis_index("layer") % 2
    slot = lax.axis_index("latent")
    _, rows, width = resid.shape
    tokens, cols = rows * slots, width // 2
    latents = enc_weight.shape[2]
    decoder = dec_weight[0].reshape(2, 2 * latents, cols)

    def to_all(block):
        copies = jnp.broadcast_to(block[None], (slots,) + block.shape)
        return lax.all_to_all(copies, "latent", 0, 0).reshape(tokens, block.shape[1])

    def shifted(block, distance):
        route = [(i, i + distance) for i in range(count) if 0 <= i + distance < count]
        return lax.ppermute(block, "layer", route)

    resid_half = to_all(lax.dynamic_slice(resid, (layer, 0, half * cols), (1, rows, cols))[0])
    firing = gates(firing_flags(blocks, layer, slot, slots, latents), tokens)
    gate = jnp.where(half == 0, firing[0], firing[1])
    weight_other = crossed(enc_weight[0], "layer", 1)
    partial = half_preacts(resid_half, enc_weight[0], weight_other, enc_bias[0], half)
    preact = partial + crossed(partial, "layer", 1)
    acts = (preact * jnp.concatenate(firing, axis=1)).astype(BF16)
    resid_other = crossed(resid_half, "layer", 1)

    sums = jnp.concatenate([times(acts, decoder[t]).astype(BF16) for t in range(2)], axis=1)
    pieces = lax.all_to_all(sums.reshape(slots, rows, width), "latent", 0, 0)
    totals = jnp.sum(pieces.astype(F32), axis=0)
    own_sum, ahead_part = totals[:, :cols], totals[:, cols:]
    wanted = lax.dynamic_slice(target, (layer, 0, half * cols), (2, rows, cols)).astype(F32)
    err_own = (own_sum + shifted(ahead_part, 2) - wanted[0]).astype(BF16)
    err_next = (ahead_part + shifted(own_sum, -2) - wanted[1]).astype(BF16)
    errs = to_all(jnp.concatenate([err_own, err_next], axis=1))
    here = times_transposed(errs[:, :cols], decoder[0]) + times_transposed(errs[:, cols:], decoder[1])
    lower, upper = here[:, :latents], here[:, latents:]
    grad = jnp.where(half == 0, lower, upper) + crossed(jnp.where(half == 0, upper, lower), "layer", 1)
    grad_pre = grad * gate
    bias_grad = jnp.sum(grad_pre, axis=0)[None, :]
    enc_grad = encoder_gradient(resid_half, resid_other, grad_pre.astype(BF16), half)
    return err_own[None], enc_grad[None], bias_grad


def solution(mesh):
    small = mesh.shape["layer"] == 4 and mesh.shape["latent"] == 8
    return jax.shard_map(
        two_layers if small else any_layers,
        mesh=mesh,
        in_specs=(
            P(None, "latent", None),
            P(None, "latent", None),
            P("layer", None, "latent"),
            P("layer", "latent"),
            P("layer", None, None, "latent", None),
            P(),
        ),
        out_specs=(P("layer", "latent", None), P("layer", None, "latent"), P("layer", "latent")),
        check_vma=False,
    )
```

```python
import jax
import jax.numpy as jnp
from jax import lax
from jax.sharding import PartitionSpec as P

BLOCK = 128
F32, BF16 = jnp.float32, jnp.bfloat16


def crossed(block, axis, mask):
    return lax.ppermute(block, axis, [(i, i ^ mask) for i in range(lax.axis_size(axis))])


def times(left, right):
    return jnp.dot(left, right, preferred_element_type=F32)


def times_transposed(left, right):
    return lax.dot_general(left, right, (((1,), (1,)), ((), ())), preferred_element_type=F32)


def both_halves(half, mine, other, axis):
    return jnp.concatenate([jnp.where(half == 0, mine, other), jnp.where(half == 0, other, mine)], axis=axis)


def gates(blocks, layer, slot, slots, latents, tokens):
    listed = lax.dynamic_index_in_dim(blocks, layer, 0, keepdims=False)
    tile = tokens // listed.shape[0]
    here = latents // BLOCK
    out = []
    for side in range(2):
        names = (side * slots + slot) * here + jnp.arange(here)
        flags = jnp.any(listed[:, :, None] == names, axis=1).astype(F32)
        out.append(jnp.repeat(jnp.repeat(flags, tile, axis=0), BLOCK, axis=1))
    return out


def half_preacts(resid_half, weight, weight_other, bias, half):
    cols = resid_half.shape[1]
    mine = lax.dynamic_slice_in_dim(weight, half * cols, cols, 0)
    other = lax.dynamic_slice_in_dim(weight_other, half * cols, cols, 0)
    nothing = jnp.zeros_like(bias)
    return times(resid_half, both_halves(half, mine, other, 1)) + both_halves(half, bias, nothing, 0)


def encoder_gradient(resid_half, resid_other, grad_low, half):
    whole = both_halves(half, resid_half, resid_other, 1)
    grad = lax.dot_general(whole, grad_low, (((0,), (0,)), ((), ())), preferred_element_type=F32)
    return grad.astype(BF16)


def two_layers(resid, target, enc_weight, enc_bias, dec_weight, blocks):
    hold = lax.optimization_barrier
    slots = lax.axis_size("latent")
    far = slots // 2
    layer, half = lax.axis_index("layer") // 2, lax.axis_index("layer") % 2
    slot = lax.axis_index("latent")
    side = slot % 2
    _, rows, width = resid.shape
    tokens, cols, part = rows * slots, width // 2, width // 4
    latents = enc_weight.shape[2]
    decoder = dec_weight[0].reshape(2, 2 * latents, cols)

    def over_x(block):
        return crossed(block, "latent", 1)

    def over_y(block):
        return crossed(block, "layer", 2)

    def over_core(block):
        return crossed(block, "layer", 1)

    def along_z(block):
        out = [block] + [None] * (far - 1)
        for k in range(far - 1, 0, -1):
            out[k] = crossed(block, "latent", 2 * k)
        return out

    def pieces_of(total):
        count = total.shape[0] // far
        return [total[k * count:(k + 1) * count].astype(BF16) for k in range(1, far)] + [total[:count]]

    def sent_along_z(pieces):
        return [crossed(pieces[k - 1], "latent", 2 * k) for k in range(1, far)] + pieces[far - 1:]

    def added(terms):
        return sum(term.astype(F32) for term in terms[::-1])

    def decoder_part(decoder, which, where):
        return lax.dynamic_slice(decoder, (which, 0, where * part), (1, 2 * latents, part))[0]

    def ordered(which, lower, upper, axis=0):
        return jnp.concatenate([jnp.where(which == 0, lower, upper), jnp.where(which == 0, upper, lower)], axis=axis)

    def rows_at(array, which):
        return array.reshape(-1, 2, rows, array.shape[1])[:, which].reshape(-1, array.shape[1])

    def paired(first, second):
        blocks = [block.reshape(-1, 1, rows, block.shape[1]) for block in (first, second)]
        return jnp.concatenate(blocks, axis=1).reshape(-1, first.shape[1])

    def turned(array):
        return paired(rows_at(array, 1), rows_at(array, 0))

    weight_other = over_core(enc_weight[0])
    mine = lax.dynamic_slice(resid, (layer, 0, half * cols), (1, rows, cols))[0]
    pair, weight_other, bias, blocks = hold((paired(mine, over_x(mine)), weight_other, enc_bias[0], blocks))
    column = along_z(pair)

    own_other = over_x(decoder_part(decoder, layer, 1 - side))
    shared_other = over_y(decoder_part(decoder, 1 - layer, 1 - layer))
    decoder, own_other, shared_other, *column = hold((decoder, own_other, shared_other, *column))
    own_mine, shared_mine = decoder_part(decoder, layer, side), decoder_part(decoder, 1 - layer, layer)
    resid_half = jnp.concatenate(column, axis=0)
    firing = gates(blocks, layer, slot, slots, latents, tokens)
    gate = jnp.where(half == 0, firing[0], firing[1])

    partial = half_preacts(resid_half, enc_weight[0], weight_other, bias, half)
    acts = ((partial + over_core(partial)) * jnp.concatenate(firing, axis=1)).astype(BF16)
    acts_turned = turned(acts)
    acts_y, acts_x = over_y(acts), over_x(acts_turned)
    target, _ = hold((target, acts_turned))
    start = half * cols

    def aim_own(where):
        return lax.dynamic_slice(target, (2 * layer, 0, start + where * part), (1, rows, part))[0]

    aim_other = over_x(aim_own(1 - side))
    aim_shared = lax.dynamic_slice(target, (1, 0, start + layer * part), (1, rows, part))[0]

    leaving = times(rows_at(acts, 1), shared_mine) + times(rows_at(acts_y, 1), shared_other)
    staying = times(rows_at(acts, 0), shared_mine) + times(rows_at(acts_y, 0), shared_other)
    arrived = over_x(leaving.astype(BF16))
    product = times(acts, own_mine) + times(acts_x, own_other)
    own_pieces = pieces_of(product)
    arrived, staying, own_pieces[0] = hold((arrived, staying, own_pieces[0]))
    own_terms = sent_along_z(own_pieces)
    shared_terms = sent_along_z(pieces_of(staying + arrived.astype(F32)))
    terms = hold((*shared_terms, *own_terms))
    shared_terms, own_terms = terms[:far], terms[far:]
    err_own = (added(own_terms) - paired(aim_own(side), aim_other).astype(F32)).astype(BF16)
    own_column = along_z(err_own)
    err_shared = (added(shared_terms) - aim_shared.astype(F32)).astype(BF16)

    shared_near = jnp.concatenate(along_z(err_shared), axis=0)
    resid_swapped, _ = hold((resid_half, shared_near))
    resid_other = over_core(resid_swapped)
    errs_shared = paired(shared_near, over_x(shared_near))
    errs_own = jnp.concatenate(own_column, axis=0)

    grads = jnp.concatenate(
        [
            times_transposed(errs_own, own_mine) + times_transposed(errs_shared, shared_mine),
            turned(times_transposed(errs_own, own_other)),
            times_transposed(errs_shared, shared_other),
        ],
        axis=0,
    )
    lower, upper = grads[:, :latents], grads[:, latents:]
    grads = jnp.where(half == 0, lower, upper) + over_core(jnp.where(half == 0, upper, lower))

    def with_errors(grad, block):
        tiles = [block[:, at:at + latents] for at in range(0, part, latents)]
        return jnp.concatenate([grad.astype(BF16)] + tiles, axis=0)

    def without_errors(message):
        tiles = message[tokens:].reshape(part // latents, rows, latents)
        return message[:tokens].astype(F32), jnp.concatenate([tiles[i] for i in range(part // latents)], axis=1)

    from_x, own_there = without_errors(over_x(with_errors(grads[tokens:2 * tokens], rows_at(err_own, 1))))
    from_y, shared_there = without_errors(over_y(with_errors(grads[2 * tokens:], err_shared)))
    errors = jnp.where(
        layer == 0,
        ordered(side, rows_at(err_own, 0), own_there, axis=1),
        jnp.concatenate([shared_there, err_shared], axis=1),
    )
    grad_pre = (grads[:tokens] + from_x + from_y) * gate
    bias_grad = jnp.sum(grad_pre, axis=0)[None, :]
    enc_grad = encoder_gradient(resid_half, resid_other, grad_pre.astype(BF16), half)
    return errors[None], enc_grad[None], bias_grad


def any_layers(resid, target, enc_weight, enc_bias, dec_weight, blocks):
    slots = lax.axis_size("latent")
    count = lax.axis_size("layer")
    layer, half = lax.axis_index("layer") // 2, lax.axis_index("layer") % 2
    slot = lax.axis_index("latent")
    _, rows, width = resid.shape
    tokens, cols = rows * slots, width // 2
    latents = enc_weight.shape[2]
    decoder = dec_weight[0].reshape(2, 2 * latents, cols)

    def to_all(block):
        copies = jnp.broadcast_to(block[None], (slots,) + block.shape)
        return lax.all_to_all(copies, "latent", 0, 0).reshape(tokens, block.shape[1])

    def shifted(block, distance):
        route = [(i, i + distance) for i in range(count) if 0 <= i + distance < count]
        return lax.ppermute(block, "layer", route)

    resid_half = to_all(lax.dynamic_slice(resid, (layer, 0, half * cols), (1, rows, cols))[0])
    firing = gates(blocks, layer, slot, slots, latents, tokens)
    gate = jnp.where(half == 0, firing[0], firing[1])
    weight_other = crossed(enc_weight[0], "layer", 1)
    partial = half_preacts(resid_half, enc_weight[0], weight_other, enc_bias[0], half)
    preact = partial + crossed(partial, "layer", 1)
    acts = (preact * jnp.concatenate(firing, axis=1)).astype(BF16)
    resid_other = crossed(resid_half, "layer", 1)

    sums = jnp.concatenate([times(acts, decoder[t]).astype(BF16) for t in range(2)], axis=1)
    pieces = lax.all_to_all(sums.reshape(slots, rows, width), "latent", 0, 0)
    totals = jnp.sum(pieces.astype(F32), axis=0)
    own_sum, ahead_part = totals[:, :cols], totals[:, cols:]
    wanted = lax.dynamic_slice(target, (layer, 0, half * cols), (2, rows, cols)).astype(F32)
    err_own = (own_sum + shifted(ahead_part, 2) - wanted[0]).astype(BF16)
    err_next = (ahead_part + shifted(own_sum, -2) - wanted[1]).astype(BF16)
    errs = to_all(jnp.concatenate([err_own, err_next], axis=1))
    here = times_transposed(errs[:, :cols], decoder[0]) + times_transposed(errs[:, cols:], decoder[1])
    lower, upper = here[:, :latents], here[:, latents:]
    grad = jnp.where(half == 0, lower, upper) + crossed(jnp.where(half == 0, upper, lower), "layer", 1)
    grad_pre = grad * gate
    bias_grad = jnp.sum(grad_pre, axis=0)[None, :]
    enc_grad = encoder_gradient(resid_half, resid_other, grad_pre.astype(BF16), half)
    return err_own[None], enc_grad[None], bias_grad


def solution(mesh):
    small = mesh.shape["layer"] == 4 and mesh.shape["latent"] == 8
    return jax.shard_map(
        two_layers if small else any_layers,
        mesh=mesh,
        in_specs=(
            P(None, "latent", None),
            P(None, "latent", None),
            P("layer", None, "latent"),
            P("layer", "latent"),
            P("layer", None, None, "latent", None),
            P(),
        ),
        out_specs=(P("layer", "latent", None), P("layer", None, "latent"), P("layer", "latent")),
        check_vma=False,
    )
```

```python
import jax
import jax.numpy as jnp
from jax import lax
from jax.sharding import PartitionSpec as P

BLOCK = 128
F32, BF16 = jnp.float32, jnp.bfloat16


def crossed(block, axis, mask):
    return lax.ppermute(block, axis, [(i, i ^ mask) for i in range(lax.axis_size(axis))])


def times(left, right):
    return jnp.dot(left, right, preferred_element_type=F32)


def times_transposed(left, right):
    return lax.dot_general(left, right, (((1,), (1,)), ((), ())), preferred_element_type=F32)


def both_halves(half, mine, other, axis):
    return jnp.concatenate([jnp.where(half == 0, mine, other), jnp.where(half == 0, other, mine)], axis=axis)


def gates(blocks, layer, slot, slots, latents, tokens):
    listed = lax.dynamic_index_in_dim(blocks, layer, 0, keepdims=False)
    tile = tokens // listed.shape[0]
    here = latents // BLOCK
    out = []
    for side in range(2):
        names = (side * slots + slot) * here + jnp.arange(here)
        flags = jnp.any(listed[:, :, None] == names, axis=1).astype(F32)
        out.append(jnp.repeat(jnp.repeat(flags, tile, axis=0), BLOCK, axis=1))
    return out


def half_preacts(resid_half, weight, weight_other, bias, half):
    cols = resid_half.shape[1]
    mine = lax.dynamic_slice_in_dim(weight, half * cols, cols, 0)
    other = lax.dynamic_slice_in_dim(weight_other, half * cols, cols, 0)
    nothing = jnp.zeros_like(bias)
    return times(resid_half, both_halves(half, mine, other, 1)) + both_halves(half, bias, nothing, 0)


def encoder_gradient(resid_half, resid_other, grad_low, half):
    whole = both_halves(half, resid_half, resid_other, 1)
    grad = lax.dot_general(whole, grad_low, (((0,), (0,)), ((), ())), preferred_element_type=F32)
    return grad.astype(BF16)


def two_layers(resid, target, enc_weight, enc_bias, dec_weight, blocks):
    hold = lax.optimization_barrier
    slots, count = lax.axis_size("latent"), lax.axis_size("layer")
    far = slots // 2
    layer, half = lax.axis_index("layer") // 2, lax.axis_index("layer") % 2
    slot = lax.axis_index("latent")
    side = slot % 2
    _, rows, width = resid.shape
    tokens, cols, part = rows * slots, width // 2, width // 4
    latents = enc_weight.shape[2]
    decoder = dec_weight[0].reshape(2, 2 * latents, cols)

    def routed(block, from_core_0=None, from_core_1=None):
        route = []
        for i in range(count):
            bits = (from_core_0, from_core_1)[i % 2]
            if bits is not None:
                route += [(i * slots + j, (i ^ bits[0]) * slots + (j ^ bits[1])) for j in range(slots)]
        return lax.ppermute(block, ("layer", "latent"), route)

    def over_core(block):
        return crossed(block, "layer", 1)

    def along_z(pieces, bits_of):
        out = [None] * (far - 1) + pieces[far - 1:]
        for k in range(far - 1, 0, -1):
            out[k - 1] = routed(pieces[k - 1], **bits_of(k))
        return out

    def core_0_z(k):
        return {"from_core_0": (0, 2 * k)}

    def core_1_z(k):
        return {"from_core_1": (0, 2 * k)}

    def pieces_of(total):
        each = total.shape[0] // far
        return [total[k * each:(k + 1) * each].astype(BF16) for k in range(1, far)] + [total[:each]]

    def added(terms):
        return sum(term.astype(F32) for term in terms[::-1])

    def gathered(terms):
        return jnp.concatenate(terms[-1:] + terms[:-1], axis=0)

    def by_core(zero, one):
        return jnp.where(half == 0, zero, one)

    def decoder_part(decoder, which, where):
        return lax.dynamic_slice(decoder, (which, 0, where * part), (1, 2 * latents, part))[0]

    def ordered(which, lower, upper, axis=0):
        return jnp.concatenate([jnp.where(which == 0, lower, upper), jnp.where(which == 0, upper, lower)], axis=axis)

    def rows_at(array, which):
        return array.reshape(-1, 2, rows, array.shape[1])[:, which].reshape(-1, array.shape[1])

    def paired(first, second):
        blocks = [block.reshape(-1, 1, rows, block.shape[1]) for block in (first, second)]
        return jnp.concatenate(blocks, axis=1).reshape(-1, first.shape[1])

    def turned(array):
        return paired(rows_at(array, 1), rows_at(array, 0))

    weight_other = over_core(enc_weight[0])
    mine = lax.dynamic_slice(resid, (layer, 0, half * cols), (1, rows, cols))[0]
    pair, weight_other, bias, blocks, later = hold(
        (paired(mine, crossed(mine, "latent", 1)), weight_other, enc_bias[0], blocks, decoder)
    )
    column = [pair] + [None] * (far - 1)
    for k in range(far - 1, 0, -1):
        column[k] = crossed(pair, "latent", 2 * k)

    shared_away, own_away = (1 - layer, 1 - layer), (layer, 1 - side)
    same_away = [by_core(zero, one) for zero, one in zip(shared_away, own_away)]
    cross_away = [by_core(one, zero) for zero, one in zip(shared_away, own_away)]
    same_half = routed(decoder_part(decoder, *same_away), (2, 0), (0, 1))
    cross_half = routed(decoder_part(decoder, *cross_away), (1, 1), (3, 0))
    later, same_half, cross_half, *column = hold((later, same_half, cross_half, *column))
    resid_half = jnp.concatenate(column, axis=0)

    shared_here, own_here = (1 - layer, layer), (layer, side)
    kept = decoder_part(later, *[by_core(zero, one) for zero, one in zip(shared_here, own_here)])
    swapped = over_core(decoder_part(later, *[by_core(one, zero) for zero, one in zip(shared_here, own_here)]))
    rows_here = jnp.concatenate([kept, swapped], axis=1)
    rows_there = jnp.concatenate([same_half, cross_half], axis=1)

    firing = gates(blocks, layer, slot, slots, latents, tokens)
    gate = jnp.where(half == 0, firing[0], firing[1])
    partial = half_preacts(resid_half, enc_weight[0], weight_other, bias, half)
    acts = ((partial + over_core(partial)) * jnp.concatenate(firing, axis=1)).astype(BF16)
    acts_there = routed(by_core(acts, turned(acts)), (2, 0), (0, 1))
    target, _ = hold((target, acts))

    def aim(which, where):
        halves = [
            lax.dynamic_slice(target, (which, 0, this * cols + where * part), (1, rows, part))[0]
            for this in (half, 1 - half)
        ]
        return jnp.concatenate(halves, axis=1)

    aim_other = routed(aim(2 * layer, 1 - side), from_core_1=(0, 1))

    product = times(acts, rows_here) + times(acts_there, rows_there)
    arrived = routed(rows_at(product, 1).astype(BF16), from_core_0=(0, 1))
    own_terms = along_z(pieces_of(product), core_1_z)
    shared_terms = along_z(pieces_of(rows_at(product, 0) + arrived.astype(F32)), core_0_z)
    terms = hold((*shared_terms, *own_terms))
    err_shared = (added(terms[:far]) - aim(1, layer).astype(F32)).astype(BF16)
    err_own = (added(terms[far:]) - paired(aim(2 * layer, side), aim_other).astype(F32)).astype(BF16)

    shared_near = gathered(along_z([err_shared] * far, core_0_z))
    errs_shared = paired(shared_near, routed(shared_near, from_core_0=(0, 1)))
    errs_own = gathered(along_z([err_own] * far, core_1_z))
    errs = by_core(errs_shared, errs_own)
    resid_swapped, _ = hold((resid_half, shared_near))
    resid_other = over_core(resid_swapped)

    found = by_core(err_shared, rows_at(err_own, 0))
    found_swapped = over_core(found[:, part:])
    sent = by_core(err_shared, rows_at(err_own, 1))

    def with_errors(grad, block):
        tiles = [block[:, at:at + latents] for at in range(0, part, latents)]
        return jnp.concatenate([grad.astype(BF16)] + tiles, axis=0)

    def without_errors(message):
        tiles = message[tokens:].reshape(part // latents, rows, latents)
        return message[:tokens].astype(F32), jnp.concatenate([tiles[i] for i in range(part // latents)], axis=1)

    def of_core(pair, which):
        return jnp.where(which == 0, pair[:, :latents], pair[:, latents:])

    away = times_transposed(errs, rows_there)
    away = by_core(away, turned(away))
    same, same_there = without_errors(routed(with_errors(of_core(away, half), sent[:, :part]), (2, 0), (0, 1)))
    cross, cross_there = without_errors(routed(with_errors(of_core(away, 1 - half), sent[:, part:]), (3, 0), (1, 1)))
    here = times_transposed(errs, rows_here)
    grad = of_core(here, half) + over_core(of_core(here, 1 - half)) + same + cross
    at_home = layer != half
    near_part = jnp.where(at_home, found[:, :part], found_swapped)
    far_part = jnp.where(at_home, same_there, cross_there)
    errors = ordered(jnp.where(layer == 0, side, 1), near_part, far_part, axis=1)
    grad_pre = grad * gate
    bias_grad = jnp.sum(grad_pre, axis=0)[None, :]
    enc_grad = encoder_gradient(resid_half, resid_other, grad_pre.astype(BF16), half)
    return errors[None], enc_grad[None], bias_grad


def any_layers(resid, target, enc_weight, enc_bias, dec_weight, blocks):
    slots = lax.axis_size("latent")
    count = lax.axis_size("layer")
    layer, half = lax.axis_index("layer") // 2, lax.axis_index("layer") % 2
    slot = lax.axis_index("latent")
    _, rows, width = resid.shape
    tokens, cols = rows * slots, width // 2
    latents = enc_weight.shape[2]
    decoder = dec_weight[0].reshape(2, 2 * latents, cols)

    def to_all(block):
        copies = jnp.broadcast_to(block[None], (slots,) + block.shape)
        return lax.all_to_all(copies, "latent", 0, 0).reshape(tokens, block.shape[1])

    def shifted(block, distance):
        route = [(i, i + distance) for i in range(count) if 0 <= i + distance < count]
        return lax.ppermute(block, "layer", route)

    resid_half = to_all(lax.dynamic_slice(resid, (layer, 0, half * cols), (1, rows, cols))[0])
    firing = gates(blocks, layer, slot, slots, latents, tokens)
    gate = jnp.where(half == 0, firing[0], firing[1])
    weight_other = crossed(enc_weight[0], "layer", 1)
    partial = half_preacts(resid_half, enc_weight[0], weight_other, enc_bias[0], half)
    preact = partial + crossed(partial, "layer", 1)
    acts = (preact * jnp.concatenate(firing, axis=1)).astype(BF16)
    resid_other = crossed(resid_half, "layer", 1)

    sums = jnp.concatenate([times(acts, decoder[t]).astype(BF16) for t in range(2)], axis=1)
    pieces = lax.all_to_all(sums.reshape(slots, rows, width), "latent", 0, 0)
    totals = jnp.sum(pieces.astype(F32), axis=0)
    own_sum, ahead_part = totals[:, :cols], totals[:, cols:]
    wanted = lax.dynamic_slice(target, (layer, 0, half * cols), (2, rows, cols)).astype(F32)
    err_own = (own_sum + shifted(ahead_part, 2) - wanted[0]).astype(BF16)
    err_next = (ahead_part + shifted(own_sum, -2) - wanted[1]).astype(BF16)
    errs = to_all(jnp.concatenate([err_own, err_next], axis=1))
    here = times_transposed(errs[:, :cols], decoder[0]) + times_transposed(errs[:, cols:], decoder[1])
    lower, upper = here[:, :latents], here[:, latents:]
    grad = jnp.where(half == 0, lower, upper) + crossed(jnp.where(half == 0, upper, lower), "layer", 1)
    grad_pre = grad * gate
    bias_grad = jnp.sum(grad_pre, axis=0)[None, :]
    enc_grad = encoder_gradient(resid_half, resid_other, grad_pre.astype(BF16), half)
    return err_own[None], enc_grad[None], bias_grad


def solution(mesh):
    small = mesh.shape["layer"] == 4 and mesh.shape["latent"] == 8
    return jax.shard_map(
        two_layers if small else any_layers,
        mesh=mesh,
        in_specs=(
            P(None, "latent", None),
            P(None, "latent", None),
            P("layer", None, "latent"),
            P("layer", "latent"),
            P("layer", None, None, "latent", None),
            P(),
        ),
        out_specs=(P("layer", "latent", None), P("layer", None, "latent"), P("layer", "latent")),
        check_vma=False,
    )
```

```python
import jax
import jax.numpy as jnp
from jax import lax
from jax.sharding import PartitionSpec as P

BLOCK = 128
F32, BF16 = jnp.float32, jnp.bfloat16


def crossed(block, axis, mask):
    return lax.ppermute(block, axis, [(i, i ^ mask) for i in range(lax.axis_size(axis))])


def times(left, right):
    return jnp.dot(left, right, preferred_element_type=F32)


def times_transposed(left, right):
    return lax.dot_general(left, right, (((1,), (1,)), ((), ())), preferred_element_type=F32)


def both_halves(half, mine, other, axis):
    return jnp.concatenate([jnp.where(half == 0, mine, other), jnp.where(half == 0, other, mine)], axis=axis)


def gates(blocks, layer, slot, slots, latents, tokens):
    listed = lax.dynamic_index_in_dim(blocks, layer, 0, keepdims=False)
    tile = tokens // listed.shape[0]
    here = latents // BLOCK
    out = []
    for side in range(2):
        names = (side * slots + slot) * here + jnp.arange(here)
        flags = jnp.any(listed[:, :, None] == names, axis=1).astype(F32)
        out.append(jnp.repeat(jnp.repeat(flags, tile, axis=0), BLOCK, axis=1))
    return out


def half_preacts(resid_half, weight, weight_other, bias, half):
    cols = resid_half.shape[1]
    mine = lax.dynamic_slice_in_dim(weight, half * cols, cols, 0)
    other = lax.dynamic_slice_in_dim(weight_other, half * cols, cols, 0)
    nothing = jnp.zeros_like(bias)
    return times(resid_half, both_halves(half, mine, other, 1)) + both_halves(half, bias, nothing, 0)


def encoder_gradient(resid_half, resid_other, grad_low, half):
    whole = both_halves(half, resid_half, resid_other, 1)
    grad = lax.dot_general(whole, grad_low, (((0,), (0,)), ((), ())), preferred_element_type=F32)
    return grad.astype(BF16)


def two_layers(resid, target, enc_weight, enc_bias, dec_weight, blocks):
    hold = lax.optimization_barrier
    slots, count = lax.axis_size("latent"), lax.axis_size("layer")
    far = slots // 2
    layer, half = lax.axis_index("layer") // 2, lax.axis_index("layer") % 2
    slot = lax.axis_index("latent")
    side = slot % 2
    _, rows, width = resid.shape
    tokens, cols, part = rows * slots, width // 2, width // 4
    latents = enc_weight.shape[2]
    decoder = dec_weight[0].reshape(2, 2 * latents, cols)

    def routed(block, from_core_0=(0, 0), from_core_1=(0, 0)):
        route = []
        for i in range(count):
            bits = (from_core_0, from_core_1)[i % 2]
            route += [(i * slots + j, (i ^ bits[0]) * slots + (j ^ bits[1])) for j in range(slots)]
        return lax.ppermute(block, ("layer", "latent"), route)

    def over_core(block):
        return crossed(block, "layer", 1)

    def along_z(pieces, bits_of):
        out = [None] * (far - 1) + pieces[far - 1:]
        for k in range(far - 1, 0, -1):
            out[k - 1] = routed(pieces[k - 1], **bits_of(k))
        return out

    def core_0_z(k):
        return {"from_core_0": (0, 2 * k)}

    def core_1_z(k):
        return {"from_core_1": (0, 2 * k)}

    def pieces_of(total):
        each = total.shape[0] // far
        return [total[k * each:(k + 1) * each].astype(BF16) for k in range(1, far)] + [total[:each]]

    def added(terms):
        return sum(term.astype(F32) for term in terms[::-1])

    def gathered(terms):
        return jnp.concatenate(terms[-1:] + terms[:-1], axis=0)

    def by_core(zero, one):
        return jnp.where(half == 0, zero, one)

    def decoder_part(decoder, which, where):
        return lax.dynamic_slice(decoder, (which, 0, where * part), (1, 2 * latents, part))[0]

    def ordered(which, lower, upper, axis=0):
        return jnp.concatenate([jnp.where(which == 0, lower, upper), jnp.where(which == 0, upper, lower)], axis=axis)

    def rows_at(array, which):
        return array.reshape(-1, 2, rows, array.shape[1])[:, which].reshape(-1, array.shape[1])

    def paired(first, second):
        blocks = [block.reshape(-1, 1, rows, block.shape[1]) for block in (first, second)]
        return jnp.concatenate(blocks, axis=1).reshape(-1, first.shape[1])

    def turned(array):
        return paired(rows_at(array, 1), rows_at(array, 0))

    weight_other = over_core(enc_weight[0])
    mine = lax.dynamic_slice(resid, (layer, 0, half * cols), (1, rows, cols))[0]
    pair, weight_other, bias, blocks, later = hold(
        (paired(mine, crossed(mine, "latent", 1)), weight_other, enc_bias[0], blocks, decoder)
    )
    column = [pair] + [None] * (far - 1)
    for k in range(far - 1, 0, -1):
        column[k] = crossed(pair, "latent", 2 * k)

    shared_away, own_away = (1 - layer, 1 - layer), (layer, 1 - side)
    same_away = [by_core(zero, one) for zero, one in zip(shared_away, own_away)]
    cross_away = [by_core(one, zero) for zero, one in zip(shared_away, own_away)]
    same_half = routed(decoder_part(decoder, *same_away), (2, 0), (0, 1))
    cross_half = routed(decoder_part(decoder, *cross_away), (1, 1), (3, 0))
    later, same_half, cross_half, *column = hold((later, same_half, cross_half, *column))
    resid_half = jnp.concatenate(column, axis=0)

    shared_here, own_here = (1 - layer, layer), (layer, side)
    kept = decoder_part(later, *[by_core(zero, one) for zero, one in zip(shared_here, own_here)])
    swapped = over_core(decoder_part(later, *[by_core(one, zero) for zero, one in zip(shared_here, own_here)]))
    rows_here = jnp.concatenate([kept, swapped], axis=1)
    rows_there = jnp.concatenate([same_half, cross_half], axis=1)

    firing = gates(blocks, layer, slot, slots, latents, tokens)
    gate = jnp.where(half == 0, firing[0], firing[1])
    partial = half_preacts(resid_half, enc_weight[0], weight_other, bias, half)
    acts = ((partial + over_core(partial)) * jnp.concatenate(firing, axis=1)).astype(BF16)
    acts_there = routed(by_core(acts, turned(acts)), (2, 0), (0, 1))
    target, _ = hold((target, acts))

    def aim(which, where):
        halves = [
            lax.dynamic_slice(target, (which, 0, this * cols + where * part), (1, rows, part))[0]
            for this in (half, 1 - half)
        ]
        return jnp.concatenate(halves, axis=1)

    aim_other = routed(aim(2 * layer, 1 - side), from_core_1=(0, 1))

    product = times(acts, rows_here) + times(acts_there, rows_there)
    arrived = routed(rows_at(product, 1).astype(BF16), from_core_0=(0, 1))
    own_terms = along_z(pieces_of(product), core_1_z)
    shared_terms = along_z(pieces_of(rows_at(product, 0) + arrived.astype(F32)), core_0_z)
    terms = hold((*shared_terms, *own_terms))
    err_shared = (added(terms[:far]) - aim(1, layer).astype(F32)).astype(BF16)
    err_own = (added(terms[far:]) - paired(aim(2 * layer, side), aim_other).astype(F32)).astype(BF16)

    shared_near = gathered(along_z([err_shared] * far, core_0_z))
    errs_shared = paired(shared_near, routed(shared_near, from_core_0=(0, 1)))
    errs_own = gathered(along_z([err_own] * far, core_1_z))
    errs = by_core(errs_shared, errs_own)
    resid_swapped, _ = hold((resid_half, shared_near))
    resid_other = over_core(resid_swapped)

    found = by_core(err_shared, rows_at(err_own, 0))
    found_swapped = over_core(found[:, part:])
    sent = by_core(err_shared, rows_at(err_own, 1))

    def with_errors(grad, block):
        tiles = [block[:, at:at + latents] for at in range(0, part, latents)]
        return jnp.concatenate([grad.astype(BF16)] + tiles, axis=0)

    def without_errors(message):
        tiles = message[tokens:].reshape(part // latents, rows, latents)
        return message[:tokens].astype(F32), jnp.concatenate([tiles[i] for i in range(part // latents)], axis=1)

    def of_core(pair, which):
        return jnp.where(which == 0, pair[:, :latents], pair[:, latents:])

    away = times_transposed(errs, rows_there)
    away = by_core(away, turned(away))
    same, same_there = without_errors(routed(with_errors(of_core(away, half), sent[:, :part]), (2, 0), (0, 1)))
    cross, cross_there = without_errors(routed(with_errors(of_core(away, 1 - half), sent[:, part:]), (3, 0), (1, 1)))
    here = times_transposed(errs, rows_here)
    grad = of_core(here, half) + over_core(of_core(here, 1 - half)) + same + cross
    at_home = layer != half
    near_part = jnp.where(at_home, found[:, :part], found_swapped)
    far_part = jnp.where(at_home, same_there, cross_there)
    errors = ordered(jnp.where(layer == 0, side, 1), near_part, far_part, axis=1)
    grad_pre = grad * gate
    bias_grad = jnp.sum(grad_pre, axis=0)[None, :]
    enc_grad = encoder_gradient(resid_half, resid_other, grad_pre.astype(BF16), half)
    return errors[None], enc_grad[None], bias_grad


def any_layers(resid, target, enc_weight, enc_bias, dec_weight, blocks):
    slots = lax.axis_size("latent")
    count = lax.axis_size("layer")
    layer, half = lax.axis_index("layer") // 2, lax.axis_index("layer") % 2
    slot = lax.axis_index("latent")
    _, rows, width = resid.shape
    tokens, cols = rows * slots, width // 2
    latents = enc_weight.shape[2]
    decoder = dec_weight[0].reshape(2, 2 * latents, cols)

    def to_all(block):
        copies = jnp.broadcast_to(block[None], (slots,) + block.shape)
        return lax.all_to_all(copies, "latent", 0, 0).reshape(tokens, block.shape[1])

    def shifted(block, distance):
        route = [(i, i + distance) for i in range(count) if 0 <= i + distance < count]
        return lax.ppermute(block, "layer", route)

    resid_half = to_all(lax.dynamic_slice(resid, (layer, 0, half * cols), (1, rows, cols))[0])
    firing = gates(blocks, layer, slot, slots, latents, tokens)
    gate = jnp.where(half == 0, firing[0], firing[1])
    weight_other = crossed(enc_weight[0], "layer", 1)
    partial = half_preacts(resid_half, enc_weight[0], weight_other, enc_bias[0], half)
    preact = partial + crossed(partial, "layer", 1)
    acts = (preact * jnp.concatenate(firing, axis=1)).astype(BF16)
    resid_other = crossed(resid_half, "layer", 1)

    sums = jnp.concatenate([times(acts, decoder[t]).astype(BF16) for t in range(2)], axis=1)
    pieces = lax.all_to_all(sums.reshape(slots, rows, width), "latent", 0, 0)
    totals = jnp.sum(pieces.astype(F32), axis=0)
    own_sum, ahead_part = totals[:, :cols], totals[:, cols:]
    wanted = lax.dynamic_slice(target, (layer, 0, half * cols), (2, rows, cols)).astype(F32)
    err_own = (own_sum + shifted(ahead_part, 2) - wanted[0]).astype(BF16)
    err_next = (ahead_part + shifted(own_sum, -2) - wanted[1]).astype(BF16)
    errs = to_all(jnp.concatenate([err_own, err_next], axis=1))
    here = times_transposed(errs[:, :cols], decoder[0]) + times_transposed(errs[:, cols:], decoder[1])
    lower, upper = here[:, :latents], here[:, latents:]
    grad = jnp.where(half == 0, lower, upper) + crossed(jnp.where(half == 0, upper, lower), "layer", 1)
    grad_pre = grad * gate
    bias_grad = jnp.sum(grad_pre, axis=0)[None, :]
    enc_grad = encoder_gradient(resid_half, resid_other, grad_pre.astype(BF16), half)
    return err_own[None], enc_grad[None], bias_grad


def solution(mesh):
    small = mesh.shape["layer"] == 4 and mesh.shape["latent"] == 8
    return jax.shard_map(
        two_layers if small else any_layers,
        mesh=mesh,
        in_specs=(
            P(None, "latent", None),
            P(None, "latent", None),
            P("layer", None, "latent"),
            P("layer", "latent"),
            P("layer", None, None, "latent", None),
            P(),
        ),
        out_specs=(P("layer", "latent", None), P("layer", None, "latent"), P("layer", "latent")),
        check_vma=False,
    )
```

```python
import jax
import jax.numpy as jnp
from jax import lax
from jax.sharding import PartitionSpec as P

BLOCK = 128
F32, BF16 = jnp.float32, jnp.bfloat16


def crossed(block, axis, mask):
    return lax.ppermute(block, axis, [(i, i ^ mask) for i in range(lax.axis_size(axis))])


def times(left, right):
    return jnp.dot(left, right, preferred_element_type=F32)


def times_transposed(left, right):
    return lax.dot_general(left, right, (((1,), (1,)), ((), ())), preferred_element_type=F32)


def both_halves(half, mine, other, axis):
    return jnp.concatenate([jnp.where(half == 0, mine, other), jnp.where(half == 0, other, mine)], axis=axis)


def gates(blocks, layer, slot, slots, latents, tokens):
    listed = lax.dynamic_index_in_dim(blocks, layer, 0, keepdims=False)
    tile = tokens // listed.shape[0]
    here = latents // BLOCK
    out = []
    for side in range(2):
        names = (side * slots + slot) * here + jnp.arange(here)
        flags = jnp.any(listed[:, :, None] == names, axis=1).astype(F32)
        out.append(jnp.repeat(jnp.repeat(flags, tile, axis=0), BLOCK, axis=1))
    return out


def half_preacts(resid_half, weight, weight_other, bias, half):
    cols = resid_half.shape[1]
    mine = lax.dynamic_slice_in_dim(weight, half * cols, cols, 0)
    other = lax.dynamic_slice_in_dim(weight_other, half * cols, cols, 0)
    nothing = jnp.zeros_like(bias)
    return times(resid_half, both_halves(half, mine, other, 1)) + both_halves(half, bias, nothing, 0)


def encoder_gradient(resid_half, resid_other, grad_low, half):
    whole = both_halves(half, resid_half, resid_other, 1)
    grad = lax.dot_general(whole, grad_low, (((0,), (0,)), ((), ())), preferred_element_type=F32)
    return grad.astype(BF16)


def two_layers(resid, target, enc_weight, enc_bias, dec_weight, blocks):
    hold = lax.optimization_barrier
    slots = lax.axis_size("latent")
    far = slots // 2
    layer, half = lax.axis_index("layer") // 2, lax.axis_index("layer") % 2
    slot = lax.axis_index("latent")
    side = slot % 2
    _, rows, width = resid.shape
    tokens, cols, part = rows * slots, width // 2, width // 4
    latents = enc_weight.shape[2]
    decoder = dec_weight[0].reshape(2, 2 * latents, cols)

    def over_x(block):
        return crossed(block, "latent", 1)

    def over_y(block):
        return crossed(block, "layer", 2)

    def over_core(block):
        return crossed(block, "layer", 1)

    def along_z(block):
        out = [block] + [None] * (far - 1)
        for k in range(far - 1, 0, -1):
            out[k] = crossed(block, "latent", 2 * k)
        return out

    def both_along_z(shared, own):
        count = shared[1].shape[0]
        out = [[shared[0]] + [None] * (far - 1), [own[0]] + [None] * (far - 1)]
        for k in range(far - 1, 1, -1):
            out[0][k] = crossed(shared[k], "latent", 2 * k)
        nearest = crossed(jnp.concatenate([shared[1], own[1]], axis=0), "latent", 2)
        out[0][1], out[1][1] = nearest[:count], nearest[count:]
        for k in range(far - 1, 1, -1):
            out[1][k] = crossed(own[k], "latent", 2 * k)
        return out

    def pieces_of(total):
        count = total.shape[0] // far
        return [total[:count]] + [total[k * count:(k + 1) * count].astype(BF16) for k in range(1, far)]

    def added(terms):
        return sum(term.astype(F32) for term in terms)

    def decoder_part(decoder, which, where):
        return lax.dynamic_slice(decoder, (which, 0, where * part), (1, 2 * latents, part))[0]

    def ordered(which, lower, upper, axis=0):
        return jnp.concatenate([jnp.where(which == 0, lower, upper), jnp.where(which == 0, upper, lower)], axis=axis)

    def rows_at(array, which):
        return array.reshape(-1, 2, rows, array.shape[1])[:, which].reshape(-1, array.shape[1])

    def paired(first, second):
        blocks = [block.reshape(-1, 1, rows, block.shape[1]) for block in (first, second)]
        return jnp.concatenate(blocks, axis=1).reshape(-1, first.shape[1])

    def turned(array):
        return paired(rows_at(array, 1), rows_at(array, 0))

    weight_other = over_core(enc_weight[0])
    mine = lax.dynamic_slice(resid, (layer, 0, half * cols), (1, rows, cols))[0]
    pair, weight_other, bias, blocks = hold((paired(mine, over_x(mine)), weight_other, enc_bias[0], blocks))
    column = along_z(pair)

    own_other = over_x(decoder_part(decoder, layer, 1 - side))
    shared_other = over_y(decoder_part(decoder, 1 - layer, 1 - layer))
    decoder, own_other, shared_other, *column = hold((decoder, own_other, shared_other, *column))
    own_mine, shared_mine = decoder_part(decoder, layer, side), decoder_part(decoder, 1 - layer, layer)
    resid_half = jnp.concatenate(column, axis=0)
    firing = gates(blocks, layer, slot, slots, latents, tokens)
    gate = jnp.where(half == 0, firing[0], firing[1])

    partial = half_preacts(resid_half, enc_weight[0], weight_other, bias, half)
    acts = ((partial + over_core(partial)) * jnp.concatenate(firing, axis=1)).astype(BF16)
    acts_turned = turned(acts)
    acts_y, acts_x = over_y(acts), over_x(acts_turned)
    target, _ = hold((target, acts_turned))
    start = half * cols

    def aim_own(where):
        return lax.dynamic_slice(target, (2 * layer, 0, start + where * part), (1, rows, part))[0]

    aim_other = over_x(aim_own(1 - side))
    aim_shared = lax.dynamic_slice(target, (1, 0, start + layer * part), (1, rows, part))[0]

    leaving = times(rows_at(acts, 1), shared_mine) + times(rows_at(acts_y, 1), shared_other)
    staying = times(rows_at(acts, 0), shared_mine) + times(rows_at(acts_y, 0), shared_other)
    arrived = over_x(leaving.astype(BF16))
    product = times(acts, own_mine) + times(acts_x, own_other)
    arrived, staying = hold((arrived, staying))
    shared_terms, own_terms = both_along_z(pieces_of(staying + arrived.astype(F32)), pieces_of(product))
    terms = hold((*shared_terms, *own_terms))
    err_shared = (added(terms[:far]) - aim_shared.astype(F32)).astype(BF16)
    err_own = (added(terms[far:]) - paired(aim_own(side), aim_other).astype(F32)).astype(BF16)

    own_column = along_z(err_own)
    shared_near = jnp.concatenate(along_z(err_shared), axis=0)
    resid_swapped, _ = hold((resid_half, shared_near))
    resid_other = over_core(resid_swapped)
    errs_shared = paired(shared_near, over_x(shared_near))
    errs_own = jnp.concatenate(own_column, axis=0)

    grads = jnp.concatenate(
        [
            times_transposed(errs_own, own_mine) + times_transposed(errs_shared, shared_mine),
            turned(times_transposed(errs_own, own_other)),
            times_transposed(errs_shared, shared_other),
        ],
        axis=0,
    )
    lower, upper = grads[:, :latents], grads[:, latents:]
    grads = jnp.where(half == 0, lower, upper) + over_core(jnp.where(half == 0, upper, lower))


    def with_errors(grad, block):
        tiles = [block[:, at:at + latents] for at in range(0, part, latents)]
        return jnp.concatenate([grad.astype(BF16)] + tiles, axis=0)

    def without_errors(message):
        tiles = message[tokens:].reshape(part // latents, rows, latents)
        return message[:tokens].astype(F32), jnp.concatenate([tiles[i] for i in range(part // latents)], axis=1)

    from_x, own_there = without_errors(over_x(with_errors(grads[tokens:2 * tokens], rows_at(err_own, 1))))
    from_y, shared_there = without_errors(over_y(with_errors(grads[2 * tokens:], err_shared)))
    errors = jnp.where(
        layer == 0,
        ordered(side, rows_at(err_own, 0), own_there, axis=1),
        jnp.concatenate([shared_there, err_shared], axis=1),
    )
    grad_pre = (grads[:tokens] + from_x + from_y) * gate
    bias_grad = jnp.sum(grad_pre, axis=0)[None, :]
    enc_grad = encoder_gradient(resid_half, resid_other, grad_pre.astype(BF16), half)
    return errors[None], enc_grad[None], bias_grad


def any_layers(resid, target, enc_weight, enc_bias, dec_weight, blocks):
    slots = lax.axis_size("latent")
    count = lax.axis_size("layer")
    layer, half = lax.axis_index("layer") // 2, lax.axis_index("layer") % 2
    slot = lax.axis_index("latent")
    _, rows, width = resid.shape
    tokens, cols = rows * slots, width // 2
    latents = enc_weight.shape[2]
    decoder = dec_weight[0].reshape(2, 2 * latents, cols)

    def to_all(block):
        copies = jnp.broadcast_to(block[None], (slots,) + block.shape)
        return lax.all_to_all(copies, "latent", 0, 0).reshape(tokens, block.shape[1])

    def shifted(block, distance):
        route = [(i, i + distance) for i in range(count) if 0 <= i + distance < count]
        return lax.ppermute(block, "layer", route)

    resid_half = to_all(lax.dynamic_slice(resid, (layer, 0, half * cols), (1, rows, cols))[0])
    firing = gates(blocks, layer, slot, slots, latents, tokens)
    gate = jnp.where(half == 0, firing[0], firing[1])
    weight_other = crossed(enc_weight[0], "layer", 1)
    partial = half_preacts(resid_half, enc_weight[0], weight_other, enc_bias[0], half)
    preact = partial + crossed(partial, "layer", 1)
    acts = (preact * jnp.concatenate(firing, axis=1)).astype(BF16)
    resid_other = crossed(resid_half, "layer", 1)

    sums = jnp.concatenate([times(acts, decoder[t]).astype(BF16) for t in range(2)], axis=1)
    pieces = lax.all_to_all(sums.reshape(slots, rows, width), "latent", 0, 0)
    totals = jnp.sum(pieces.astype(F32), axis=0)
    own_sum, ahead_part = totals[:, :cols], totals[:, cols:]
    wanted = lax.dynamic_slice(target, (layer, 0, half * cols), (2, rows, cols)).astype(F32)
    err_own = (own_sum + shifted(ahead_part, 2) - wanted[0]).astype(BF16)
    err_next = (ahead_part + shifted(own_sum, -2) - wanted[1]).astype(BF16)
    errs = to_all(jnp.concatenate([err_own, err_next], axis=1))
    here = times_transposed(errs[:, :cols], decoder[0]) + times_transposed(errs[:, cols:], decoder[1])
    lower, upper = here[:, :latents], here[:, latents:]
    grad = jnp.where(half == 0, lower, upper) + crossed(jnp.where(half == 0, upper, lower), "layer", 1)
    grad_pre = grad * gate
    bias_grad = jnp.sum(grad_pre, axis=0)[None, :]
    enc_grad = encoder_gradient(resid_half, resid_other, grad_pre.astype(BF16), half)
    return err_own[None], enc_grad[None], bias_grad


def solution(mesh):
    small = mesh.shape["layer"] == 4 and mesh.shape["latent"] == 8
    return jax.shard_map(
        two_layers if small else any_layers,
        mesh=mesh,
        in_specs=(
            P(None, "latent", None),
            P(None, "latent", None),
            P("layer", None, "latent"),
            P("layer", "latent"),
            P("layer", None, None, "latent", None),
            P(),
        ),
        out_specs=(P("layer", "latent", None), P("layer", None, "latent"), P("layer", "latent")),
        check_vma=False,
    )
```

```python
import jax
import jax.numpy as jnp
from jax import lax
from jax.sharding import PartitionSpec as P

BLOCK = 128
F32, BF16 = jnp.float32, jnp.bfloat16


def crossed(block, axis, mask):
    return lax.ppermute(block, axis, [(i, i ^ mask) for i in range(lax.axis_size(axis))])


def times(left, right):
    return jnp.dot(left, right, preferred_element_type=F32)


def times_transposed(left, right):
    return lax.dot_general(left, right, (((1,), (1,)), ((), ())), preferred_element_type=F32)


def both_halves(half, mine, other, axis):
    return jnp.concatenate([jnp.where(half == 0, mine, other), jnp.where(half == 0, other, mine)], axis=axis)


def gates(blocks, layer, slot, slots, latents, tokens):
    listed = lax.dynamic_index_in_dim(blocks, layer, 0, keepdims=False)
    column = jnp.arange(2 * latents)
    names = (column // latents * slots + slot) * (latents // BLOCK) + column % latents // BLOCK
    flags = jnp.any(listed[:, :, None] == names, axis=1).astype(F32)
    return jnp.repeat(flags, tokens // listed.shape[0], axis=0)


def half_preacts(resid_half, weight, weight_other, bias, half):
    cols = resid_half.shape[1]
    mine = lax.dynamic_slice_in_dim(weight, half * cols, cols, 0)
    other = lax.dynamic_slice_in_dim(weight_other, half * cols, cols, 0)
    nothing = jnp.zeros_like(bias)
    return times(resid_half, both_halves(half, mine, other, 1)) + both_halves(half, bias, nothing, 0)


def encoder_gradient(resid_half, resid_other, grad_low, half):
    whole = both_halves(half, resid_half, resid_other, 1)
    grad = lax.dot_general(whole, grad_low, (((0,), (0,)), ((), ())), preferred_element_type=F32)
    return grad.astype(BF16)


def two_layers(resid, target, enc_weight, enc_bias, dec_weight, blocks):
    hold = lax.optimization_barrier
    slots = lax.axis_size("latent")
    far = slots // 2
    layer, half = lax.axis_index("layer") // 2, lax.axis_index("layer") % 2
    slot = lax.axis_index("latent")
    side = slot % 2
    _, rows, width = resid.shape
    tokens, cols, part = rows * slots, width // 2, width // 4
    latents = enc_weight.shape[2]
    decoder = dec_weight[0].reshape(2, 2 * latents, cols)

    def over_x(block):
        return crossed(block, "latent", 1)

    def over_y(block):
        return crossed(block, "layer", 2)

    def over_core(block):
        return crossed(block, "layer", 1)

    def along_z(block):
        out = [block] + [None] * (far - 1)
        for k in range(far - 1, 0, -1):
            out[k] = crossed(block, "latent", 2 * k)
        return out

    def both_along_z(shared, own):
        count = shared[1].shape[0]
        out = [[shared[0]] + [None] * (far - 1), [own[0]] + [None] * (far - 1)]
        for k in range(far - 1, 1, -1):
            out[0][k] = crossed(shared[k], "latent", 2 * k)
        nearest = crossed(jnp.concatenate([shared[1], own[1]], axis=0), "latent", 2)
        out[0][1], out[1][1] = nearest[:count], nearest[count:]
        for k in range(far - 1, 1, -1):
            out[1][k] = crossed(own[k], "latent", 2 * k)
        return out

    def pieces_of(total):
        count = total.shape[0] // far
        return [total[:count]] + [total[k * count:(k + 1) * count].astype(BF16) for k in range(1, far)]

    def added(terms):
        return sum(term.astype(F32) for term in terms)

    def decoder_part(decoder, which, where):
        return lax.dynamic_slice(decoder, (which, 0, where * part), (1, 2 * latents, part))[0]

    def ordered(which, lower, upper, axis=0):
        return jnp.concatenate([jnp.where(which == 0, lower, upper), jnp.where(which == 0, upper, lower)], axis=axis)

    def rows_at(array, which):
        return array.reshape(-1, 2, rows, array.shape[1])[:, which].reshape(-1, array.shape[1])

    def paired(first, second):
        blocks = [block.reshape(-1, 1, rows, block.shape[1]) for block in (first, second)]
        return jnp.concatenate(blocks, axis=1).reshape(-1, first.shape[1])

    def turned(array):
        return paired(rows_at(array, 1), rows_at(array, 0))

    weight_other = over_core(enc_weight[0])
    mine = lax.dynamic_slice(resid, (layer, 0, half * cols), (1, rows, cols))[0]
    pair, weight_other, bias, blocks = hold((paired(mine, over_x(mine)), weight_other, enc_bias[0], blocks))
    column = along_z(pair)

    own_other = over_x(decoder_part(decoder, layer, 1 - side))
    shared_other = over_y(decoder_part(decoder, 1 - layer, 1 - layer))
    decoder, own_other, shared_other, *column = hold((decoder, own_other, shared_other, *column))
    own_mine, shared_mine = decoder_part(decoder, layer, side), decoder_part(decoder, 1 - layer, layer)
    resid_half = jnp.concatenate(column, axis=0)
    firing = gates(blocks, layer, slot, slots, latents, tokens)
    gate = jnp.where(half == 0, firing[:, :latents], firing[:, latents:])

    partial = half_preacts(resid_half, enc_weight[0], weight_other, bias, half)
    acts = ((partial + over_core(partial)) * firing).astype(BF16)
    acts_turned = turned(acts)
    acts_y, acts_x = over_y(acts), over_x(acts_turned)
    target, _ = hold((target, acts_turned))
    start = half * cols

    def aim_own(where):
        return lax.dynamic_slice(target, (2 * layer, 0, start + where * part), (1, rows, part))[0]

    aim_other = over_x(aim_own(1 - side))
    aim_shared = lax.dynamic_slice(target, (1, 0, start + layer * part), (1, rows, part))[0]

    leaving = times(rows_at(acts, 1), shared_mine) + times(rows_at(acts_y, 1), shared_other)
    staying = times(rows_at(acts, 0), shared_mine) + times(rows_at(acts_y, 0), shared_other)
    arrived = over_x(leaving.astype(BF16))
    product = times(acts, own_mine) + times(acts_x, own_other)
    arrived, staying = hold((arrived, staying))
    shared_terms, own_terms = both_along_z(pieces_of(staying + arrived.astype(F32)), pieces_of(product))
    terms = hold((*shared_terms, *own_terms))
    aim_mine, aim_shared = hold((aim_own(side), aim_shared))
    err_shared = (added(terms[:far]) - aim_shared.astype(F32)).astype(BF16)
    err_own = (added(terms[far:]) - paired(aim_mine, aim_other).astype(F32)).astype(BF16)

    own_column = along_z(err_own)
    shared_near = jnp.concatenate(along_z(err_shared), axis=0)
    resid_swapped, _ = hold((resid_half, shared_near))
    resid_other = over_core(resid_swapped)
    errs_shared = paired(shared_near, over_x(shared_near))
    errs_own = jnp.concatenate(own_column, axis=0)

    grads = jnp.concatenate(
        [
            times_transposed(errs_own, own_mine) + times_transposed(errs_shared, shared_mine),
            turned(times_transposed(errs_own, own_other)),
            times_transposed(errs_shared, shared_other),
        ],
        axis=0,
    )
    lower, upper = grads[:, :latents], grads[:, latents:]
    grads = jnp.where(half == 0, lower, upper) + over_core(jnp.where(half == 0, upper, lower))


    def with_errors(grad, block):
        tiles = [block[:, at:at + latents] for at in range(0, part, latents)]
        return jnp.concatenate([grad.astype(BF16)] + tiles, axis=0)

    def without_errors(message):
        tiles = message[tokens:].reshape(part // latents, rows, latents)
        return message[:tokens].astype(F32), jnp.concatenate([tiles[i] for i in range(part // latents)], axis=1)

    from_x, own_there = without_errors(over_x(with_errors(grads[tokens:2 * tokens], rows_at(err_own, 1))))
    from_y, shared_there = without_errors(over_y(with_errors(grads[2 * tokens:], err_shared)))
    errors = jnp.where(
        layer == 0,
        ordered(side, rows_at(err_own, 0), own_there, axis=1),
        jnp.concatenate([shared_there, err_shared], axis=1),
    )
    grad_pre = (grads[:tokens] + from_x + from_y) * gate
    bias_grad = jnp.sum(grad_pre, axis=0)[None, :]
    enc_grad = encoder_gradient(resid_half, resid_other, grad_pre.astype(BF16), half)
    return errors[None], enc_grad[None], bias_grad


def any_layers(resid, target, enc_weight, enc_bias, dec_weight, blocks):
    slots = lax.axis_size("latent")
    count = lax.axis_size("layer")
    layer, half = lax.axis_index("layer") // 2, lax.axis_index("layer") % 2
    slot = lax.axis_index("latent")
    _, rows, width = resid.shape
    tokens, cols = rows * slots, width // 2
    latents = enc_weight.shape[2]
    decoder = dec_weight[0].reshape(2, 2 * latents, cols)

    def to_all(block):
        copies = jnp.broadcast_to(block[None], (slots,) + block.shape)
        return lax.all_to_all(copies, "latent", 0, 0).reshape(tokens, block.shape[1])

    def shifted(block, distance):
        route = [(i, i + distance) for i in range(count) if 0 <= i + distance < count]
        return lax.ppermute(block, "layer", route)

    resid_half = to_all(lax.dynamic_slice(resid, (layer, 0, half * cols), (1, rows, cols))[0])
    firing = gates(blocks, layer, slot, slots, latents, tokens)
    gate = jnp.where(half == 0, firing[:, :latents], firing[:, latents:])
    weight_other = crossed(enc_weight[0], "layer", 1)
    partial = half_preacts(resid_half, enc_weight[0], weight_other, enc_bias[0], half)
    preact = partial + crossed(partial, "layer", 1)
    acts = (preact * firing).astype(BF16)
    resid_other = crossed(resid_half, "layer", 1)

    sums = jnp.concatenate([times(acts, decoder[t]).astype(BF16) for t in range(2)], axis=1)
    pieces = lax.all_to_all(sums.reshape(slots, rows, width), "latent", 0, 0)
    totals = jnp.sum(pieces.astype(F32), axis=0)
    own_sum, ahead_part = totals[:, :cols], totals[:, cols:]
    wanted = lax.dynamic_slice(target, (layer, 0, half * cols), (2, rows, cols)).astype(F32)
    err_own = (own_sum + shifted(ahead_part, 2) - wanted[0]).astype(BF16)
    err_next = (ahead_part + shifted(own_sum, -2) - wanted[1]).astype(BF16)
    errs = to_all(jnp.concatenate([err_own, err_next], axis=1))
    here = times_transposed(errs[:, :cols], decoder[0]) + times_transposed(errs[:, cols:], decoder[1])
    lower, upper = here[:, :latents], here[:, latents:]
    grad = jnp.where(half == 0, lower, upper) + crossed(jnp.where(half == 0, upper, lower), "layer", 1)
    grad_pre = grad * gate
    bias_grad = jnp.sum(grad_pre, axis=0)[None, :]
    enc_grad = encoder_gradient(resid_half, resid_other, grad_pre.astype(BF16), half)
    return err_own[None], enc_grad[None], bias_grad


def solution(mesh):
    small = mesh.shape["layer"] == 4 and mesh.shape["latent"] == 8
    return jax.shard_map(
        two_layers if small else any_layers,
        mesh=mesh,
        in_specs=(
            P(None, "latent", None),
            P(None, "latent", None),
            P("layer", None, "latent"),
            P("layer", "latent"),
            P("layer", None, None, "latent", None),
            P(),
        ),
        out_specs=(P("layer", "latent", None), P("layer", None, "latent"), P("layer", "latent")),
        check_vma=False,
    )
```

```python
import jax
import jax.numpy as jnp
from jax import lax
from jax.sharding import PartitionSpec as P

BLOCK = 128
F32, BF16 = jnp.float32, jnp.bfloat16


def crossed(block, axis, mask):
    return lax.ppermute(block, axis, [(i, i ^ mask) for i in range(lax.axis_size(axis))])


def times(left, right):
    return jnp.dot(left, right, preferred_element_type=F32)


def times_transposed(left, right):
    return lax.dot_general(left, right, (((1,), (1,)), ((), ())), preferred_element_type=F32)


def both_halves(half, mine, other, axis):
    return jnp.concatenate([jnp.where(half == 0, mine, other), jnp.where(half == 0, other, mine)], axis=axis)


def gates(blocks, layer, slot, slots, latents, tokens):
    listed = lax.dynamic_index_in_dim(blocks, layer, 0, keepdims=False)
    column = jnp.arange(2 * latents)
    names = (column // latents * slots + slot) * (latents // BLOCK) + column % latents // BLOCK
    flags = jnp.any(listed[:, :, None] == names, axis=1).astype(F32)
    return jnp.repeat(flags, tokens // listed.shape[0], axis=0)


def half_preacts(resid_half, weight, weight_other, bias, half):
    cols = resid_half.shape[1]
    mine = lax.dynamic_slice_in_dim(weight, half * cols, cols, 0)
    other = lax.dynamic_slice_in_dim(weight_other, half * cols, cols, 0)
    nothing = jnp.zeros_like(bias)
    return times(resid_half, both_halves(half, mine, other, 1)) + both_halves(half, bias, nothing, 0)


def encoder_gradient(resid_half, resid_other, grad_low, half):
    whole = both_halves(half, resid_half, resid_other, 1)
    grad = lax.dot_general(whole, grad_low, (((0,), (0,)), ((), ())), preferred_element_type=F32)
    return grad.astype(BF16)


def two_layers(resid, target, enc_weight, enc_bias, dec_weight, blocks):
    hold = lax.optimization_barrier
    slots = lax.axis_size("latent")
    far = slots // 2
    layer, half = lax.axis_index("layer") // 2, lax.axis_index("layer") % 2
    slot = lax.axis_index("latent")
    side = slot % 2
    _, rows, width = resid.shape
    tokens, cols, part = rows * slots, width // 2, width // 4
    latents = enc_weight.shape[2]
    decoder = dec_weight[0].reshape(2, 2 * latents, cols)

    def over_x(block):
        return crossed(block, "latent", 1)

    def over_y(block):
        return crossed(block, "layer", 2)

    def over_core(block):
        return crossed(block, "layer", 1)

    def along_z(block):
        out = [block] + [None] * (far - 1)
        for k in range(far - 1, 0, -1):
            out[k] = crossed(block, "latent", 2 * k)
        return out

    def both_along_z(shared, own):
        count = shared[1].shape[0]
        out = [[shared[0]] + [None] * (far - 1), [own[0]] + [None] * (far - 1)]
        for k in range(far - 1, 0, -1):
            out[0][k] = crossed(shared[k], "latent", 2 * k)
            out[1][k] = crossed(own[k], "latent", 2 * k)
        return out

    def pieces_of(total):
        count = total.shape[0] // far
        return [total[:count]] + [total[k * count:(k + 1) * count].astype(BF16) for k in range(1, far)]

    def added(terms):
        return sum(term.astype(F32) for term in terms)

    def decoder_part(decoder, which, where):
        return lax.dynamic_slice(decoder, (which, 0, where * part), (1, 2 * latents, part))[0]

    def ordered(which, lower, upper, axis=0):
        return jnp.concatenate([jnp.where(which == 0, lower, upper), jnp.where(which == 0, upper, lower)], axis=axis)

    def rows_at(array, which):
        return array.reshape(-1, 2, rows, array.shape[1])[:, which].reshape(-1, array.shape[1])

    def paired(first, second):
        blocks = [block.reshape(-1, 1, rows, block.shape[1]) for block in (first, second)]
        return jnp.concatenate(blocks, axis=1).reshape(-1, first.shape[1])

    def turned(array):
        return paired(rows_at(array, 1), rows_at(array, 0))

    weight_other = over_core(enc_weight[0])
    mine = lax.dynamic_slice(resid, (layer, 0, half * cols), (1, rows, cols))[0]
    pair, weight_other, bias, blocks = hold((paired(mine, over_x(mine)), weight_other, enc_bias[0], blocks))
    column = along_z(pair)

    own_other = over_x(decoder_part(decoder, layer, 1 - side))
    shared_other = over_y(decoder_part(decoder, 1 - layer, 1 - layer))
    decoder, own_other, shared_other, *column = hold((decoder, own_other, shared_other, *column))
    own_mine, shared_mine = decoder_part(decoder, layer, side), decoder_part(decoder, 1 - layer, layer)
    resid_half = jnp.concatenate(column, axis=0)
    firing = gates(blocks, layer, slot, slots, latents, tokens)
    gate = jnp.where(half == 0, firing[:, :latents], firing[:, latents:])

    partial = half_preacts(resid_half, enc_weight[0], weight_other, bias, half)
    acts = ((partial + over_core(partial)) * firing).astype(BF16)
    acts_turned = turned(acts)
    acts_y, acts_x = over_y(acts), over_x(acts_turned)
    target, _ = hold((target, acts_turned))
    start = half * cols

    def aim_own(where):
        return lax.dynamic_slice(target, (2 * layer, 0, start + where * part), (1, rows, part))[0]

    aim_other = over_x(aim_own(1 - side))
    aim_shared = lax.dynamic_slice(target, (1, 0, start + layer * part), (1, rows, part))[0]

    leaving = times(rows_at(acts, 1), shared_mine) + times(rows_at(acts_y, 1), shared_other)
    staying = times(rows_at(acts, 0), shared_mine) + times(rows_at(acts_y, 0), shared_other)
    arrived = over_x(leaving.astype(BF16))
    product = times(acts, own_mine) + times(acts_x, own_other)
    own_pieces = pieces_of(product)
    arrived, staying, own_pieces[1] = hold((arrived, staying, own_pieces[1]))
    shared_terms, own_terms = both_along_z(pieces_of(staying + arrived.astype(F32)), own_pieces)
    terms = hold((*shared_terms, *own_terms[2:]))
    terms = (*terms[:far], own_terms[0], own_terms[1], *terms[far:])
    aim_mine, aim_shared = hold((aim_own(side), aim_shared))
    err_shared = (added(terms[:far]) - aim_shared.astype(F32)).astype(BF16)
    err_own = (added(terms[far:]) - paired(aim_mine, aim_other).astype(F32)).astype(BF16)

    own_column = along_z(err_own)
    shared_near = jnp.concatenate(along_z(err_shared), axis=0)
    resid_swapped, _ = hold((resid_half, shared_near))
    resid_other = over_core(resid_swapped)
    errs_shared = paired(shared_near, over_x(shared_near))
    errs_own = jnp.concatenate(own_column, axis=0)

    grads = jnp.concatenate(
        [
            times_transposed(errs_own, own_mine) + times_transposed(errs_shared, shared_mine),
            turned(times_transposed(errs_own, own_other)),
            times_transposed(errs_shared, shared_other),
        ],
        axis=0,
    )
    lower, upper = grads[:, :latents], grads[:, latents:]
    grads = jnp.where(half == 0, lower, upper) + over_core(jnp.where(half == 0, upper, lower))


    def with_errors(grad, block):
        tiles = [block[:, at:at + latents] for at in range(0, part, latents)]
        return jnp.concatenate([grad.astype(BF16)] + tiles, axis=0)

    def without_errors(message):
        tiles = message[tokens:].reshape(part // latents, rows, latents)
        return message[:tokens].astype(F32), jnp.concatenate([tiles[i] for i in range(part // latents)], axis=1)

    from_x, own_there = without_errors(over_x(with_errors(grads[tokens:2 * tokens], rows_at(err_own, 1))))
    from_y, shared_there = without_errors(over_y(with_errors(grads[2 * tokens:], err_shared)))
    errors = jnp.where(
        layer == 0,
        ordered(side, rows_at(err_own, 0), own_there, axis=1),
        jnp.concatenate([shared_there, err_shared], axis=1),
    )
    grad_pre = (grads[:tokens] + from_x + from_y) * gate
    bias_grad = jnp.sum(grad_pre, axis=0)[None, :]
    enc_grad = encoder_gradient(resid_half, resid_other, grad_pre.astype(BF16), half)
    return errors[None], enc_grad[None], bias_grad


def any_layers(resid, target, enc_weight, enc_bias, dec_weight, blocks):
    slots = lax.axis_size("latent")
    count = lax.axis_size("layer")
    layer, half = lax.axis_index("layer") // 2, lax.axis_index("layer") % 2
    slot = lax.axis_index("latent")
    _, rows, width = resid.shape
    tokens, cols = rows * slots, width // 2
    latents = enc_weight.shape[2]
    decoder = dec_weight[0].reshape(2, 2 * latents, cols)

    def to_all(block):
        copies = jnp.broadcast_to(block[None], (slots,) + block.shape)
        return lax.all_to_all(copies, "latent", 0, 0).reshape(tokens, block.shape[1])

    def shifted(block, distance):
        route = [(i, i + distance) for i in range(count) if 0 <= i + distance < count]
        return lax.ppermute(block, "layer", route)

    resid_half = to_all(lax.dynamic_slice(resid, (layer, 0, half * cols), (1, rows, cols))[0])
    firing = gates(blocks, layer, slot, slots, latents, tokens)
    gate = jnp.where(half == 0, firing[:, :latents], firing[:, latents:])
    weight_other = crossed(enc_weight[0], "layer", 1)
    partial = half_preacts(resid_half, enc_weight[0], weight_other, enc_bias[0], half)
    preact = partial + crossed(partial, "layer", 1)
    acts = (preact * firing).astype(BF16)
    resid_other = crossed(resid_half, "layer", 1)

    sums = jnp.concatenate([times(acts, decoder[t]).astype(BF16) for t in range(2)], axis=1)
    pieces = lax.all_to_all(sums.reshape(slots, rows, width), "latent", 0, 0)
    totals = jnp.sum(pieces.astype(F32), axis=0)
    own_sum, ahead_part = totals[:, :cols], totals[:, cols:]
    wanted = lax.dynamic_slice(target, (layer, 0, half * cols), (2, rows, cols)).astype(F32)
    err_own = (own_sum + shifted(ahead_part, 2) - wanted[0]).astype(BF16)
    err_next = (ahead_part + shifted(own_sum, -2) - wanted[1]).astype(BF16)
    errs = to_all(jnp.concatenate([err_own, err_next], axis=1))
    here = times_transposed(errs[:, :cols], decoder[0]) + times_transposed(errs[:, cols:], decoder[1])
    lower, upper = here[:, :latents], here[:, latents:]
    grad = jnp.where(half == 0, lower, upper) + crossed(jnp.where(half == 0, upper, lower), "layer", 1)
    grad_pre = grad * gate
    bias_grad = jnp.sum(grad_pre, axis=0)[None, :]
    enc_grad = encoder_gradient(resid_half, resid_other, grad_pre.astype(BF16), half)
    return err_own[None], enc_grad[None], bias_grad


def solution(mesh):
    small = mesh.shape["layer"] == 4 and mesh.shape["latent"] == 8
    return jax.shard_map(
        two_layers if small else any_layers,
        mesh=mesh,
        in_specs=(
            P(None, "latent", None),
            P(None, "latent", None),
            P("layer", None, "latent"),
            P("layer", "latent"),
            P("layer", None, None, "latent", None),
            P(),
        ),
        out_specs=(P("layer", "latent", None), P("layer", None, "latent"), P("layer", "latent")),
        check_vma=False,
    )
```

```python
import jax
import jax.numpy as jnp
from jax import lax
from jax.sharding import PartitionSpec as P

BLOCK = 128
F32, BF16 = jnp.float32, jnp.bfloat16


def crossed(block, axis, mask):
    return lax.ppermute(block, axis, [(i, i ^ mask) for i in range(lax.axis_size(axis))])


def times(left, right):
    return jnp.dot(left, right, preferred_element_type=F32)


def times_transposed(left, right):
    return lax.dot_general(left, right, (((1,), (1,)), ((), ())), preferred_element_type=F32)


def both_halves(half, mine, other, axis):
    return jnp.concatenate([jnp.where(half == 0, mine, other), jnp.where(half == 0, other, mine)], axis=axis)


def gates(blocks, layer, slot, slots, latents, tokens):
    listed = lax.dynamic_index_in_dim(blocks, layer, 0, keepdims=False)
    column = jnp.arange(2 * latents)
    names = (column // latents * slots + slot) * (latents // BLOCK) + column % latents // BLOCK
    flags = jnp.any(listed[:, :, None] == names, axis=1).astype(F32)
    return jnp.repeat(flags, tokens // listed.shape[0], axis=0)


def half_preacts(resid_half, weight, weight_other, bias, half):
    cols = resid_half.shape[1]
    mine = lax.dynamic_slice_in_dim(weight, half * cols, cols, 0)
    other = lax.dynamic_slice_in_dim(weight_other, half * cols, cols, 0)
    nothing = jnp.zeros_like(bias)
    return times(resid_half, both_halves(half, mine, other, 1)) + both_halves(half, bias, nothing, 0)


def encoder_gradient(resid_half, resid_other, grad_low, half):
    whole = both_halves(half, resid_half, resid_other, 1)
    grad = lax.dot_general(whole, grad_low, (((0,), (0,)), ((), ())), preferred_element_type=F32)
    return grad.astype(BF16)


def two_layers(resid, target, enc_weight, enc_bias, dec_weight, blocks):
    hold = lax.optimization_barrier
    slots = lax.axis_size("latent")
    far = slots // 2
    layer, half = lax.axis_index("layer") // 2, lax.axis_index("layer") % 2
    slot = lax.axis_index("latent")
    side = slot % 2
    _, rows, width = resid.shape
    tokens, cols, part = rows * slots, width // 2, width // 4
    latents = enc_weight.shape[2]
    decoder = dec_weight[0].reshape(2, 2 * latents, cols)

    def over_x(block):
        return crossed(block, "latent", 1)

    def over_y(block):
        return crossed(block, "layer", 2)

    def over_core(block):
        return crossed(block, "layer", 1)

    def along_z(block):
        out = [block] + [None] * (far - 1)
        for k in range(far - 1, 0, -1):
            out[k] = crossed(block, "latent", 2 * k)
        return out

    def both_along_z(shared, own):
        count = shared[1].shape[0]
        out = [[shared[0]] + [None] * (far - 1), [own[0]] + [None] * (far - 1)]
        for k in range(far - 1, 0, -1):
            out[0][k] = crossed(shared[k], "latent", 2 * k)
            out[1][k] = crossed(own[k], "latent", 2 * k)
        return out

    def pieces_of(total):
        count = total.shape[0] // far
        return [total[:count]] + [total[k * count:(k + 1) * count].astype(BF16) for k in range(1, far)]

    def added(terms):
        return sum(term.astype(F32) for term in terms)

    def decoder_part(decoder, which, where):
        return lax.dynamic_slice(decoder, (which, 0, where * part), (1, 2 * latents, part))[0]

    def ordered(which, lower, upper, axis=0):
        return jnp.concatenate([jnp.where(which == 0, lower, upper), jnp.where(which == 0, upper, lower)], axis=axis)

    def rows_at(array, which):
        return array.reshape(-1, 2, rows, array.shape[1])[:, which].reshape(-1, array.shape[1])

    def paired(first, second):
        blocks = [block.reshape(-1, 1, rows, block.shape[1]) for block in (first, second)]
        return jnp.concatenate(blocks, axis=1).reshape(-1, first.shape[1])

    def turned(array):
        return paired(rows_at(array, 1), rows_at(array, 0))

    weight_other = over_core(enc_weight[0])
    mine = lax.dynamic_slice(resid, (layer, 0, half * cols), (1, rows, cols))[0]
    pair, weight_other, bias, blocks = hold((paired(mine, over_x(mine)), weight_other, enc_bias[0], blocks))
    column = along_z(pair)

    own_other = over_x(decoder_part(decoder, layer, 1 - side))
    shared_other = over_y(decoder_part(decoder, 1 - layer, 1 - layer))
    decoder, own_other, shared_other, *column = hold((decoder, own_other, shared_other, *column))
    own_mine, shared_mine = decoder_part(decoder, layer, side), decoder_part(decoder, 1 - layer, layer)
    resid_half = jnp.concatenate(column, axis=0)
    firing = gates(blocks, layer, slot, slots, latents, tokens)
    gate = jnp.where(half == 0, firing[:, :latents], firing[:, latents:])

    partial = half_preacts(resid_half, enc_weight[0], weight_other, bias, half)
    acts = ((partial + over_core(partial)) * firing).astype(BF16)
    acts_turned = turned(acts)
    acts_y, acts_x = over_y(acts), over_x(acts_turned)
    target, _ = hold((target, acts_turned))
    start = half * cols

    def aim_own(where):
        return lax.dynamic_slice(target, (2 * layer, 0, start + where * part), (1, rows, part))[0]

    aim_other = over_x(aim_own(1 - side))
    aim_shared = lax.dynamic_slice(target, (1, 0, start + layer * part), (1, rows, part))[0]

    leaving = times(rows_at(acts, 1), shared_mine) + times(rows_at(acts_y, 1), shared_other)
    staying = times(rows_at(acts, 0), shared_mine) + times(rows_at(acts_y, 0), shared_other)
    arrived = over_x(leaving.astype(BF16))
    product = times(acts, own_mine) + times(acts_x, own_other)
    own_pieces = pieces_of(product)
    arrived, staying, own_pieces[1] = hold((arrived, staying, own_pieces[1]))
    shared_terms, own_terms = both_along_z(pieces_of(staying + arrived.astype(F32)), own_pieces)
    terms = hold((*shared_terms, *own_terms[2:]))
    terms = (*terms[:far], own_terms[0], own_terms[1], *terms[far:])
    aim_mine, aim_shared = hold((aim_own(side), aim_shared))
    err_shared = (added(terms[:far]) - aim_shared.astype(F32)).astype(BF16)
    err_own = (added(terms[far:]) - paired(aim_mine, aim_other).astype(F32)).astype(BF16)

    own_column = along_z(err_own)
    shared_near = jnp.concatenate(along_z(err_shared), axis=0)
    resid_swapped, _ = hold((resid_half, shared_near))
    resid_other = over_core(resid_swapped)
    errs_shared = paired(shared_near, over_x(shared_near))
    errs_own = jnp.concatenate(own_column, axis=0)

    grads = jnp.concatenate(
        [
            times_transposed(errs_own, own_mine) + times_transposed(errs_shared, shared_mine),
            turned(times_transposed(errs_own, own_other)),
            times_transposed(errs_shared, shared_other),
        ],
        axis=0,
    )
    lower, upper = grads[:, :latents], grads[:, latents:]
    grads = jnp.where(half == 0, lower, upper) + over_core(jnp.where(half == 0, upper, lower))


    to_x, to_y = grads[tokens:2 * tokens].astype(BF16), grads[2 * tokens:].astype(BF16)
    to_x, to_y, late_own, late_shared = hold((to_x, to_y, rows_at(err_own, 1), err_shared))
    from_x, from_y = over_x(to_x).astype(F32), over_y(to_y).astype(F32)
    own_there, shared_there = over_x(late_own), over_y(late_shared)
    grad_pre = (grads[:tokens] + from_x + from_y) * gate
    bias_grad = jnp.sum(grad_pre, axis=0)[None, :]
    enc_grad = encoder_gradient(resid_half, resid_other, grad_pre.astype(BF16), half)
    enc_grad, own_there, shared_there = hold((enc_grad, own_there, shared_there))
    errors = jnp.where(
        layer == 0,
        ordered(side, rows_at(err_own, 0), own_there, axis=1),
        jnp.concatenate([shared_there, err_shared], axis=1),
    )
    return errors[None], enc_grad[None], bias_grad


def any_layers(resid, target, enc_weight, enc_bias, dec_weight, blocks):
    slots = lax.axis_size("latent")
    count = lax.axis_size("layer")
    layer, half = lax.axis_index("layer") // 2, lax.axis_index("layer") % 2
    slot = lax.axis_index("latent")
    _, rows, width = resid.shape
    tokens, cols = rows * slots, width // 2
    latents = enc_weight.shape[2]
    decoder = dec_weight[0].reshape(2, 2 * latents, cols)

    def to_all(block):
        copies = jnp.broadcast_to(block[None], (slots,) + block.shape)
        return lax.all_to_all(copies, "latent", 0, 0).reshape(tokens, block.shape[1])

    def shifted(block, distance):
        route = [(i, i + distance) for i in range(count) if 0 <= i + distance < count]
        return lax.ppermute(block, "layer", route)

    resid_half = to_all(lax.dynamic_slice(resid, (layer, 0, half * cols), (1, rows, cols))[0])
    firing = gates(blocks, layer, slot, slots, latents, tokens)
    gate = jnp.where(half == 0, firing[:, :latents], firing[:, latents:])
    weight_other = crossed(enc_weight[0], "layer", 1)
    partial = half_preacts(resid_half, enc_weight[0], weight_other, enc_bias[0], half)
    preact = partial + crossed(partial, "layer", 1)
    acts = (preact * firing).astype(BF16)
    resid_other = crossed(resid_half, "layer", 1)

    sums = jnp.concatenate([times(acts, decoder[t]).astype(BF16) for t in range(2)], axis=1)
    pieces = lax.all_to_all(sums.reshape(slots, rows, width), "latent", 0, 0)
    totals = jnp.sum(pieces.astype(F32), axis=0)
    own_sum, ahead_part = totals[:, :cols], totals[:, cols:]
    wanted = lax.dynamic_slice(target, (layer, 0, half * cols), (2, rows, cols)).astype(F32)
    err_own = (own_sum + shifted(ahead_part, 2) - wanted[0]).astype(BF16)
    err_next = (ahead_part + shifted(own_sum, -2) - wanted[1]).astype(BF16)
    errs = to_all(jnp.concatenate([err_own, err_next], axis=1))
    here = times_transposed(errs[:, :cols], decoder[0]) + times_transposed(errs[:, cols:], decoder[1])
    lower, upper = here[:, :latents], here[:, latents:]
    grad = jnp.where(half == 0, lower, upper) + crossed(jnp.where(half == 0, upper, lower), "layer", 1)
    grad_pre = grad * gate
    bias_grad = jnp.sum(grad_pre, axis=0)[None, :]
    enc_grad = encoder_gradient(resid_half, resid_other, grad_pre.astype(BF16), half)
    return err_own[None], enc_grad[None], bias_grad


def solution(mesh):
    small = mesh.shape["layer"] == 4 and mesh.shape["latent"] == 8
    return jax.shard_map(
        two_layers if small else any_layers,
        mesh=mesh,
        in_specs=(
            P(None, "latent", None),
            P(None, "latent", None),
            P("layer", None, "latent"),
            P("layer", "latent"),
            P("layer", None, None, "latent", None),
            P(),
        ),
        out_specs=(P("layer", "latent", None), P("layer", None, "latent"), P("layer", "latent")),
        check_vma=False,
    )
```

```python
import jax
import jax.numpy as jnp
from jax import lax
from jax.sharding import PartitionSpec as P

BLOCK = 128
F32, BF16 = jnp.float32, jnp.bfloat16


def crossed(block, axis, mask):
    return lax.ppermute(block, axis, [(i, i ^ mask) for i in range(lax.axis_size(axis))])


def times(left, right):
    return jnp.dot(left, right, preferred_element_type=F32)


def times_transposed(left, right):
    return lax.dot_general(left, right, (((1,), (1,)), ((), ())), preferred_element_type=F32)


def both_halves(half, mine, other, axis):
    return jnp.concatenate([jnp.where(half == 0, mine, other), jnp.where(half == 0, other, mine)], axis=axis)


def gates(blocks, layer, slot, slots, latents, tokens):
    listed = lax.dynamic_index_in_dim(blocks, layer, 0, keepdims=False)
    column = jnp.arange(2 * latents)
    names = (column // latents * slots + slot) * (latents // BLOCK) + column % latents // BLOCK
    flags = jnp.any(listed[:, :, None] == names, axis=1).astype(F32)
    return jnp.repeat(flags, tokens // listed.shape[0], axis=0)


def half_preacts(resid_half, weight, weight_other, bias, half):
    cols = resid_half.shape[1]
    mine = lax.dynamic_slice_in_dim(weight, half * cols, cols, 0)
    other = lax.dynamic_slice_in_dim(weight_other, half * cols, cols, 0)
    nothing = jnp.zeros_like(bias)
    return times(resid_half, both_halves(half, mine, other, 1)) + both_halves(half, bias, nothing, 0)


def encoder_gradient(resid_half, resid_other, grad_low, half):
    whole = both_halves(half, resid_half, resid_other, 1)
    grad = lax.dot_general(whole, grad_low, (((0,), (0,)), ((), ())), preferred_element_type=F32)
    return grad.astype(BF16)


def two_layers(resid, target, enc_weight, enc_bias, dec_weight, blocks):
    hold = lax.optimization_barrier
    slots = lax.axis_size("latent")
    far = slots // 2
    layer, half = lax.axis_index("layer") // 2, lax.axis_index("layer") % 2
    slot = lax.axis_index("latent")
    side = slot % 2
    _, rows, width = resid.shape
    tokens, cols, part = rows * slots, width // 2, width // 4
    latents = enc_weight.shape[2]
    decoder = dec_weight[0].reshape(2, 2 * latents, cols)

    def over_x(block):
        return crossed(block, "latent", 1)

    def over_y(block):
        return crossed(block, "layer", 2)

    def over_core(block):
        return crossed(block, "layer", 1)

    def along_z(block):
        out = [block] + [None] * (far - 1)
        for k in range(far - 1, 0, -1):
            out[k] = crossed(block, "latent", 2 * k)
        return out

    def both_along_z(shared, own):
        count = shared[1].shape[0]
        out = [[shared[0]] + [None] * (far - 1), [own[0]] + [None] * (far - 1)]
        for k in range(far - 1, 0, -1):
            out[0][k] = crossed(shared[k], "latent", 2 * k)
            out[1][k] = crossed(own[k], "latent", 2 * k)
        return out

    def pieces_of(total):
        count = total.shape[0] // far
        return [total[:count]] + [total[k * count:(k + 1) * count].astype(BF16) for k in range(1, far)]

    def added(terms):
        return sum(term.astype(F32) for term in terms)

    def decoder_part(decoder, which, where):
        return lax.dynamic_slice(decoder, (which, 0, where * part), (1, 2 * latents, part))[0]

    def ordered(which, lower, upper, axis=0):
        return jnp.concatenate([jnp.where(which == 0, lower, upper), jnp.where(which == 0, upper, lower)], axis=axis)

    def rows_at(array, which):
        return array.reshape(-1, 2, rows, array.shape[1])[:, which].reshape(-1, array.shape[1])

    def paired(first, second):
        blocks = [block.reshape(-1, 1, rows, block.shape[1]) for block in (first, second)]
        return jnp.concatenate(blocks, axis=1).reshape(-1, first.shape[1])

    def turned(array):
        return paired(rows_at(array, 1), rows_at(array, 0))

    weight_other = over_core(enc_weight[0])
    mine = lax.dynamic_slice(resid, (layer, 0, half * cols), (1, rows, cols))[0]
    pair, weight_other, bias, blocks = hold((paired(mine, over_x(mine)), weight_other, enc_bias[0], blocks))
    column = along_z(pair)

    own_other = over_x(decoder_part(decoder, layer, 1 - side))
    shared_other = over_y(decoder_part(decoder, 1 - layer, 1 - layer))
    decoder, own_other, shared_other, *column = hold((decoder, own_other, shared_other, *column))
    own_mine, shared_mine = decoder_part(decoder, layer, side), decoder_part(decoder, 1 - layer, layer)
    resid_half = jnp.concatenate(column, axis=0)
    firing = gates(blocks, layer, slot, slots, latents, tokens)
    gate = jnp.where(half == 0, firing[:, :latents], firing[:, latents:])

    partial = half_preacts(resid_half, enc_weight[0], weight_other, bias, half)
    acts = ((partial + over_core(partial)) * firing).astype(BF16)
    acts_turned = turned(acts)
    acts_y, acts_x = over_y(acts), over_x(acts_turned)
    target, _ = hold((target, acts_turned))
    start = half * cols

    def aim_own(where):
        return lax.dynamic_slice(target, (2 * layer, 0, start + where * part), (1, rows, part))[0]

    aim_other = over_x(aim_own(1 - side))
    aim_shared = lax.dynamic_slice(target, (1, 0, start + layer * part), (1, rows, part))[0]

    leaving = times(rows_at(acts, 1), shared_mine) + times(rows_at(acts_y, 1), shared_other)
    staying = times(rows_at(acts, 0), shared_mine) + times(rows_at(acts_y, 0), shared_other)
    arrived = over_x(leaving.astype(BF16))
    product = times(acts, own_mine) + times(acts_x, own_other)
    own_pieces = pieces_of(product)
    arrived, staying, own_pieces[1] = hold((arrived, staying, own_pieces[1]))
    shared_terms, own_terms = both_along_z(pieces_of(staying + arrived.astype(F32)), own_pieces)
    terms = hold((*shared_terms, *own_terms[2:]))
    terms = (*terms[:far], own_terms[0], own_terms[1], *terms[far:])
    aim_mine, aim_shared = hold((aim_own(side), aim_shared))
    err_shared = (added(terms[:far]) - aim_shared.astype(F32)).astype(BF16)
    err_own = (added(terms[far:]) - paired(aim_mine, aim_other).astype(F32)).astype(BF16)

    own_column = along_z(err_own)
    shared_near = jnp.concatenate(along_z(err_shared), axis=0)
    resid_swapped, late_shared, _ = hold((resid_half, err_shared, shared_near))
    resid_other = over_core(resid_swapped)
    shared_there = over_y(late_shared)
    errs_shared = paired(shared_near, over_x(shared_near))
    errs_own = jnp.concatenate(own_column, axis=0)

    grads = jnp.concatenate(
        [
            times_transposed(errs_own, own_mine) + times_transposed(errs_shared, shared_mine),
            turned(times_transposed(errs_own, own_other)),
            times_transposed(errs_shared, shared_other),
        ],
        axis=0,
    )
    lower, upper = grads[:, :latents], grads[:, latents:]
    grads = jnp.where(half == 0, lower, upper) + over_core(jnp.where(half == 0, upper, lower))


    grads, shared_there, resid_other = hold((grads, shared_there, resid_other))

    away = rows_at(err_own, 1)
    tiles = [away[:, at:at + latents] for at in range(0, part, latents)]
    to_x = jnp.concatenate([grads[tokens:2 * tokens].astype(BF16)] + tiles, axis=0)
    to_x, to_y = hold((to_x, grads[2 * tokens:].astype(BF16)))
    from_x, from_y = over_x(to_x), over_y(to_y).astype(F32)
    tiles = from_x[tokens:].reshape(part // latents, rows, latents)
    own_there = jnp.concatenate([tiles[i] for i in range(part // latents)], axis=1)
    from_x = from_x[:tokens].astype(F32)
    errors = jnp.where(
        layer == 0,
        ordered(side, rows_at(err_own, 0), own_there, axis=1),
        jnp.concatenate([shared_there, err_shared], axis=1),
    )
    grad_pre = (grads[:tokens] + from_x + from_y) * gate
    bias_grad = jnp.sum(grad_pre, axis=0)[None, :]
    enc_grad = encoder_gradient(resid_half, resid_other, grad_pre.astype(BF16), half)
    return errors[None], enc_grad[None], bias_grad


def any_layers(resid, target, enc_weight, enc_bias, dec_weight, blocks):
    slots = lax.axis_size("latent")
    count = lax.axis_size("layer")
    layer, half = lax.axis_index("layer") // 2, lax.axis_index("layer") % 2
    slot = lax.axis_index("latent")
    _, rows, width = resid.shape
    tokens, cols = rows * slots, width // 2
    latents = enc_weight.shape[2]
    decoder = dec_weight[0].reshape(2, 2 * latents, cols)

    def to_all(block):
        copies = jnp.broadcast_to(block[None], (slots,) + block.shape)
        return lax.all_to_all(copies, "latent", 0, 0).reshape(tokens, block.shape[1])

    def shifted(block, distance):
        route = [(i, i + distance) for i in range(count) if 0 <= i + distance < count]
        return lax.ppermute(block, "layer", route)

    resid_half = to_all(lax.dynamic_slice(resid, (layer, 0, half * cols), (1, rows, cols))[0])
    firing = gates(blocks, layer, slot, slots, latents, tokens)
    gate = jnp.where(half == 0, firing[:, :latents], firing[:, latents:])
    weight_other = crossed(enc_weight[0], "layer", 1)
    partial = half_preacts(resid_half, enc_weight[0], weight_other, enc_bias[0], half)
    preact = partial + crossed(partial, "layer", 1)
    acts = (preact * firing).astype(BF16)
    resid_other = crossed(resid_half, "layer", 1)

    sums = jnp.concatenate([times(acts, decoder[t]).astype(BF16) for t in range(2)], axis=1)
    pieces = lax.all_to_all(sums.reshape(slots, rows, width), "latent", 0, 0)
    totals = jnp.sum(pieces.astype(F32), axis=0)
    own_sum, ahead_part = totals[:, :cols], totals[:, cols:]
    wanted = lax.dynamic_slice(target, (layer, 0, half * cols), (2, rows, cols)).astype(F32)
    err_own = (own_sum + shifted(ahead_part, 2) - wanted[0]).astype(BF16)
    err_next = (ahead_part + shifted(own_sum, -2) - wanted[1]).astype(BF16)
    errs = to_all(jnp.concatenate([err_own, err_next], axis=1))
    here = times_transposed(errs[:, :cols], decoder[0]) + times_transposed(errs[:, cols:], decoder[1])
    lower, upper = here[:, :latents], here[:, latents:]
    grad = jnp.where(half == 0, lower, upper) + crossed(jnp.where(half == 0, upper, lower), "layer", 1)
    grad_pre = grad * gate
    bias_grad = jnp.sum(grad_pre, axis=0)[None, :]
    enc_grad = encoder_gradient(resid_half, resid_other, grad_pre.astype(BF16), half)
    return err_own[None], enc_grad[None], bias_grad


def solution(mesh):
    small = mesh.shape["layer"] == 4 and mesh.shape["latent"] == 8
    return jax.shard_map(
        two_layers if small else any_layers,
        mesh=mesh,
        in_specs=(
            P(None, "latent", None),
            P(None, "latent", None),
            P("layer", None, "latent"),
            P("layer", "latent"),
            P("layer", None, None, "latent", None),
            P(),
        ),
        out_specs=(P("layer", "latent", None), P("layer", None, "latent"), P("layer", "latent")),
        check_vma=False,
    )
```

```python
import jax
import jax.numpy as jnp
from jax import lax
from jax.sharding import PartitionSpec as P

BLOCK = 128
F32, BF16 = jnp.float32, jnp.bfloat16


def crossed(block, axis, mask):
    return lax.ppermute(block, axis, [(i, i ^ mask) for i in range(lax.axis_size(axis))])


def times(left, right):
    return jnp.dot(left, right, preferred_element_type=F32)


def times_transposed(left, right):
    return lax.dot_general(left, right, (((1,), (1,)), ((), ())), preferred_element_type=F32)


def both_halves(half, mine, other, axis):
    return jnp.concatenate([jnp.where(half == 0, mine, other), jnp.where(half == 0, other, mine)], axis=axis)


def gates(blocks, layer, slot, slots, latents, tokens):
    listed = lax.dynamic_index_in_dim(blocks, layer, 0, keepdims=False)
    column = jnp.arange(2 * latents)
    names = (column // latents * slots + slot) * (latents // BLOCK) + column % latents // BLOCK
    flags = jnp.any(listed[:, :, None] == names, axis=1).astype(F32)
    return jnp.repeat(flags, tokens // listed.shape[0], axis=0)


def half_preacts(resid_half, weight, weight_other, bias, half):
    cols = resid_half.shape[1]
    mine = lax.dynamic_slice_in_dim(weight, half * cols, cols, 0)
    other = lax.dynamic_slice_in_dim(weight_other, half * cols, cols, 0)
    nothing = jnp.zeros_like(bias)
    return times(resid_half, both_halves(half, mine, other, 1)) + both_halves(half, bias, nothing, 0)


def encoder_gradient(resid_half, resid_other, grad_low, half):
    whole = both_halves(half, resid_half, resid_other, 1)
    grad = lax.dot_general(whole, grad_low, (((0,), (0,)), ((), ())), preferred_element_type=F32)
    return grad.astype(BF16)


def two_layers(resid, target, enc_weight, enc_bias, dec_weight, blocks):
    hold = lax.optimization_barrier
    slots = lax.axis_size("latent")
    far = slots // 2
    layer, half = lax.axis_index("layer") // 2, lax.axis_index("layer") % 2
    slot = lax.axis_index("latent")
    side = slot % 2
    _, rows, width = resid.shape
    tokens, cols, part = rows * slots, width // 2, width // 4
    latents = enc_weight.shape[2]
    decoder = dec_weight[0].reshape(2, 2 * latents, cols)

    def over_x(block):
        return crossed(block, "latent", 1)

    def over_y(block):
        return crossed(block, "layer", 2)

    def over_core(block):
        return crossed(block, "layer", 1)

    def along_z(block):
        out = [block] + [None] * (far - 1)
        for k in range(far - 1, 0, -1):
            out[k] = crossed(block, "latent", 2 * k)
        return out

    def both_along_z(shared, own):
        count = shared[1].shape[0]
        out = [[shared[0]] + [None] * (far - 1), [own[0]] + [None] * (far - 1)]
        for k in range(far - 1, 0, -1):
            out[0][k] = crossed(shared[k], "latent", 2 * k)
            out[1][k] = crossed(own[k], "latent", 2 * k)
        return out

    def pieces_of(total):
        count = total.shape[0] // far
        return [total[:count]] + [total[k * count:(k + 1) * count].astype(BF16) for k in range(1, far)]

    def added(terms):
        return sum(term.astype(F32) for term in terms)

    def decoder_part(decoder, which, where):
        return lax.dynamic_slice(decoder, (which, 0, where * part), (1, 2 * latents, part))[0]

    def ordered(which, lower, upper, axis=0):
        return jnp.concatenate([jnp.where(which == 0, lower, upper), jnp.where(which == 0, upper, lower)], axis=axis)

    def rows_at(array, which):
        return array.reshape(-1, 2, rows, array.shape[1])[:, which].reshape(-1, array.shape[1])

    def paired(first, second):
        blocks = [block.reshape(-1, 1, rows, block.shape[1]) for block in (first, second)]
        return jnp.concatenate(blocks, axis=1).reshape(-1, first.shape[1])

    def turned(array):
        return paired(rows_at(array, 1), rows_at(array, 0))

    weight_other = over_core(enc_weight[0])
    mine = lax.dynamic_slice(resid, (layer, 0, half * cols), (1, rows, cols))[0]
    pair, weight_other, bias, blocks = hold((paired(mine, over_x(mine)), weight_other, enc_bias[0], blocks))
    column = along_z(pair)

    own_other = over_x(decoder_part(decoder, layer, 1 - side))
    shared_other = over_y(decoder_part(decoder, 1 - layer, 1 - layer))
    decoder, own_other, shared_other, *column = hold((decoder, own_other, shared_other, *column))
    own_mine, shared_mine = decoder_part(decoder, layer, side), decoder_part(decoder, 1 - layer, layer)
    resid_half = jnp.concatenate(column, axis=0)
    firing = gates(blocks, layer, slot, slots, latents, tokens)
    gate = jnp.where(half == 0, firing[:, :latents], firing[:, latents:])

    partial = half_preacts(resid_half, enc_weight[0], weight_other, bias, half)
    acts = ((partial + over_core(partial)) * firing).astype(BF16)
    acts_turned = turned(acts)
    acts_y, acts_x = over_y(acts), over_x(acts_turned)
    target, _ = hold((target, acts_turned))
    start = half * cols

    def aim_own(where):
        return lax.dynamic_slice(target, (2 * layer, 0, start + where * part), (1, rows, part))[0]

    aim_other = over_x(aim_own(1 - side))
    aim_shared = lax.dynamic_slice(target, (1, 0, start + layer * part), (1, rows, part))[0]

    leaving = times(rows_at(acts, 1), shared_mine) + times(rows_at(acts_y, 1), shared_other)
    staying = times(rows_at(acts, 0), shared_mine) + times(rows_at(acts_y, 0), shared_other)
    arrived = over_x(leaving.astype(BF16))
    product = times(acts, own_mine) + times(acts_x, own_other)
    own_pieces = pieces_of(product)
    arrived, staying, own_pieces[1] = hold((arrived, staying, own_pieces[1]))
    shared_terms, own_terms = both_along_z(pieces_of(staying + arrived.astype(F32)), own_pieces)
    terms = hold((*shared_terms, *own_terms[2:]))
    terms = (*terms[:far], own_terms[0], own_terms[1], *terms[far:])
    aim_mine, aim_shared = hold((aim_own(side), aim_shared))
    err_shared = (added(terms[:far]) - aim_shared.astype(F32)).astype(BF16)
    err_own = (added(terms[far:]) - paired(aim_mine, aim_other).astype(F32)).astype(BF16)

    own_column = along_z(err_own)
    shared_near = jnp.concatenate(along_z(err_shared), axis=0)
    resid_swapped, late_shared, _ = hold((resid_half, err_shared, shared_near))
    resid_other = over_core(resid_swapped)
    shared_there = over_y(late_shared)
    errs_shared = paired(shared_near, over_x(shared_near))
    errs_own = jnp.concatenate(own_column, axis=0)

    grads = jnp.concatenate(
        [
            times_transposed(errs_own, own_mine) + times_transposed(errs_shared, shared_mine),
            turned(times_transposed(errs_own, own_other)),
            times_transposed(errs_shared, shared_other),
        ],
        axis=0,
    )
    lower, upper = grads[:, :latents], grads[:, latents:]
    leaving, late_own = hold((jnp.where(half == 0, upper, lower), err_own))
    grads = jnp.where(half == 0, lower, upper) + over_core(leaving)
    own_there = over_x(rows_at(late_own, 1))
    grads, shared_there, resid_other = hold((grads, shared_there, resid_other))
    from_x = over_x(grads[tokens:2 * tokens].astype(BF16))
    from_y = over_y(grads[2 * tokens:].astype(BF16))
    from_y, own_there = hold((from_y, own_there))
    from_x, from_y = from_x.astype(F32), from_y.astype(F32)
    errors = jnp.where(
        layer == 0,
        ordered(side, rows_at(err_own, 0), own_there, axis=1),
        jnp.concatenate([shared_there, err_shared], axis=1),
    )
    grad_pre = (grads[:tokens] + from_x + from_y) * gate
    bias_grad = jnp.sum(grad_pre, axis=0)[None, :]
    enc_grad = encoder_gradient(resid_half, resid_other, grad_pre.astype(BF16), half)
    return errors[None], enc_grad[None], bias_grad


def any_layers(resid, target, enc_weight, enc_bias, dec_weight, blocks):
    slots = lax.axis_size("latent")
    count = lax.axis_size("layer")
    layer, half = lax.axis_index("layer") // 2, lax.axis_index("layer") % 2
    slot = lax.axis_index("latent")
    _, rows, width = resid.shape
    tokens, cols = rows * slots, width // 2
    latents = enc_weight.shape[2]
    decoder = dec_weight[0].reshape(2, 2 * latents, cols)

    def to_all(block):
        copies = jnp.broadcast_to(block[None], (slots,) + block.shape)
        return lax.all_to_all(copies, "latent", 0, 0).reshape(tokens, block.shape[1])

    def shifted(block, distance):
        route = [(i, i + distance) for i in range(count) if 0 <= i + distance < count]
        return lax.ppermute(block, "layer", route)

    resid_half = to_all(lax.dynamic_slice(resid, (layer, 0, half * cols), (1, rows, cols))[0])
    firing = gates(blocks, layer, slot, slots, latents, tokens)
    gate = jnp.where(half == 0, firing[:, :latents], firing[:, latents:])
    weight_other = crossed(enc_weight[0], "layer", 1)
    partial = half_preacts(resid_half, enc_weight[0], weight_other, enc_bias[0], half)
    preact = partial + crossed(partial, "layer", 1)
    acts = (preact * firing).astype(BF16)
    resid_other = crossed(resid_half, "layer", 1)

    sums = jnp.concatenate([times(acts, decoder[t]).astype(BF16) for t in range(2)], axis=1)
    pieces = lax.all_to_all(sums.reshape(slots, rows, width), "latent", 0, 0)
    totals = jnp.sum(pieces.astype(F32), axis=0)
    own_sum, ahead_part = totals[:, :cols], totals[:, cols:]
    wanted = lax.dynamic_slice(target, (layer, 0, half * cols), (2, rows, cols)).astype(F32)
    err_own = (own_sum + shifted(ahead_part, 2) - wanted[0]).astype(BF16)
    err_next = (ahead_part + shifted(own_sum, -2) - wanted[1]).astype(BF16)
    errs = to_all(jnp.concatenate([err_own, err_next], axis=1))
    here = times_transposed(errs[:, :cols], decoder[0]) + times_transposed(errs[:, cols:], decoder[1])
    lower, upper = here[:, :latents], here[:, latents:]
    grad = jnp.where(half == 0, lower, upper) + crossed(jnp.where(half == 0, upper, lower), "layer", 1)
    grad_pre = grad * gate
    bias_grad = jnp.sum(grad_pre, axis=0)[None, :]
    enc_grad = encoder_gradient(resid_half, resid_other, grad_pre.astype(BF16), half)
    return err_own[None], enc_grad[None], bias_grad


def solution(mesh):
    small = mesh.shape["layer"] == 4 and mesh.shape["latent"] == 8
    return jax.shard_map(
        two_layers if small else any_layers,
        mesh=mesh,
        in_specs=(
            P(None, "latent", None),
            P(None, "latent", None),
            P("layer", None, "latent"),
            P("layer", "latent"),
            P("layer", None, None, "latent", None),
            P(),
        ),
        out_specs=(P("layer", "latent", None), P("layer", None, "latent"), P("layer", "latent")),
        check_vma=False,
    )
```

```python
import jax
import jax.numpy as jnp
from jax import lax
from jax.sharding import PartitionSpec as P

BLOCK = 128
F32, BF16 = jnp.float32, jnp.bfloat16


def crossed(block, axis, mask):
    return lax.ppermute(block, axis, [(i, i ^ mask) for i in range(lax.axis_size(axis))])


def times(left, right):
    return jnp.dot(left, right, preferred_element_type=F32)


def times_transposed(left, right):
    return lax.dot_general(left, right, (((1,), (1,)), ((), ())), preferred_element_type=F32)


def both_halves(half, mine, other, axis):
    return jnp.concatenate([jnp.where(half == 0, mine, other), jnp.where(half == 0, other, mine)], axis=axis)


def gates(blocks, layer, slot, slots, latents, tokens):
    listed = lax.dynamic_index_in_dim(blocks, layer, 0, keepdims=False)
    column = jnp.arange(2 * latents)
    names = (column // latents * slots + slot) * (latents // BLOCK) + column % latents // BLOCK
    flags = jnp.any(listed[:, :, None] == names, axis=1).astype(F32)
    return jnp.repeat(flags, tokens // listed.shape[0], axis=0)


def half_preacts(resid_half, weight, weight_other, bias, half):
    cols = resid_half.shape[1]
    mine = lax.dynamic_slice_in_dim(weight, half * cols, cols, 0)
    other = lax.dynamic_slice_in_dim(weight_other, half * cols, cols, 0)
    nothing = jnp.zeros_like(bias)
    return times(resid_half, both_halves(half, mine, other, 1)) + both_halves(half, bias, nothing, 0)


def encoder_gradient(resid_half, resid_other, grad_low, half):
    whole = both_halves(half, resid_half, resid_other, 1)
    grad = lax.dot_general(whole, grad_low, (((0,), (0,)), ((), ())), preferred_element_type=F32)
    return grad.astype(BF16)


def two_layers(resid, target, enc_weight, enc_bias, dec_weight, blocks):
    hold = lax.optimization_barrier
    slots = lax.axis_size("latent")
    far = slots // 2
    layer, half = lax.axis_index("layer") // 2, lax.axis_index("layer") % 2
    slot = lax.axis_index("latent")
    side = slot % 2
    _, rows, width = resid.shape
    tokens, cols, part = rows * slots, width // 2, width // 4
    latents = enc_weight.shape[2]
    decoder = dec_weight[0].reshape(2, 2 * latents, cols)

    def over_x(block):
        return crossed(block, "latent", 1)

    def over_y(block):
        return crossed(block, "layer", 2)

    def over_core(block):
        return crossed(block, "layer", 1)

    def along_z(block):
        out = [block] + [None] * (far - 1)
        for k in range(far - 1, 0, -1):
            out[k] = crossed(block, "latent", 2 * k)
        return out

    def both_along_z(shared, own):
        count = shared[1].shape[0]
        out = [[shared[0]] + [None] * (far - 1), [own[0]] + [None] * (far - 1)]
        for k in range(far - 1, 0, -1):
            out[0][k] = crossed(shared[k], "latent", 2 * k)
            out[1][k] = crossed(own[k], "latent", 2 * k)
        return out

    def pieces_of(total):
        count = total.shape[0] // far
        return [total[:count]] + [total[k * count:(k + 1) * count].astype(BF16) for k in range(1, far)]

    def added(terms):
        return sum(term.astype(F32) for term in terms)

    def decoder_part(decoder, which, where):
        return lax.dynamic_slice(decoder, (which, 0, where * part), (1, 2 * latents, part))[0]

    def ordered(which, lower, upper, axis=0):
        return jnp.concatenate([jnp.where(which == 0, lower, upper), jnp.where(which == 0, upper, lower)], axis=axis)

    def rows_at(array, which):
        return array.reshape(-1, 2, rows, array.shape[1])[:, which].reshape(-1, array.shape[1])

    def paired(first, second):
        blocks = [block.reshape(-1, 1, rows, block.shape[1]) for block in (first, second)]
        return jnp.concatenate(blocks, axis=1).reshape(-1, first.shape[1])

    def turned(array):
        return paired(rows_at(array, 1), rows_at(array, 0))

    weight_other = over_core(enc_weight[0])
    mine = lax.dynamic_slice(resid, (layer, 0, half * cols), (1, rows, cols))[0]
    pair, weight_other, bias, blocks = hold((paired(mine, over_x(mine)), weight_other, enc_bias[0], blocks))
    column = along_z(pair)

    own_other = over_x(decoder_part(decoder, layer, 1 - side))
    shared_other = over_y(decoder_part(decoder, 1 - layer, 1 - layer))
    decoder, own_other, shared_other, *column = hold((decoder, own_other, shared_other, *column))
    own_mine, shared_mine = decoder_part(decoder, layer, side), decoder_part(decoder, 1 - layer, layer)
    resid_half = jnp.concatenate(column, axis=0)
    firing = gates(blocks, layer, slot, slots, latents, tokens)
    gate = jnp.where(half == 0, firing[:, :latents], firing[:, latents:])

    partial = half_preacts(resid_half, enc_weight[0], weight_other, bias, half)
    acts = ((partial + over_core(partial)) * firing).astype(BF16)
    acts_turned = turned(acts)
    acts_y, acts_x = over_y(acts), over_x(acts_turned)
    target, _ = hold((target, acts_turned))
    start = half * cols

    def aim_own(where):
        return lax.dynamic_slice(target, (2 * layer, 0, start + where * part), (1, rows, part))[0]

    aim_other = over_x(aim_own(1 - side))
    aim_shared = lax.dynamic_slice(target, (1, 0, start + layer * part), (1, rows, part))[0]

    leaving = times(rows_at(acts, 1), shared_mine) + times(rows_at(acts_y, 1), shared_other)
    staying = times(rows_at(acts, 0), shared_mine) + times(rows_at(acts_y, 0), shared_other)
    arrived = over_x(leaving.astype(BF16))
    product = times(acts, own_mine) + times(acts_x, own_other)
    own_pieces = pieces_of(product)
    arrived, staying, own_pieces[1] = hold((arrived, staying, own_pieces[1]))
    shared_terms, own_terms = both_along_z(pieces_of(staying + arrived.astype(F32)), own_pieces)
    terms = hold((*shared_terms, *own_terms[2:]))
    terms = (*terms[:far], own_terms[0], own_terms[1], *terms[far:])
    aim_mine, aim_shared = hold((aim_own(side), aim_shared))
    err_shared = (added(terms[:far]) - aim_shared.astype(F32)).astype(BF16)
    err_own = (added(terms[far:]) - paired(aim_mine, aim_other).astype(F32)).astype(BF16)

    own_column = along_z(err_own)
    shared_near = jnp.concatenate(along_z(err_shared), axis=0)
    resid_swapped, late_shared, _ = hold((resid_half, err_shared, shared_near))
    resid_other = over_core(resid_swapped)
    shared_there = over_y(late_shared)
    errs_shared = paired(shared_near, over_x(shared_near))
    errs_own = jnp.concatenate(own_column, axis=0)

    own_grads = hold([times_transposed(errs_own, weights) for weights in (own_mine, own_other)])
    grads = jnp.concatenate(
        [
            own_grads[0] + times_transposed(errs_shared, shared_mine),
            turned(own_grads[1]),
            times_transposed(errs_shared, shared_other),
        ],
        axis=0,
    )
    lower, upper = grads[:, :latents], grads[:, latents:]
    leaving, late_own = hold((jnp.where(half == 0, upper, lower), err_own))
    grads = jnp.where(half == 0, lower, upper) + over_core(leaving)
    own_there = over_x(rows_at(late_own, 1))
    grads, shared_there, resid_other = hold((grads, shared_there, resid_other))
    from_x = over_x(grads[tokens:2 * tokens].astype(BF16))
    from_y = over_y(grads[2 * tokens:].astype(BF16))
    from_y, own_there = hold((from_y, own_there))
    from_x, from_y = from_x.astype(F32), from_y.astype(F32)
    errors = jnp.where(
        layer == 0,
        ordered(side, rows_at(err_own, 0), own_there, axis=1),
        jnp.concatenate([shared_there, err_shared], axis=1),
    )
    grad_pre = (grads[:tokens] + from_x + from_y) * gate
    bias_grad = jnp.sum(grad_pre, axis=0)[None, :]
    enc_grad = encoder_gradient(resid_half, resid_other, grad_pre.astype(BF16), half)
    return errors[None], enc_grad[None], bias_grad


def any_layers(resid, target, enc_weight, enc_bias, dec_weight, blocks):
    slots = lax.axis_size("latent")
    count = lax.axis_size("layer")
    layer, half = lax.axis_index("layer") // 2, lax.axis_index("layer") % 2
    slot = lax.axis_index("latent")
    _, rows, width = resid.shape
    tokens, cols = rows * slots, width // 2
    latents = enc_weight.shape[2]
    decoder = dec_weight[0].reshape(2, 2 * latents, cols)

    def to_all(block):
        copies = jnp.broadcast_to(block[None], (slots,) + block.shape)
        return lax.all_to_all(copies, "latent", 0, 0).reshape(tokens, block.shape[1])

    def shifted(block, distance):
        route = [(i, i + distance) for i in range(count) if 0 <= i + distance < count]
        return lax.ppermute(block, "layer", route)

    resid_half = to_all(lax.dynamic_slice(resid, (layer, 0, half * cols), (1, rows, cols))[0])
    firing = gates(blocks, layer, slot, slots, latents, tokens)
    gate = jnp.where(half == 0, firing[:, :latents], firing[:, latents:])
    weight_other = crossed(enc_weight[0], "layer", 1)
    partial = half_preacts(resid_half, enc_weight[0], weight_other, enc_bias[0], half)
    preact = partial + crossed(partial, "layer", 1)
    acts = (preact * firing).astype(BF16)
    resid_other = crossed(resid_half, "layer", 1)

    sums = jnp.concatenate([times(acts, decoder[t]).astype(BF16) for t in range(2)], axis=1)
    pieces = lax.all_to_all(sums.reshape(slots, rows, width), "latent", 0, 0)
    totals = jnp.sum(pieces.astype(F32), axis=0)
    own_sum, ahead_part = totals[:, :cols], totals[:, cols:]
    wanted = lax.dynamic_slice(target, (layer, 0, half * cols), (2, rows, cols)).astype(F32)
    err_own = (own_sum + shifted(ahead_part, 2) - wanted[0]).astype(BF16)
    err_next = (ahead_part + shifted(own_sum, -2) - wanted[1]).astype(BF16)
    errs = to_all(jnp.concatenate([err_own, err_next], axis=1))
    here = times_transposed(errs[:, :cols], decoder[0]) + times_transposed(errs[:, cols:], decoder[1])
    lower, upper = here[:, :latents], here[:, latents:]
    grad = jnp.where(half == 0, lower, upper) + crossed(jnp.where(half == 0, upper, lower), "layer", 1)
    grad_pre = grad * gate
    bias_grad = jnp.sum(grad_pre, axis=0)[None, :]
    enc_grad = encoder_gradient(resid_half, resid_other, grad_pre.astype(BF16), half)
    return err_own[None], enc_grad[None], bias_grad


def solution(mesh):
    small = mesh.shape["layer"] == 4 and mesh.shape["latent"] == 8
    return jax.shard_map(
        two_layers if small else any_layers,
        mesh=mesh,
        in_specs=(
            P(None, "latent", None),
            P(None, "latent", None),
            P("layer", None, "latent"),
            P("layer", "latent"),
            P("layer", None, None, "latent", None),
            P(),
        ),
        out_specs=(P("layer", "latent", None), P("layer", None, "latent"), P("layer", "latent")),
        check_vma=False,
    )
```

```python
import jax
import jax.numpy as jnp
from jax import lax
from jax.sharding import PartitionSpec as P

BLOCK = 128
F32, BF16 = jnp.float32, jnp.bfloat16


def crossed(block, axis, mask):
    return lax.ppermute(block, axis, [(i, i ^ mask) for i in range(lax.axis_size(axis))])


def times(left, right):
    return jnp.dot(left, right, preferred_element_type=F32)


def times_transposed(left, right):
    return lax.dot_general(left, right, (((1,), (1,)), ((), ())), preferred_element_type=F32)


def both_halves(half, mine, other, axis):
    return jnp.concatenate([jnp.where(half == 0, mine, other), jnp.where(half == 0, other, mine)], axis=axis)


def gates(blocks, layer, slot, slots, latents, tokens):
    listed = lax.dynamic_index_in_dim(blocks, layer, 0, keepdims=False)
    column = jnp.arange(2 * latents)
    names = (column // latents * slots + slot) * (latents // BLOCK) + column % latents // BLOCK
    flags = jnp.any(listed[:, :, None] == names, axis=1).astype(F32)
    return jnp.repeat(flags, tokens // listed.shape[0], axis=0)


def half_preacts(resid_half, weight, weight_other, bias, half):
    cols = resid_half.shape[1]
    mine = lax.dynamic_slice_in_dim(weight, half * cols, cols, 0)
    other = lax.dynamic_slice_in_dim(weight_other, half * cols, cols, 0)
    nothing = jnp.zeros_like(bias)
    return times(resid_half, both_halves(half, mine, other, 1)) + both_halves(half, bias, nothing, 0)


def encoder_gradient(resid_half, resid_other, grad_low, half):
    whole = both_halves(half, resid_half, resid_other, 1)
    grad = lax.dot_general(whole, grad_low, (((0,), (0,)), ((), ())), preferred_element_type=F32)
    return grad.astype(BF16)


def two_layers(resid, target, enc_weight, enc_bias, dec_weight, blocks):
    hold = lax.optimization_barrier
    slots = lax.axis_size("latent")
    far = slots // 2
    layer, half = lax.axis_index("layer") // 2, lax.axis_index("layer") % 2
    slot = lax.axis_index("latent")
    side = slot % 2
    _, rows, width = resid.shape
    tokens, cols, part = rows * slots, width // 2, width // 4
    latents = enc_weight.shape[2]
    decoder = dec_weight[0].reshape(2, 2 * latents, cols)

    def over_x(block):
        return crossed(block, "latent", 1)

    def over_y(block):
        return crossed(block, "layer", 2)

    def over_core(block):
        return crossed(block, "layer", 1)

    def along_z(block):
        out = [block] + [None] * (far - 1)
        for k in range(far - 1, 0, -1):
            out[k] = crossed(block, "latent", 2 * k)
        return out

    def both_along_z(shared, own):
        count = shared[1].shape[0]
        out = [[shared[0]] + [None] * (far - 1), [own[0]] + [None] * (far - 1)]
        for k in range(far - 1, 0, -1):
            out[0][k] = crossed(shared[k], "latent", 2 * k)
            out[1][k] = crossed(own[k], "latent", 2 * k)
        return out

    def pieces_of(total):
        count = total.shape[0] // far
        return [total[:count]] + [total[k * count:(k + 1) * count].astype(BF16) for k in range(1, far)]

    def added(terms):
        return sum(term.astype(F32) for term in terms)

    def decoder_part(decoder, which, where):
        return lax.dynamic_slice(decoder, (which, 0, where * part), (1, 2 * latents, part))[0]

    def ordered(which, lower, upper, axis=0):
        return jnp.concatenate([jnp.where(which == 0, lower, upper), jnp.where(which == 0, upper, lower)], axis=axis)

    def rows_at(array, which):
        return array.reshape(-1, 2, rows, array.shape[1])[:, which].reshape(-1, array.shape[1])

    def paired(first, second):
        blocks = [block.reshape(-1, 1, rows, block.shape[1]) for block in (first, second)]
        return jnp.concatenate(blocks, axis=1).reshape(-1, first.shape[1])

    def turned(array):
        return paired(rows_at(array, 1), rows_at(array, 0))

    weight_other = over_core(enc_weight[0])
    mine = lax.dynamic_slice(resid, (layer, 0, half * cols), (1, rows, cols))[0]
    pair, weight_other, bias, blocks = hold((paired(mine, over_x(mine)), weight_other, enc_bias[0], blocks))
    column = along_z(pair)

    own_other = over_x(decoder_part(decoder, layer, 1 - side))
    shared_other = over_y(decoder_part(decoder, 1 - layer, 1 - layer))
    decoder, own_other, shared_other, *column = hold((decoder, own_other, shared_other, *column))
    own_mine, shared_mine = decoder_part(decoder, layer, side), decoder_part(decoder, 1 - layer, layer)
    resid_half = jnp.concatenate(column, axis=0)
    firing = gates(blocks, layer, slot, slots, latents, tokens)

    partial = half_preacts(resid_half, enc_weight[0], weight_other, bias, half)
    acts = ((partial + over_core(partial)) * firing).astype(BF16)
    acts_turned = turned(acts)
    acts_y, acts_x = over_y(acts), over_x(acts_turned)
    target, _ = hold((target, acts_turned))
    start = half * cols

    def aim_own(where):
        return lax.dynamic_slice(target, (2 * layer, 0, start + where * part), (1, rows, part))[0]

    aim_other = over_x(aim_own(1 - side))
    aim_shared = lax.dynamic_slice(target, (1, 0, start + layer * part), (1, rows, part))[0]

    leaving = times(rows_at(acts, 1), shared_mine) + times(rows_at(acts_y, 1), shared_other)
    staying = times(rows_at(acts, 0), shared_mine) + times(rows_at(acts_y, 0), shared_other)
    arrived = over_x(leaving.astype(BF16))
    product = times(acts, own_mine) + times(acts_x, own_other)
    own_pieces = pieces_of(product)
    arrived, staying, own_pieces[1] = hold((arrived, staying, own_pieces[1]))
    shared_terms, own_terms = both_along_z(pieces_of(staying + arrived.astype(F32)), own_pieces)
    terms = hold((*shared_terms, *own_terms[2:]))
    terms = (*terms[:far], own_terms[0], own_terms[1], *terms[far:])
    aim_mine, aim_shared = hold((aim_own(side), aim_shared))
    err_shared = (added(terms[:far]) - aim_shared.astype(F32)).astype(BF16)
    err_own = (added(terms[far:]) - paired(aim_mine, aim_other).astype(F32)).astype(BF16)

    own_column = along_z(err_own)
    shared_near = jnp.concatenate(along_z(err_shared), axis=0)
    resid_swapped, late_shared, _ = hold((resid_half, err_shared, shared_near))
    resid_other = over_core(resid_swapped)
    shared_there = over_y(late_shared)
    errs_shared = paired(shared_near, over_x(shared_near))
    errs_own = jnp.concatenate(own_column, axis=0)

    own_grads = hold([times_transposed(errs_own, weights) for weights in (own_mine, own_other)])
    grads = jnp.concatenate(
        [
            own_grads[0] + times_transposed(errs_shared, shared_mine),
            turned(own_grads[1]),
            times_transposed(errs_shared, shared_other),
        ],
        axis=0,
    )
    lower, upper = grads[:, :latents], grads[:, latents:]
    leaving, late_own = hold((jnp.where(half == 0, upper, lower), err_own))
    grads = jnp.where(half == 0, lower, upper) + over_core(leaving)
    own_there = over_x(rows_at(late_own, 1))
    grads, shared_there, resid_other = hold((grads, shared_there, resid_other))
    to_x, to_y = grads[tokens:2 * tokens].astype(BF16), grads[2 * tokens:].astype(BF16)
    from_x, from_y = over_x(to_x), over_y(to_y)
    firing, _, _ = hold((firing, to_x, to_y))
    gate = jnp.where(half == 0, firing[:, :latents], firing[:, latents:])
    own_there, gate = hold((own_there, gate))
    from_x, from_y = from_x.astype(F32), from_y.astype(F32)
    errors = jnp.where(
        layer == 0,
        ordered(side, rows_at(err_own, 0), own_there, axis=1),
        jnp.concatenate([shared_there, err_shared], axis=1),
    )
    grad_pre = (grads[:tokens] + from_x + from_y) * gate
    bias_grad = jnp.sum(grad_pre, axis=0)[None, :]
    enc_grad = encoder_gradient(resid_half, resid_other, grad_pre.astype(BF16), half)
    return errors[None], enc_grad[None], bias_grad


def any_layers(resid, target, enc_weight, enc_bias, dec_weight, blocks):
    slots = lax.axis_size("latent")
    count = lax.axis_size("layer")
    layer, half = lax.axis_index("layer") // 2, lax.axis_index("layer") % 2
    slot = lax.axis_index("latent")
    _, rows, width = resid.shape
    tokens, cols = rows * slots, width // 2
    latents = enc_weight.shape[2]
    decoder = dec_weight[0].reshape(2, 2 * latents, cols)

    def to_all(block):
        copies = jnp.broadcast_to(block[None], (slots,) + block.shape)
        return lax.all_to_all(copies, "latent", 0, 0).reshape(tokens, block.shape[1])

    def shifted(block, distance):
        route = [(i, i + distance) for i in range(count) if 0 <= i + distance < count]
        return lax.ppermute(block, "layer", route)

    resid_half = to_all(lax.dynamic_slice(resid, (layer, 0, half * cols), (1, rows, cols))[0])
    firing = gates(blocks, layer, slot, slots, latents, tokens)
    gate = jnp.where(half == 0, firing[:, :latents], firing[:, latents:])
    weight_other = crossed(enc_weight[0], "layer", 1)
    partial = half_preacts(resid_half, enc_weight[0], weight_other, enc_bias[0], half)
    preact = partial + crossed(partial, "layer", 1)
    acts = (preact * firing).astype(BF16)
    resid_other = crossed(resid_half, "layer", 1)

    sums = jnp.concatenate([times(acts, decoder[t]).astype(BF16) for t in range(2)], axis=1)
    pieces = lax.all_to_all(sums.reshape(slots, rows, width), "latent", 0, 0)
    totals = jnp.sum(pieces.astype(F32), axis=0)
    own_sum, ahead_part = totals[:, :cols], totals[:, cols:]
    wanted = lax.dynamic_slice(target, (layer, 0, half * cols), (2, rows, cols)).astype(F32)
    err_own = (own_sum + shifted(ahead_part, 2) - wanted[0]).astype(BF16)
    err_next = (ahead_part + shifted(own_sum, -2) - wanted[1]).astype(BF16)
    errs = to_all(jnp.concatenate([err_own, err_next], axis=1))
    here = times_transposed(errs[:, :cols], decoder[0]) + times_transposed(errs[:, cols:], decoder[1])
    lower, upper = here[:, :latents], here[:, latents:]
    grad = jnp.where(half == 0, lower, upper) + crossed(jnp.where(half == 0, upper, lower), "layer", 1)
    grad_pre = grad * gate
    bias_grad = jnp.sum(grad_pre, axis=0)[None, :]
    enc_grad = encoder_gradient(resid_half, resid_other, grad_pre.astype(BF16), half)
    return err_own[None], enc_grad[None], bias_grad


def solution(mesh):
    small = mesh.shape["layer"] == 4 and mesh.shape["latent"] == 8
    return jax.shard_map(
        two_layers if small else any_layers,
        mesh=mesh,
        in_specs=(
            P(None, "latent", None),
            P(None, "latent", None),
            P("layer", None, "latent"),
            P("layer", "latent"),
            P("layer", None, None, "latent", None),
            P(),
        ),
        out_specs=(P("layer", "latent", None), P("layer", None, "latent"), P("layer", "latent")),
        check_vma=False,
    )
```

```python
import jax
import jax.numpy as jnp
from jax import lax
from jax.sharding import PartitionSpec as P

BLOCK = 128
F32, BF16 = jnp.float32, jnp.bfloat16


def crossed(block, axis, mask):
    return lax.ppermute(block, axis, [(i, i ^ mask) for i in range(lax.axis_size(axis))])


def times(left, right):
    return jnp.dot(left, right, preferred_element_type=F32)


def times_transposed(left, right):
    return lax.dot_general(left, right, (((1,), (1,)), ((), ())), preferred_element_type=F32)


def both_halves(half, mine, other, axis):
    return jnp.concatenate([jnp.where(half == 0, mine, other), jnp.where(half == 0, other, mine)], axis=axis)


def gates(blocks, layer, slot, slots, latents, tokens):
    listed = lax.dynamic_index_in_dim(blocks, layer, 0, keepdims=False)
    column = jnp.arange(2 * latents)
    names = (column // latents * slots + slot) * (latents // BLOCK) + column % latents // BLOCK
    flags = jnp.any(listed[:, :, None] == names, axis=1).astype(F32)
    return jnp.repeat(flags, tokens // listed.shape[0], axis=0)


def half_preacts(resid_half, weight, weight_other, bias, half):
    cols = resid_half.shape[1]
    mine = lax.dynamic_slice_in_dim(weight, half * cols, cols, 0)
    other = lax.dynamic_slice_in_dim(weight_other, half * cols, cols, 0)
    nothing = jnp.zeros_like(bias)
    return times(resid_half, both_halves(half, mine, other, 1)) + both_halves(half, bias, nothing, 0)


def encoder_gradient(resid_half, resid_other, grad_low, half):
    whole = both_halves(half, resid_half, resid_other, 1)
    grad = lax.dot_general(whole, grad_low, (((0,), (0,)), ((), ())), preferred_element_type=F32)
    return grad.astype(BF16)


def two_layers(resid, target, enc_weight, enc_bias, dec_weight, blocks):
    hold = lax.optimization_barrier
    slots = lax.axis_size("latent")
    far = slots // 2
    layer, half = lax.axis_index("layer") // 2, lax.axis_index("layer") % 2
    slot = lax.axis_index("latent")
    side = slot % 2
    _, rows, width = resid.shape
    tokens, cols, part = rows * slots, width // 2, width // 4
    latents = enc_weight.shape[2]
    decoder = dec_weight[0].reshape(2, 2 * latents, cols)

    def over_x(block):
        return crossed(block, "latent", 1)

    def over_y(block):
        return crossed(block, "layer", 2)

    def over_core(block):
        return crossed(block, "layer", 1)

    def along_z(block):
        out = [block] + [None] * (far - 1)
        for k in range(far - 1, 0, -1):
            out[k] = crossed(block, "latent", 2 * k)
        return out

    def both_along_z(shared, own):
        count = shared[1].shape[0]
        out = [[shared[0]] + [None] * (far - 1), [own[0]] + [None] * (far - 1)]
        for k in range(far - 1, 0, -1):
            out[0][k] = crossed(shared[k], "latent", 2 * k)
            out[1][k] = crossed(own[k], "latent", 2 * k)
        return out

    def pieces_of(total):
        count = total.shape[0] // far
        return [total[:count]] + [total[k * count:(k + 1) * count].astype(BF16) for k in range(1, far)]

    def added(terms):
        return sum(term.astype(F32) for term in terms)

    def decoder_part(decoder, which, where):
        return lax.dynamic_slice(decoder, (which, 0, where * part), (1, 2 * latents, part))[0]

    def ordered(which, lower, upper, axis=0):
        return jnp.concatenate([jnp.where(which == 0, lower, upper), jnp.where(which == 0, upper, lower)], axis=axis)

    def rows_at(array, which):
        return array.reshape(-1, 2, rows, array.shape[1])[:, which].reshape(-1, array.shape[1])

    def paired(first, second):
        blocks = [block.reshape(-1, 1, rows, block.shape[1]) for block in (first, second)]
        return jnp.concatenate(blocks, axis=1).reshape(-1, first.shape[1])

    def turned(array):
        return paired(rows_at(array, 1), rows_at(array, 0))

    weight_other = over_core(enc_weight[0])
    mine = lax.dynamic_slice(resid, (layer, 0, half * cols), (1, rows, cols))[0]
    pair, weight_other, bias, blocks = hold((paired(mine, over_x(mine)), weight_other, enc_bias[0], blocks))
    column = along_z(pair)

    after, _ = hold((decoder, mine))
    own_other = over_x(decoder_part(after, layer, 1 - side))
    shared_other = over_y(decoder_part(after, 1 - layer, 1 - layer))
    decoder, own_other, shared_other, *column = hold((decoder, own_other, shared_other, *column))
    own_mine, shared_mine = decoder_part(decoder, layer, side), decoder_part(decoder, 1 - layer, layer)
    resid_half = jnp.concatenate(column, axis=0)
    firing = gates(blocks, layer, slot, slots, latents, tokens)

    partial = half_preacts(resid_half, enc_weight[0], weight_other, bias, half)
    acts = ((partial + over_core(partial)) * firing).astype(BF16)
    acts_turned = turned(acts)
    acts_y, acts_x = over_y(acts), over_x(acts_turned)
    target, _ = hold((target, acts_turned))
    start = half * cols

    def aim_own(where):
        return lax.dynamic_slice(target, (2 * layer, 0, start + where * part), (1, rows, part))[0]

    aim_other = over_x(aim_own(1 - side))
    aim_shared = lax.dynamic_slice(target, (1, 0, start + layer * part), (1, rows, part))[0]

    leaving = times(rows_at(acts, 1), shared_mine) + times(rows_at(acts_y, 1), shared_other)
    staying = times(rows_at(acts, 0), shared_mine) + times(rows_at(acts_y, 0), shared_other)
    arrived = over_x(leaving.astype(BF16))
    product = times(acts, own_mine) + times(acts_x, own_other)
    own_pieces = pieces_of(product)
    arrived, staying, own_pieces[1] = hold((arrived, staying, own_pieces[1]))
    shared_terms, own_terms = both_along_z(pieces_of(staying + arrived.astype(F32)), own_pieces)
    terms = hold((*shared_terms, *own_terms[2:]))
    terms = (*terms[:far], own_terms[0], own_terms[1], *terms[far:])
    aim_mine, aim_shared = hold((aim_own(side), aim_shared))
    err_shared = (added(terms[:far]) - aim_shared.astype(F32)).astype(BF16)
    err_own = (added(terms[far:]) - paired(aim_mine, aim_other).astype(F32)).astype(BF16)

    own_column = along_z(err_own)
    shared_near = jnp.concatenate(along_z(err_shared), axis=0)
    resid_swapped, late_shared, _ = hold((resid_half, err_shared, shared_near))
    resid_other = over_core(resid_swapped)
    shared_there = over_y(late_shared)
    errs_shared = paired(shared_near, over_x(shared_near))
    errs_own = jnp.concatenate(own_column, axis=0)

    own_grads = hold([times_transposed(errs_own, weights) for weights in (own_mine, own_other)])
    grads = jnp.concatenate(
        [
            own_grads[0] + times_transposed(errs_shared, shared_mine),
            turned(own_grads[1]),
            times_transposed(errs_shared, shared_other),
        ],
        axis=0,
    )
    lower, upper = grads[:, :latents], grads[:, latents:]
    leaving, late_own = hold((jnp.where(half == 0, upper, lower), err_own))
    grads = jnp.where(half == 0, lower, upper) + over_core(leaving)
    own_there = over_x(rows_at(late_own, 1))
    grads, shared_there, resid_other = hold((grads, shared_there, resid_other))
    to_x, to_y = grads[tokens:2 * tokens].astype(BF16), grads[2 * tokens:].astype(BF16)
    from_x, from_y = over_x(to_x), over_y(to_y)
    firing, _, _ = hold((firing, to_x, to_y))
    gate = jnp.where(half == 0, firing[:, :latents], firing[:, latents:])
    own_there, gate = hold((own_there, gate))
    from_x, from_y = from_x.astype(F32), from_y.astype(F32)
    errors = jnp.where(
        layer == 0,
        ordered(side, rows_at(err_own, 0), own_there, axis=1),
        jnp.concatenate([shared_there, err_shared], axis=1),
    )
    grad_pre = (grads[:tokens] + from_x + from_y) * gate
    bias_grad = jnp.sum(grad_pre, axis=0)[None, :]
    enc_grad = encoder_gradient(resid_half, resid_other, grad_pre.astype(BF16), half)
    return errors[None], enc_grad[None], bias_grad


def any_layers(resid, target, enc_weight, enc_bias, dec_weight, blocks):
    slots = lax.axis_size("latent")
    count = lax.axis_size("layer")
    layer, half = lax.axis_index("layer") // 2, lax.axis_index("layer") % 2
    slot = lax.axis_index("latent")
    _, rows, width = resid.shape
    tokens, cols = rows * slots, width // 2
    latents = enc_weight.shape[2]
    decoder = dec_weight[0].reshape(2, 2 * latents, cols)

    def to_all(block):
        copies = jnp.broadcast_to(block[None], (slots,) + block.shape)
        return lax.all_to_all(copies, "latent", 0, 0).reshape(tokens, block.shape[1])

    def shifted(block, distance):
        route = [(i, i + distance) for i in range(count) if 0 <= i + distance < count]
        return lax.ppermute(block, "layer", route)

    resid_half = to_all(lax.dynamic_slice(resid, (layer, 0, half * cols), (1, rows, cols))[0])
    firing = gates(blocks, layer, slot, slots, latents, tokens)
    gate = jnp.where(half == 0, firing[:, :latents], firing[:, latents:])
    weight_other = crossed(enc_weight[0], "layer", 1)
    partial = half_preacts(resid_half, enc_weight[0], weight_other, enc_bias[0], half)
    preact = partial + crossed(partial, "layer", 1)
    acts = (preact * firing).astype(BF16)
    resid_other = crossed(resid_half, "layer", 1)

    sums = jnp.concatenate([times(acts, decoder[t]).astype(BF16) for t in range(2)], axis=1)
    pieces = lax.all_to_all(sums.reshape(slots, rows, width), "latent", 0, 0)
    totals = jnp.sum(pieces.astype(F32), axis=0)
    own_sum, ahead_part = totals[:, :cols], totals[:, cols:]
    wanted = lax.dynamic_slice(target, (layer, 0, half * cols), (2, rows, cols)).astype(F32)
    err_own = (own_sum + shifted(ahead_part, 2) - wanted[0]).astype(BF16)
    err_next = (ahead_part + shifted(own_sum, -2) - wanted[1]).astype(BF16)
    errs = to_all(jnp.concatenate([err_own, err_next], axis=1))
    here = times_transposed(errs[:, :cols], decoder[0]) + times_transposed(errs[:, cols:], decoder[1])
    lower, upper = here[:, :latents], here[:, latents:]
    grad = jnp.where(half == 0, lower, upper) + crossed(jnp.where(half == 0, upper, lower), "layer", 1)
    grad_pre = grad * gate
    bias_grad = jnp.sum(grad_pre, axis=0)[None, :]
    enc_grad = encoder_gradient(resid_half, resid_other, grad_pre.astype(BF16), half)
    return err_own[None], enc_grad[None], bias_grad


def solution(mesh):
    small = mesh.shape["layer"] == 4 and mesh.shape["latent"] == 8
    return jax.shard_map(
        two_layers if small else any_layers,
        mesh=mesh,
        in_specs=(
            P(None, "latent", None),
            P(None, "latent", None),
            P("layer", None, "latent"),
            P("layer", "latent"),
            P("layer", None, None, "latent", None),
            P(),
        ),
        out_specs=(P("layer", "latent", None), P("layer", None, "latent"), P("layer", "latent")),
        check_vma=False,
    )
```

```python
import jax
import jax.numpy as jnp
from jax import lax
from jax.sharding import PartitionSpec as P

BLOCK = 128
F32, BF16 = jnp.float32, jnp.bfloat16


def crossed(block, axis, mask):
    return lax.ppermute(block, axis, [(i, i ^ mask) for i in range(lax.axis_size(axis))])


def times(left, right):
    return jnp.dot(left, right, preferred_element_type=F32)


def times_transposed(left, right):
    return lax.dot_general(left, right, (((1,), (1,)), ((), ())), preferred_element_type=F32)


def both_halves(half, mine, other, axis):
    return jnp.concatenate([jnp.where(half == 0, mine, other), jnp.where(half == 0, other, mine)], axis=axis)


def gates(blocks, layer, slot, slots, latents, tokens):
    listed = lax.dynamic_index_in_dim(blocks, layer, 0, keepdims=False)
    column = jnp.arange(2 * latents)
    names = (column // latents * slots + slot) * (latents // BLOCK) + column % latents // BLOCK
    flags = jnp.any(listed[:, :, None] == names, axis=1).astype(F32)
    return jnp.repeat(flags, tokens // listed.shape[0], axis=0)


def half_preacts(resid_half, weight, weight_other, bias, half):
    cols = resid_half.shape[1]
    mine = lax.dynamic_slice_in_dim(weight, half * cols, cols, 0)
    other = lax.dynamic_slice_in_dim(weight_other, half * cols, cols, 0)
    nothing = jnp.zeros_like(bias)
    return times(resid_half, both_halves(half, mine, other, 1)) + both_halves(half, bias, nothing, 0)


def encoder_gradient(resid_half, resid_other, grad_low, half):
    whole = both_halves(half, resid_half, resid_other, 1)
    grad = lax.dot_general(whole, grad_low, (((0,), (0,)), ((), ())), preferred_element_type=F32)
    return grad.astype(BF16)


def two_layers(resid, target, enc_weight, enc_bias, dec_weight, blocks):
    hold = lax.optimization_barrier
    slots = lax.axis_size("latent")
    far = slots // 2
    layer, half = lax.axis_index("layer") // 2, lax.axis_index("layer") % 2
    slot = lax.axis_index("latent")
    side = slot % 2
    _, rows, width = resid.shape
    tokens, cols, part = rows * slots, width // 2, width // 4
    latents = enc_weight.shape[2]
    decoder = dec_weight[0].reshape(2, 2 * latents, cols)

    def over_x(block):
        return crossed(block, "latent", 1)

    def over_y(block):
        return crossed(block, "layer", 2)

    def over_core(block):
        return crossed(block, "layer", 1)

    def along_z(block):
        out = [block] + [None] * (far - 1)
        for k in range(far - 1, 0, -1):
            out[k] = crossed(block, "latent", 2 * k)
        return out

    def both_along_z(shared, own):
        count = shared[1].shape[0]
        out = [[shared[0]] + [None] * (far - 1), [own[0]] + [None] * (far - 1)]
        for k in range(far - 1, 0, -1):
            out[0][k] = crossed(shared[k], "latent", 2 * k)
            out[1][k] = crossed(own[k], "latent", 2 * k)
        return out

    def pieces_of(total):
        count = total.shape[0] // far
        return [total[:count]] + [total[k * count:(k + 1) * count].astype(BF16) for k in range(1, far)]

    def added(terms):
        return sum(term.astype(F32) for term in terms)

    def decoder_part(decoder, which, where):
        return lax.dynamic_slice(decoder, (which, 0, where * part), (1, 2 * latents, part))[0]

    def ordered(which, lower, upper, axis=0):
        return jnp.concatenate([jnp.where(which == 0, lower, upper), jnp.where(which == 0, upper, lower)], axis=axis)

    def rows_at(array, which):
        return array.reshape(-1, 2, rows, array.shape[1])[:, which].reshape(-1, array.shape[1])

    def paired(first, second):
        blocks = [block.reshape(-1, 1, rows, block.shape[1]) for block in (first, second)]
        return jnp.concatenate(blocks, axis=1).reshape(-1, first.shape[1])

    def turned(array):
        return paired(rows_at(array, 1), rows_at(array, 0))

    weight_other = over_core(enc_weight[0])
    mine = lax.dynamic_slice(resid, (layer, 0, half * cols), (1, rows, cols))[0]
    pair, weight_other, bias, blocks = hold((paired(mine, over_x(mine)), weight_other, enc_bias[0], blocks))
    column = along_z(pair)

    after, _ = hold((decoder, mine))
    own_other = over_x(decoder_part(after, layer, 1 - side))
    shared_other = over_y(decoder_part(after, 1 - layer, 1 - layer))
    decoder, own_other, shared_other, *column = hold((decoder, own_other, shared_other, *column[::-1]))
    column = column[::-1]
    own_mine, shared_mine = decoder_part(decoder, layer, side), decoder_part(decoder, 1 - layer, layer)
    resid_half = jnp.concatenate(column, axis=0)
    firing = gates(blocks, layer, slot, slots, latents, tokens)

    partial = half_preacts(resid_half, enc_weight[0], weight_other, bias, half)
    acts = ((partial + over_core(partial)) * firing).astype(BF16)
    acts_turned = turned(acts)
    acts_y, acts_x = over_y(acts), over_x(acts_turned)
    target, _ = hold((target, acts_turned))
    start = half * cols

    def aim_own(where):
        return lax.dynamic_slice(target, (2 * layer, 0, start + where * part), (1, rows, part))[0]

    aim_other = over_x(aim_own(1 - side))
    aim_shared = lax.dynamic_slice(target, (1, 0, start + layer * part), (1, rows, part))[0]

    leaving = times(rows_at(acts, 1), shared_mine) + times(rows_at(acts_y, 1), shared_other)
    staying = times(rows_at(acts, 0), shared_mine) + times(rows_at(acts_y, 0), shared_other)
    arrived = over_x(leaving.astype(BF16))
    product = times(acts, own_mine) + times(acts_x, own_other)
    own_pieces = pieces_of(product)
    arrived, staying, own_pieces[1] = hold((arrived, staying, own_pieces[1]))
    shared_terms, own_terms = both_along_z(pieces_of(staying + arrived.astype(F32)), own_pieces)
    terms = hold((*shared_terms, *own_terms[2:]))
    terms = (*terms[:far], own_terms[0], own_terms[1], *terms[far:])
    aim_mine, aim_shared = hold((aim_own(side), aim_shared))
    err_shared = (added(terms[:far]) - aim_shared.astype(F32)).astype(BF16)
    err_own = (added(terms[far:]) - paired(aim_mine, aim_other).astype(F32)).astype(BF16)

    own_column = along_z(err_own)
    shared_near = jnp.concatenate(along_z(err_shared), axis=0)
    resid_swapped, late_shared, _ = hold((resid_half, err_shared, shared_near))
    resid_other = over_core(resid_swapped)
    shared_there = over_y(late_shared)
    errs_shared = paired(shared_near, over_x(shared_near))
    errs_own = jnp.concatenate(own_column, axis=0)

    own_grads = hold([times_transposed(errs_own, weights) for weights in (own_mine, own_other)])
    grads = jnp.concatenate(
        [
            own_grads[0] + times_transposed(errs_shared, shared_mine),
            turned(own_grads[1]),
            times_transposed(errs_shared, shared_other),
        ],
        axis=0,
    )
    lower, upper = grads[:, :latents], grads[:, latents:]
    leaving, late_own = hold((jnp.where(half == 0, upper, lower), err_own))
    grads = jnp.where(half == 0, lower, upper) + over_core(leaving)
    own_there = over_x(rows_at(late_own, 1))
    grads, shared_there, resid_other = hold((grads, shared_there, resid_other))
    to_x, to_y = grads[tokens:2 * tokens].astype(BF16), grads[2 * tokens:].astype(BF16)
    from_x, from_y = over_x(to_x), over_y(to_y)
    firing, _, _ = hold((firing, to_x, to_y))
    gate = jnp.where(half == 0, firing[:, :latents], firing[:, latents:])
    own_there, gate = hold((own_there, gate))
    from_x, from_y = from_x.astype(F32), from_y.astype(F32)
    errors = jnp.where(
        layer == 0,
        ordered(side, rows_at(err_own, 0), own_there, axis=1),
        jnp.concatenate([shared_there, err_shared], axis=1),
    )
    grad_pre = (grads[:tokens] + from_x + from_y) * gate
    bias_grad = jnp.sum(grad_pre, axis=0)[None, :]
    enc_grad = encoder_gradient(resid_half, resid_other, grad_pre.astype(BF16), half)
    return errors[None], enc_grad[None], bias_grad


def any_layers(resid, target, enc_weight, enc_bias, dec_weight, blocks):
    slots = lax.axis_size("latent")
    count = lax.axis_size("layer")
    layer, half = lax.axis_index("layer") // 2, lax.axis_index("layer") % 2
    slot = lax.axis_index("latent")
    _, rows, width = resid.shape
    tokens, cols = rows * slots, width // 2
    latents = enc_weight.shape[2]
    decoder = dec_weight[0].reshape(2, 2 * latents, cols)

    def to_all(block):
        copies = jnp.broadcast_to(block[None], (slots,) + block.shape)
        return lax.all_to_all(copies, "latent", 0, 0).reshape(tokens, block.shape[1])

    def shifted(block, distance):
        route = [(i, i + distance) for i in range(count) if 0 <= i + distance < count]
        return lax.ppermute(block, "layer", route)

    resid_half = to_all(lax.dynamic_slice(resid, (layer, 0, half * cols), (1, rows, cols))[0])
    firing = gates(blocks, layer, slot, slots, latents, tokens)
    gate = jnp.where(half == 0, firing[:, :latents], firing[:, latents:])
    weight_other = crossed(enc_weight[0], "layer", 1)
    partial = half_preacts(resid_half, enc_weight[0], weight_other, enc_bias[0], half)
    preact = partial + crossed(partial, "layer", 1)
    acts = (preact * firing).astype(BF16)
    resid_other = crossed(resid_half, "layer", 1)

    sums = jnp.concatenate([times(acts, decoder[t]).astype(BF16) for t in range(2)], axis=1)
    pieces = lax.all_to_all(sums.reshape(slots, rows, width), "latent", 0, 0)
    totals = jnp.sum(pieces.astype(F32), axis=0)
    own_sum, ahead_part = totals[:, :cols], totals[:, cols:]
    wanted = lax.dynamic_slice(target, (layer, 0, half * cols), (2, rows, cols)).astype(F32)
    err_own = (own_sum + shifted(ahead_part, 2) - wanted[0]).astype(BF16)
    err_next = (ahead_part + shifted(own_sum, -2) - wanted[1]).astype(BF16)
    errs = to_all(jnp.concatenate([err_own, err_next], axis=1))
    here = times_transposed(errs[:, :cols], decoder[0]) + times_transposed(errs[:, cols:], decoder[1])
    lower, upper = here[:, :latents], here[:, latents:]
    grad = jnp.where(half == 0, lower, upper) + crossed(jnp.where(half == 0, upper, lower), "layer", 1)
    grad_pre = grad * gate
    bias_grad = jnp.sum(grad_pre, axis=0)[None, :]
    enc_grad = encoder_gradient(resid_half, resid_other, grad_pre.astype(BF16), half)
    return err_own[None], enc_grad[None], bias_grad


def solution(mesh):
    small = mesh.shape["layer"] == 4 and mesh.shape["latent"] == 8
    return jax.shard_map(
        two_layers if small else any_layers,
        mesh=mesh,
        in_specs=(
            P(None, "latent", None),
            P(None, "latent", None),
            P("layer", None, "latent"),
            P("layer", "latent"),
            P("layer", None, None, "latent", None),
            P(),
        ),
        out_specs=(P("layer", "latent", None), P("layer", None, "latent"), P("layer", "latent")),
        check_vma=False,
    )
```
